32 devices in a mesh: code: 8 (over z, y), dp: 4 (over x, core).
Axes of the slice: x: 2, y: 2, z: 4, core: 2. Of those that a mesh axis runs over, the one named last changes fastest.
Arguments:
- codebook: bfloat16 [32768, 768], P(('code', 'dp')), may hold values from -6 to 6
- weight_in: bfloat16 [768, 1024], replicated, may hold values from -0.21875 to 0.21875
- bias_in: float32 [1024], replicated, may hold values from -3 to 3
- weight_out: bfloat16 [1024, 256], replicated, may hold values from -0.1875 to 0.1875
- bias_out: float32 [256], replicated, may hold values from -3 to 3
- latents: float32 [32768, 256], P(('code', 'dp')), may hold values from -6 to 6
- cotangent: float32 [32768, 256], P(('code', 'dp')), may hold values from -6 to 6
- code_owner: int32 [32768, 1], P(('code', 'dp')), may hold values from 0 to 31; in each aligned block of 1024 rows (0 to 1023, 1024 to 2047, ...) at most 64 rows name the same one
- code_row: int32 [32768], P(('code', 'dp')), may hold values from 0 to 1023
Outputs:
- latent_grad: float32 [32768, 256], P(('code', 'dp'))
- grad_weight_in: float32 [768, 1024], replicated
- grad_bias_in: float32 [1024], replicated
- grad_weight_out: float32 [1024, 256], replicated
- grad_bias_out: float32 [256], replicated
The draws below stay inside these ranges and needn't reach their ends.
Inputs may be any that keep to these rules, and one draw needn't show every extreme that they name: In the rows of one device no owner is named by more than 64 rows, a bound that some block reaches; a latent's code is code_owner * 1024 + code_row.
All inputs are finite; a program needn't handle non-finite values.
Results may differ from the reference program's by a relative error of at most 0.0023.
Values sent between devices are 32-bit elements; how exact they have to be, the bound alone decides.
No kernel may reach another device: no remote copies, remote signals or barrier semaphores. Data moves between devices by JAX's collectives and lax.ppermute only.
A program may use at most 128 MiB of HBM per device.

```python
import math
import jax
import jax.numpy as jnp
import numpy as np
from jax import lax

DIM_IN = 768
HIDDEN_SIZE = 1024
CODE_DIM = 256
ROWS_DEV = 1024
LAT_DEV = 1024
VOCAB = 32768
LATENTS = 32768
CAP = 64
DEVICES = 32


def place_ends(array, stream_key, least, largest):
    shape = array.shape
    index_at = [jax.random.randint(jax.random.fold_in(stream_key, axis), (), 0, shape[axis]) for axis in range(len(shape))]
    array = array.at[tuple(index_at)].set(least)
    longest = shape.index(max(shape))
    index_at[longest] = (index_at[longest] + 1) % shape[longest]
    return array.at[tuple(index_at)].set(largest)


def levels(stream_key, shape, split, least, high):
    factor_of = 1.0
    for dim, blocks in split:
        steps = jax.random.uniform(jax.random.fold_in(jax.random.fold_in(stream_key, 6), dim), (blocks,), jnp.float32, least / len(split), high / len(split))
        factor_of = factor_of * jnp.repeat(jnp.exp(steps), shape[dim] // blocks).reshape((-1,) + (1,) * (len(shape) - 1 - dim))
    return factor_of


def cumulative_ranks(amount, slope):
    loads = [(1 << 20) // math.isqrt(grade ** slope) + 1 for grade in range(1, amount + 1)]
    deviation = 1 + sum(loads) // (1 << 30)
    return np.cumsum(np.array([max(1, weight // deviation) for weight in loads]))


def skewed_ids(stream_key, extent, amount, lean):
    grid = cumulative_ranks(amount, lean)
    pick = jax.random.randint(jax.random.fold_in(stream_key, 1), extent, 0, int(grid[amount - 1]))
    standing = jnp.searchsorted(jnp.asarray(grid, jnp.int32), pick, side="right")
    return jax.random.permutation(jax.random.fold_in(stream_key, 2), amount)[standing].astype(jnp.int32)


def routed_block(rng, own, number, rows, number_of, top, bound, slope):
    order = jax.random.permutation(rng, number_of)
    packed, usual = shares(number_of, rows * top, bound, slope, True), shares(number_of, rows * top, bound, slope, False)
    places = jnp.arange(number_of)

    def named(lengths, rotation):
        used = int((lengths > 0).sum())
        fixed = max(1, used // 4)
        moved = fixed + (places - fixed + rotation * (used - fixed)) % max(1, number_of - fixed)
        return jnp.zeros((number_of,), jnp.int32).at[order[jnp.where(places < fixed, places, moved)]].set(jnp.asarray(lengths, jnp.int32))

    lengths = jnp.where(number % 4 == 0, named(packed, number // 4), named(usual, number - number // 4 - 1))
    mixed = jax.random.permutation(jax.random.fold_in(own, 3), number_of)
    giver, taker = mixed[0:number_of // 2 * 2:2], mixed[1:number_of // 2 * 2:2]
    margin = jnp.minimum(lengths[giver] - 1, bound - lengths[taker]) // 2
    margin = jnp.where((giver == order[0]) | (taker == order[0]) | (lengths[taker] == 0), 0, jnp.maximum(margin, 0))
    moved = jax.random.randint(jax.random.fold_in(own, 4), (number_of // 2,), 0, 1 << 20) % (margin + 1)
    lengths = lengths.at[giver].add(-moved).at[taker].add(moved)
    items = jnp.searchsorted(jnp.cumsum(lengths), jnp.arange(rows * top), side="right").astype(jnp.int32)
    table = items.reshape(top, rows).T
    table = table[jax.random.permutation(jax.random.fold_in(own, 1), rows)]
    rotation = jax.random.randint(jax.random.fold_in(own, 2), (rows, 1), 0, top)
    return jnp.take_along_axis(table, (jnp.arange(top)[None, :] + rotation) % top, axis=1)


def shares(number_of, total, limit, lean, full):
    weights = [(1 << 20) // math.isqrt(standing ** lean) + 1 for standing in range(1, number_of + 1)]
    largest = limit if full else min(limit, max(-(-total // number_of), total * weights[0] // sum(weights)))
    least = 1 if total - largest >= number_of - 1 else 0
    given, rest = [largest] + [least] * (number_of - 1), total - largest - least * (number_of - 1)
    while rest > 0:
        free = [i for i in range(1, number_of) if given[i] < largest] or [i for i in range(1, number_of) if given[i] < limit]
        mass, left = sum([weights[i] for i in free]), rest
        for i in free:
            addition = min(limit - given[i], max(1, left * weights[i] // mass), rest)
            given[i] = given[i] + addition
            rest = rest - addition
    return np.array(given)


def centred(rng, dims, scale, most, shards=(), dtype=jnp.bfloat16):
    values = scale * jax.random.normal(rng, dims, jnp.float32)
    if shards:
        values = values * levels(rng, dims, shards, -0.22, 0.18)
    return jnp.clip(values, -most, most).astype(dtype)


def setup_inputs(seed: int = 0) -> dict:
    arg_keys = jax.random.split(jax.random.key(seed), 10)
    codebook = centred(arg_keys[0], (VOCAB, DIM_IN), 1.0, 6.0, ((0, 32),))
    weight_in = centred(arg_keys[1], (DIM_IN, HIDDEN_SIZE), DIM_IN ** -0.5, 0.21875)
    bias_in = centred(arg_keys[2], (HIDDEN_SIZE,), 0.5, 3.0, (), jnp.float32)
    weight_out = centred(arg_keys[3], (HIDDEN_SIZE, CODE_DIM), HIDDEN_SIZE ** -0.5, 0.1875)
    bias_out = centred(arg_keys[4], (CODE_DIM,), 0.5, 3.0, (), jnp.float32)
    latents = centred(arg_keys[5], (LATENTS, CODE_DIM), 1.0, 6.0, ((0, 32),), jnp.float32)
    cotangent = centred(arg_keys[6], (LATENTS, CODE_DIM), 1.0, 6.0, ((0, 32),), jnp.float32)
    code_owner_keys = jax.random.split(jax.random.fold_in(arg_keys[7], 1), LATENTS // LAT_DEV)
    code_owner_turns = jax.random.permutation(jax.random.fold_in(arg_keys[7], 3), LATENTS // LAT_DEV)
    code_owner = jax.vmap(lambda own, number: routed_block(jax.random.fold_in(arg_keys[7], 2), own, number, LAT_DEV, DEVICES, 1, CAP, 2))(code_owner_keys, code_owner_turns).reshape((LATENTS, 1))
    code_row = place_ends(skewed_ids(arg_keys[8], (LATENTS,), ROWS_DEV, 2), jax.random.fold_in(arg_keys[8], 3), 0, ROWS_DEV - 1).astype(jnp.int32)
    return {"codebook": codebook, "weight_in": weight_in, "bias_in": bias_in, "weight_out": weight_out, "bias_out": bias_out, "latents": latents, "cotangent": cotangent, "code_owner": code_owner, "code_row": code_row}


scale_gelu = 0.7978845608028654
cubic_term = 0.044715


def gelu_value(x):
    inner = scale_gelu * (x + cubic_term * x * x * x)
    return 0.5 * x * (1.0 + jnp.tanh(inner))


def gelu_slope(x):
    tangent = jnp.tanh(scale_gelu * (x + cubic_term * x * x * x))
    return 0.5 * (1.0 + tangent) + 0.5 * x * (1.0 - tangent * tangent) * scale_gelu * (1.0 + 3.0 * cubic_term * x * x)


def reference(codebook, weight_in, bias_in, weight_out, bias_out, latents, cotangent, code_owner, code_row):
    index = (code_owner[:, 0] * ROWS_DEV + code_row).astype(jnp.int32)
    blocks = codebook.reshape(VOCAB // ROWS_DEV, ROWS_DEV, DIM_IN)

    def forward(block):
        preact = jnp.dot(block, weight_in, preferred_element_type=jnp.float32) + bias_in
        hidden = gelu_value(preact).astype(jnp.bfloat16)
        return jnp.dot(hidden, weight_out, preferred_element_type=jnp.float32) + bias_out

    projected = lax.map(forward, blocks).reshape(VOCAB, CODE_DIM)
    chosen = jnp.take(projected, index, axis=0)
    residual = chosen - latents
    latent_grad = cotangent - 0.25 * residual
    code_grad = jax.ops.segment_sum(cotangent + residual, index, num_segments=VOCAB)
    grad_blocks = code_grad.reshape(VOCAB // ROWS_DEV, ROWS_DEV, CODE_DIM)

    def backward(carry, items):
        block, grad_block = items
        preact = jnp.dot(block, weight_in, preferred_element_type=jnp.float32) + bias_in
        hidden = gelu_value(preact).astype(jnp.bfloat16)
        code_low = grad_block.astype(jnp.bfloat16)
        gw_out = lax.dot_general(hidden, code_low, (((0,), (0,)), ((), ())), preferred_element_type=jnp.float32)
        back = lax.dot_general(code_low, weight_out, (((1,), (1,)), ((), ())), preferred_element_type=jnp.float32)
        preact_grad = (back * gelu_slope(preact)).astype(jnp.bfloat16)
        gb_in = jnp.sum(preact_grad.astype(jnp.float32), axis=0)
        gw_in = lax.dot_general(block, preact_grad, (((0,), (0,)), ((), ())), preferred_element_type=jnp.float32)
        gb_out = jnp.sum(grad_block, axis=0)
        return (carry[0] + gw_in, carry[1] + gb_in, carry[2] + gw_out, carry[3] + gb_out), None

    start = (jnp.zeros((DIM_IN, HIDDEN_SIZE), jnp.float32), jnp.zeros((HIDDEN_SIZE,), jnp.float32),
             jnp.zeros((HIDDEN_SIZE, CODE_DIM), jnp.float32), jnp.zeros((CODE_DIM,), jnp.float32))
    sums, _ = lax.scan(backward, start, (blocks, grad_blocks))
    return latent_grad, sums[0], sums[1], sums[2], sums[3]
```

```python
import jax
import jax.numpy as jnp
from jax import lax
from jax.sharding import PartitionSpec as P

scale_gelu = 0.7978845608028654
cubic_term = 0.044715
AXES = ("code", "dp")


def gelu_parts(x):
    tangent = jnp.tanh(scale_gelu * (x + cubic_term * x * x * x))
    value = 0.5 * x * (1.0 + tangent)
    slope = 0.5 * (1.0 + tangent) + 0.5 * x * (1.0 - tangent * tangent) * scale_gelu * (
        1.0 + 3.0 * cubic_term * x * x
    )
    return value, slope


def split_two(x):
    high = lax.reduce_precision(x, 8, 7)
    low = (x - high).astype(jnp.bfloat16)
    return jnp.concatenate([high.astype(jnp.bfloat16), low], axis=1)


def pick(chooser, rows):
    width = rows.shape[1]
    both = jnp.dot(chooser, split_two(rows), preferred_element_type=jnp.float32)
    return both[:, :width] + both[:, width:]


def per_device(
    codebook, weight_in, bias_in, weight_out, bias_out, latents, cotangent, code_owner, code_row
):
    devices = lax.axis_size("code") * lax.axis_size("dp")
    rows = codebook.shape[0]
    count, width = latents.shape
    capacity = max(2, 2 * count // devices)
    owners = code_owner[:, 0]

    position = jnp.arange(count, dtype=jnp.int32)
    same = (owners[:, None] == owners[None, :]) & (position[None, :] < position[:, None])
    ranks = jnp.sum(same.astype(jnp.int32), axis=1)
    slots = owners * capacity + ranks
    slot_ids = jnp.arange(devices * capacity, dtype=jnp.int32)
    to_slot = slot_ids[:, None] == slots[None, :]
    wanted = jnp.max(jnp.where(to_slot, code_row[None, :], -1), axis=1)
    outgoing = pick(to_slot.astype(jnp.bfloat16), cotangent - latents)

    wanted = lax.all_to_all(
        wanted.reshape(devices, 1, capacity), AXES, split_axis=0, concat_axis=0, tiled=True
    ).reshape(-1)
    incoming = lax.all_to_all(
        outgoing.reshape(devices, capacity, width), AXES, split_axis=0, concat_axis=0, tiled=True
    ).reshape(-1, width)

    preact = jnp.dot(codebook, weight_in, preferred_element_type=jnp.float32) + bias_in
    hidden, slope = gelu_parts(preact)
    hidden = hidden.astype(jnp.bfloat16)
    projected = jnp.dot(hidden, weight_out, preferred_element_type=jnp.float32) + bias_out

    row_ids = jnp.arange(rows, dtype=jnp.int32)
    asked = wanted[:, None] == row_ids[None, :]
    picked = pick(asked.astype(jnp.bfloat16), projected)
    answers = lax.all_to_all(
        picked.reshape(devices, capacity, width), AXES, split_axis=0, concat_axis=0, tiled=True
    ).reshape(-1, width)

    by_code = row_ids[:, None] == wanted[None, :]
    times = jnp.sum(by_code.astype(jnp.float32), axis=1, keepdims=True)
    code_grad = pick(by_code.astype(jnp.bfloat16), incoming) + times * projected
    code_low = code_grad.astype(jnp.bfloat16)
    gw_out = lax.dot_general(
        hidden, code_low, (((0,), (0,)), ((), ())), preferred_element_type=jnp.float32
    )
    back = lax.dot_general(
        code_low, weight_out, (((1,), (1,)), ((), ())), preferred_element_type=jnp.float32
    )
    preact_grad = (back * slope).astype(jnp.bfloat16)
    gb_in = jnp.sum(preact_grad.astype(jnp.float32), axis=0)
    gw_in = lax.dot_general(
        codebook, preact_grad, (((0,), (0,)), ((), ())), preferred_element_type=jnp.float32
    )
    gb_out = jnp.sum(code_grad, axis=0)
    gw_in, gb_in, gw_out, gb_out = lax.psum((gw_in, gb_in, gw_out, gb_out), AXES)

    from_slot = slots[:, None] == slot_ids[None, :]
    chosen = pick(from_slot.astype(jnp.bfloat16), answers)
    latent_grad = cotangent - 0.25 * (chosen - latents)
    return (latent_grad, gw_in, gb_in, gw_out, gb_out)


def solution(mesh):
    rows = P(AXES, None)
    return jax.shard_map(
        per_device,
        mesh=mesh,
        in_specs=(rows, P(), P(), P(), P(), rows, rows, rows, P(AXES)),
        out_specs=(rows, P(), P(), P(), P()),
        check_vma=False,
    )
```

```python
import jax
import jax.numpy as jnp
from jax import lax
from jax.sharding import PartitionSpec as P

scale_gelu = 0.7978845608028654
cubic_term = 0.044715
AXES = ("code", "dp")


def gelu_parts(x):
    tangent = jnp.tanh(scale_gelu * (x + cubic_term * x * x * x))
    value = 0.5 * x * (1.0 + tangent)
    slope = 0.5 * (1.0 + tangent) + 0.5 * x * (1.0 - tangent * tangent) * scale_gelu * (
        1.0 + 3.0 * cubic_term * x * x
    )
    return value, slope


def split_two(x):
    high = lax.reduce_precision(x, 8, 7)
    low = (x - high).astype(jnp.bfloat16)
    return jnp.concatenate([high.astype(jnp.bfloat16), low], axis=1)


def pick(chooser, rows):
    width = rows.shape[1]
    both = jnp.dot(chooser, split_two(rows), preferred_element_type=jnp.float32)
    return both[:, :width] + both[:, width:]


def per_device(
    codebook, weight_in, bias_in, weight_out, bias_out, latents, cotangent, code_owner, code_row
):
    devices = lax.axis_size("code") * lax.axis_size("dp")
    rows = codebook.shape[0]
    count, width = latents.shape
    capacity = max(2, 2 * count // devices)
    owners = code_owner[:, 0]

    position = jnp.arange(count, dtype=jnp.int32)
    same = (owners[:, None] == owners[None, :]) & (position[None, :] < position[:, None])
    ranks = jnp.sum(same.astype(jnp.int32), axis=1)
    slots = owners * capacity + ranks
    slot_ids = jnp.arange(devices * capacity, dtype=jnp.int32)
    to_slot = slot_ids[:, None] == slots[None, :]
    wanted = jnp.max(jnp.where(to_slot, code_row[None, :], -1), axis=1)
    outgoing = pick(to_slot.astype(jnp.bfloat16), cotangent - latents)

    wanted, outgoing, codebook = lax.optimization_barrier((wanted, outgoing, codebook))
    wanted = lax.all_to_all(
        wanted.reshape(devices, 1, capacity), AXES, split_axis=0, concat_axis=0, tiled=True
    ).reshape(-1)
    incoming = lax.all_to_all(
        outgoing.reshape(devices, capacity, width), AXES, split_axis=0, concat_axis=0, tiled=True
    ).reshape(-1, width)

    preact = jnp.dot(codebook, weight_in, preferred_element_type=jnp.float32) + bias_in
    hidden, slope = gelu_parts(preact)
    hidden = hidden.astype(jnp.bfloat16)
    projected = jnp.dot(hidden, weight_out, preferred_element_type=jnp.float32) + bias_out

    row_ids = jnp.arange(rows, dtype=jnp.int32)
    asked = wanted[:, None] == row_ids[None, :]
    picked = pick(asked.astype(jnp.bfloat16), projected)
    incoming, picked = lax.optimization_barrier((incoming, picked))
    answers = lax.all_to_all(
        picked.reshape(devices, capacity, width), AXES, split_axis=0, concat_axis=0, tiled=True
    ).reshape(-1, width)

    by_code = row_ids[:, None] == wanted[None, :]
    times = jnp.sum(by_code.astype(jnp.float32), axis=1, keepdims=True)
    code_grad = pick(by_code.astype(jnp.bfloat16), incoming) + times * projected
    code_low = code_grad.astype(jnp.bfloat16)
    gw_out = lax.dot_general(
        code_low, hidden, (((0,), (0,)), ((), ())), preferred_element_type=jnp.float32
    )
    back = lax.dot_general(
        code_low, weight_out, (((1,), (1,)), ((), ())), preferred_element_type=jnp.float32
    )
    preact_grad = (back * slope).astype(jnp.bfloat16)
    gb_in = jnp.sum(preact_grad.astype(jnp.float32), axis=0)
    gw_in = lax.dot_general(
        codebook, preact_grad, (((0,), (0,)), ((), ())), preferred_element_type=jnp.float32
    )
    gb_out = jnp.sum(code_grad, axis=0)
    biases = jnp.concatenate([gb_in, gb_out])[None, :]
    weights = jnp.concatenate([gw_in, gw_out], axis=0)
    part = lax.psum_scatter(weights, AXES, scatter_dimension=0, tiled=True)
    weights = lax.all_gather(part, AXES, axis=0, tiled=True)
    biases = jnp.sum(lax.all_gather(biases, AXES, axis=0, tiled=True), axis=0)
    dim_in, hidden_size = weight_in.shape
    gw_in, gw_out = weights[:dim_in], weights[dim_in:].T
    gb_in, gb_out = biases[:hidden_size], biases[hidden_size:]

    from_slot = slots[:, None] == slot_ids[None, :]
    chosen = pick(from_slot.astype(jnp.bfloat16), answers)
    latent_grad = cotangent - 0.25 * (chosen - latents)
    return (latent_grad, gw_in, gb_in, gw_out, gb_out)


def solution(mesh):
    rows = P(AXES, None)
    return jax.shard_map(
        per_device,
        mesh=mesh,
        in_specs=(rows, P(), P(), P(), P(), rows, rows, rows, P(AXES)),
        out_specs=(rows, P(), P(), P(), P()),
        check_vma=False,
    )
```

```python
import functools

import jax
import jax.numpy as jnp
from jax import lax
from jax.experimental import pallas as pl
from jax.experimental.pallas import tpu as pltpu
from jax.sharding import Mesh, PartitionSpec as P

scale_gelu = 0.7978845608028654
cubic_term = 0.044715
LANES = 128
EXTRA = 8
AXES = ("outer", "inner", "chip", "core")


def gelu_parts(x):
    tangent = jnp.tanh(scale_gelu * (x + cubic_term * x * x * x))
    value = 0.5 * x * (1.0 + tangent)
    slope = 0.5 * (1.0 + tangent) + 0.5 * x * (1.0 - tangent * tangent) * scale_gelu * (
        1.0 + 3.0 * cubic_term * x * x
    )
    return value, slope


def split_two(x):
    high = lax.reduce_precision(x, 8, 7)
    low = (x - high).astype(jnp.bfloat16)
    return jnp.concatenate([high.astype(jnp.bfloat16), low], axis=1)


def pick(chooser, rows):
    width = rows.shape[1]
    both = jnp.dot(chooser, split_two(rows), preferred_element_type=jnp.float32)
    return both[:, :width] + both[:, width:]


def dot(a, b):
    return jnp.dot(a, b, preferred_element_type=jnp.float32)


def route_kernel(devices, capacity, owner_ref, row_ref, latents_ref, cotangent_ref,
                 out_ref, slot_ref, parts_ref):
    count, width = latents_ref.shape
    step = pl.program_id(0)
    tile = out_ref.shape[0] * capacity

    @pl.when(step == 0)
    def _():
        before = (
            lax.broadcasted_iota(jnp.int32, (LANES, LANES), 0)
            < lax.broadcasted_iota(jnp.int32, (LANES, LANES), 1)
        ).astype(jnp.bfloat16)
        owner_ids = lax.broadcasted_iota(jnp.int32, (devices, LANES), 0)
        lane = lax.broadcasted_iota(jnp.int32, (LANES, LANES), 1)
        seen = jnp.zeros((devices, 1), jnp.float32)
        for start in range(0, count, LANES):
            part = pl.ds(start, LANES)
            owners = owner_ref[:, part]
            mine = (owner_ids == owners).astype(jnp.float32)
            ranks = dot(mine.astype(jnp.bfloat16), before) + seen
            rank = jnp.sum(mine * ranks, axis=0, keepdims=True)
            seen = seen + jnp.sum(mine, axis=1, keepdims=True)
            slot_ref[:, part] = owners * capacity + rank.astype(jnp.int32)
            rows = jnp.transpose(
                jnp.broadcast_to(row_ref[:, part].astype(jnp.float32), (LANES, LANES))
            )
            tall = jnp.floor(rows * (1.0 / 32.0))
            extra = jnp.where(lane == 0, tall, jnp.where(lane == 1, rows - 32.0 * tall, 0.0))
            extra = jnp.where(lane == 2, 1.0, extra)
            parts_ref[part, 2 * width :] = extra.astype(jnp.bfloat16)
            value = cotangent_ref[part, :] - latents_ref[part, :]
            high = value.astype(jnp.bfloat16)
            parts_ref[part, :width] = high
            parts_ref[part, width : 2 * width] = (value - high.astype(jnp.float32)).astype(
                jnp.bfloat16
            )

    ids = lax.broadcasted_iota(jnp.int32, (tile, count), 0) + step * tile
    chooser = (ids == slot_ref[...]).astype(jnp.float32).astype(jnp.bfloat16)
    both = dot(chooser, parts_ref[...])
    value = both[:, :width] + both[:, width : 2 * width]
    turned = jnp.transpose(both[:, 2 * width :])
    wanted = 32.0 * turned[0:1] + turned[1:2] + turned[2:3] - 1.0
    lane = lax.broadcasted_iota(jnp.int32, (EXTRA, LANES), 1)
    for k in range(out_ref.shape[0]):
        own = slice(k * capacity, (k + 1) * capacity)
        for j in range(width // LANES):
            out_ref[k, j * capacity : (j + 1) * capacity, :] = value[own, j * LANES : (j + 1) * LANES]
        at = k * capacity // LANES * LANES
        row = jnp.broadcast_to(wanted[:, at : at + LANES], (EXTRA, LANES))
        shift = k * capacity - at
        if shift:
            row = pltpu.roll(row, LANES - shift, 1)
        out_ref[k, width // LANES * capacity :, :] = jnp.where(lane < capacity, row, -1.0)


def route(devices, capacity, code_owner, code_row, latents, cotangent):
    count, width = latents.shape
    per_step = max(1, 256 // capacity)
    block = width // LANES * capacity + EXTRA
    whole = lambda *shape: pl.BlockSpec(shape, lambda i: (0,) * len(shape))
    return pl.pallas_call(
        functools.partial(route_kernel, devices, capacity),
        grid=(devices // per_step,),
        in_specs=[whole(1, count), whole(1, count), whole(count, width), whole(count, width)],
        out_specs=[
            pl.BlockSpec((per_step, block, LANES), lambda i: (i, 0, 0)),
            whole(1, count),
        ],
        out_shape=[
            jax.ShapeDtypeStruct((devices, block, LANES), jnp.float32),
            jax.ShapeDtypeStruct((1, count), jnp.int32),
        ],
        scratch_shapes=[pltpu.VMEM((count, 2 * width + LANES), jnp.bfloat16)],
        compiler_params=pltpu.CompilerParams(vmem_limit_bytes=40 * 2**20),
        name="route",
    )(code_owner.reshape(1, count), code_row.reshape(1, count), latents, cotangent)


def backward_kernel(sizes, capacity, incoming_hbm, hidden_hbm, slope_hbm, projected_hbm,
                    codebook_hbm, weight_hbm, mine_hbm, theirs_hbm, incoming, hidden, slope,
                    projected, codebook, weight, parts, wanted, low, grad, flat, in_sem, out_sem):
    outer, inner, chip, core = sizes
    devices = outer * inner * chip * core
    me = lax.axis_index("core")
    width = projected.shape[1]
    dim_in, rows = codebook.shape
    hidden_size = hidden.shape[0]
    length = flat.shape[1] - EXTRA
    pairs = list(zip(
        (incoming_hbm, projected_hbm, weight_hbm, slope_hbm, hidden_hbm, codebook_hbm),
        (incoming, projected, weight, slope, hidden, codebook),
    ))
    loads = [pltpu.make_async_copy(a, b, in_sem.at[k]) for k, (a, b) in enumerate(pairs)]
    for load in loads:
        load.start()
    for d in range(devices):
        flat[d, length:, :] = jnp.zeros((EXTRA, LANES), jnp.float32)
    loads[0].wait()

    blocks = width // LANES
    for s in range(devices):
        own = pl.ds(s * capacity, capacity)
        for j in range(blocks):
            value = incoming[s, j * capacity : (j + 1) * capacity, :]
            high = value.astype(jnp.bfloat16)
            parts[own, j * LANES : (j + 1) * LANES] = high
            parts[own, width + j * LANES : width + (j + 1) * LANES] = (
                value - high.astype(jnp.float32)
            ).astype(jnp.bfloat16)
    per_row = LANES // capacity
    for t in range(devices * capacity // LANES):
        row = None
        for k in range(per_row):
            one = incoming[t * per_row + k, blocks * capacity :, :]
            if k:
                one = pltpu.roll(one, k * capacity, 1)
            row = one if row is None else jnp.maximum(row, one)
        wanted[:, t * LANES : (t + 1) * LANES] = row.astype(jnp.int32)

    loads[1].wait()
    loads[2].wait()
    loads[3].wait()
    tile = min(256, rows)
    bias_in = jnp.zeros((1, hidden_size), jnp.float32)
    bias_out = jnp.zeros((1, width), jnp.float32)
    for start in range(0, rows, tile):
        part = pl.ds(start, tile)
        ids = lax.broadcasted_iota(jnp.int32, (tile, wanted.shape[1]), 0) + start
        chooser = (ids == wanted[0:1, :]).astype(jnp.float32)
        times = jnp.sum(chooser, axis=1, keepdims=True)
        both = dot(chooser.astype(jnp.bfloat16), parts[...])
        code_grad = both[:, :width] + both[:, width:] + times * projected[part, :]
        bias_out += jnp.sum(code_grad, axis=0, keepdims=True)
        code_low = code_grad.astype(jnp.bfloat16)
        low[part, :] = code_low
        preact_grad = (dot(code_low, weight[...]) * slope[part, :]).astype(jnp.bfloat16)
        grad[part, :] = preact_grad
        bias_in += jnp.sum(preact_grad.astype(jnp.float32), axis=0, keepdims=True)

    biases = [bias_in[:, k : k + LANES] for k in range(0, hidden_size, LANES)]
    biases += [bias_out[:, k : k + LANES] for k in range(0, width, LANES)]
    for j, bias in enumerate(biases):
        flat[j // EXTRA, length + j % EXTRA : length + j % EXTRA + 1, :] = bias

    places = {}
    for i in range(inner):
        for x in range(chip):
            for o in range(outer):
                places[((o * inner + i) * chip + x) * core] = (i * chip + x) * outer + o
    stores = []

    def send(first, last):
        for d in range(first, last, core):
            for target, shift in ((theirs_hbm, 1 - me), (mine_hbm, me)):
                k = len(stores)
                copy = pltpu.make_async_copy(
                    flat.at[d + shift], target.at[places[d]], out_sem.at[k]
                )
                copy.start()
                stores.append(copy)

    def keep(row, value):
        for k in range(0, value.shape[0], length):
            flat[(row + k) // length, :length, :] = value[k : k + length, :]

    base = dim_in * hidden_size // LANES
    loads[4].wait()
    out = dot(hidden[...], low[...])
    for j in range(blocks):
        keep(base + j * hidden_size, out[:, j * LANES : (j + 1) * LANES])
    send(base // length, devices)
    loads[5].wait()
    wide = 2 * LANES
    done = 0
    for start in range(0, hidden_size, wide):
        out = dot(codebook[...], grad[:, start : start + wide])
        for j in range(wide // LANES):
            keep((start // LANES + j) * dim_in, out[:, j * LANES : (j + 1) * LANES])
        ready = (start + wide) // LANES * dim_in // length // core * core
        send(done, ready)
        done = ready
    for copy in stores:
        copy.wait()


def backward(sizes, capacity, incoming, hidden_t, slope, projected, codebook_t, weight_t):
    devices = incoming.shape[0]
    rows, width = projected.shape
    dim_in, hidden_size = codebook_t.shape[0], hidden_t.shape[0]
    length = (dim_in + width) * hidden_size // LANES // devices
    half = jax.ShapeDtypeStruct((devices // 2, length + EXTRA, LANES), jnp.float32)
    operands = (incoming, hidden_t, slope, projected, codebook_t, weight_t)
    vmem = lambda shape, dtype: pltpu.VMEM(shape, dtype)
    slots = devices * capacity
    return pl.pallas_call(
        functools.partial(backward_kernel, sizes, capacity),
        in_specs=[pl.BlockSpec(memory_space=pl.ANY)] * 6,
        out_specs=[pl.BlockSpec(memory_space=pl.ANY)] * 2,
        out_shape=[half, half],
        scratch_shapes=[vmem(a.shape, a.dtype) for a in operands]
        + [
            vmem((slots, 2 * width), jnp.bfloat16),
            vmem((EXTRA, slots), jnp.int32),
            vmem((rows, width), jnp.bfloat16),
            vmem((rows, hidden_size), jnp.bfloat16),
            vmem((devices, length + EXTRA, LANES), jnp.float32),
            pltpu.SemaphoreType.DMA((6,)),
            pltpu.SemaphoreType.DMA((devices,)),
        ],
        compiler_params=pltpu.CompilerParams(vmem_limit_bytes=56 * 2**20),
        name="backward",
    )(*operands)


def assemble_kernel(total_hbm, weight_in_hbm, weight_out_hbm, sems):
    devices = total_hbm.shape[0]
    length = total_hbm.shape[1] - EXTRA
    dim_in, hidden_size = weight_in_hbm.shape
    copies = []
    for d in range(devices):
        at, target, height = d * length, weight_in_hbm, dim_in
        if at >= dim_in * hidden_size // LANES:
            at, target, height = at - dim_in * hidden_size // LANES, weight_out_hbm, hidden_size
        place = target.at[
            pl.ds(at % height, length), pl.ds(at // height * LANES, LANES)
        ]
        copy = pltpu.make_async_copy(total_hbm.at[d, pl.ds(0, length)], place, sems.at[d])
        copy.start()
        copies.append(copy)
    for copy in copies:
        copy.wait()


def assemble(total, dim_in, hidden_size, width):
    hbm = pl.BlockSpec(memory_space=pl.ANY)
    return pl.pallas_call(
        assemble_kernel,
        in_specs=[hbm],
        out_specs=[hbm, hbm],
        out_shape=[
            jax.ShapeDtypeStruct((dim_in, hidden_size), jnp.float32),
            jax.ShapeDtypeStruct((hidden_size, width), jnp.float32),
        ],
        scratch_shapes=[pltpu.SemaphoreType.DMA((total.shape[0],))],
        name="assemble",
    )(total)


def per_device(
    sizes, codebook, weight_in, bias_in, weight_out, bias_out, latents, cotangent, code_owner, code_row
):
    outer, inner, chip, core = sizes
    devices = outer * inner * chip * core
    rows, dim_in = codebook.shape
    hidden_size = weight_in.shape[1]
    count, width = latents.shape
    capacity = max(2, 2 * count // devices)

    outgoing, slots = route(devices, capacity, code_owner, code_row, latents, cotangent)
    outgoing, codebook = lax.optimization_barrier((outgoing, codebook))
    incoming = lax.all_to_all(outgoing, AXES, split_axis=0, concat_axis=0, tiled=True)

    preact = dot(codebook, weight_in) + bias_in
    hidden, slope = gelu_parts(preact)
    hidden = hidden.astype(jnp.bfloat16)
    projected = dot(hidden, weight_out) + bias_out

    mine, theirs = backward(
        sizes, capacity, incoming, hidden.T, slope, projected, codebook.T, weight_out.T
    )
    theirs, incoming = lax.optimization_barrier((theirs, incoming))
    arrived = lax.ppermute(theirs, "core", [(k, core - 1 - k) for k in range(core)])

    wanted = incoming[:, -EXTRA, :capacity].reshape(-1)
    asked = wanted[:, None] == jnp.arange(rows, dtype=jnp.float32)[None, :]
    picked = pick(asked.astype(jnp.bfloat16), projected)
    answers = lax.all_to_all(
        picked.reshape(devices, capacity, width), AXES, split_axis=0, concat_axis=0, tiled=True
    ).reshape(-1, width)

    part = mine + arrived
    part = part.reshape((inner * chip, outer) + part.shape[1:])
    part = lax.all_to_all(part, ("inner", "chip"), split_axis=0, concat_axis=0, tiled=True)
    part = jnp.sum(part, axis=0)
    part = lax.all_to_all(part, "outer", split_axis=0, concat_axis=0, tiled=True)
    part = jnp.sum(part, axis=0, keepdims=True)
    total = lax.all_gather(part, AXES, axis=0, tiled=True)
    gw_in, gw_out = assemble(total, dim_in, hidden_size, width)
    biases = total[:2, -EXTRA:, :].reshape(-1)
    gb_in, gb_out = biases[:hidden_size], biases[hidden_size : hidden_size + width]

    slot_ids = jnp.arange(devices * capacity, dtype=jnp.int32)
    from_slot = slots.reshape(-1, 1) == slot_ids[None, :]
    chosen = pick(from_slot.astype(jnp.bfloat16), answers)
    latent_grad = cotangent - 0.25 * (chosen - latents)
    return (latent_grad, gw_in, gb_in, gw_out, gb_out)


def solution(mesh):
    code, data = mesh.shape["code"], mesh.shape["dp"]
    core = 2
    outer = 1
    while outer * outer < code:
        outer *= 2
    sizes = (outer, code // outer, data // core, core)
    fine = Mesh(mesh.devices.reshape(sizes), AXES)
    rows = P(AXES, None)
    return jax.shard_map(
        functools.partial(per_device, sizes),
        mesh=fine,
        in_specs=(rows, P(), P(), P(), P(), rows, rows, rows, P(AXES)),
        out_specs=(rows, P(), P(), P(), P()),
        check_vma=False,
    )
```

```python
import functools

import jax
import jax.numpy as jnp
from jax import lax
from jax.experimental import pallas as pl
from jax.experimental.pallas import tpu as pltpu
from jax.sharding import Mesh, PartitionSpec as P

scale_gelu = 0.7978845608028654
cubic_term = 0.044715
LANES = 128
EXTRA = 8
AXES = ("outer", "inner", "chip", "core")


def gelu_parts(x):
    tangent = jnp.tanh(scale_gelu * (x + cubic_term * x * x * x))
    value = 0.5 * x * (1.0 + tangent)
    slope = 0.5 * (1.0 + tangent) + 0.5 * x * (1.0 - tangent * tangent) * scale_gelu * (
        1.0 + 3.0 * cubic_term * x * x
    )
    return value, slope


def split_two(x):
    high = lax.reduce_precision(x, 8, 7)
    low = (x - high).astype(jnp.bfloat16)
    return jnp.concatenate([high.astype(jnp.bfloat16), low], axis=1)


def pick(chooser, rows):
    width = rows.shape[1]
    both = jnp.dot(chooser, split_two(rows), preferred_element_type=jnp.float32)
    return both[:, :width] + both[:, width:]


def dot(a, b):
    return jnp.dot(a, b, preferred_element_type=jnp.float32)


def route_kernel(devices, capacity, owner_ref, row_ref, latents_ref, cotangent_ref,
                 out_ref, slot_ref, parts_ref):
    count, width = latents_ref.shape
    step = pl.program_id(0)
    tile = out_ref.shape[0] * capacity

    @pl.when(step == 0)
    def _():
        before = (
            lax.broadcasted_iota(jnp.int32, (LANES, LANES), 0)
            < lax.broadcasted_iota(jnp.int32, (LANES, LANES), 1)
        ).astype(jnp.bfloat16)
        owner_ids = lax.broadcasted_iota(jnp.int32, (devices, LANES), 0)
        lane = lax.broadcasted_iota(jnp.int32, (LANES, LANES), 1)
        seen = jnp.zeros((devices, 1), jnp.float32)
        for start in range(0, count, LANES):
            part = pl.ds(start, LANES)
            owners = owner_ref[:, part]
            mine = (owner_ids == owners).astype(jnp.float32)
            ranks = dot(mine.astype(jnp.bfloat16), before) + seen
            rank = jnp.sum(mine * ranks, axis=0, keepdims=True)
            seen = seen + jnp.sum(mine, axis=1, keepdims=True)
            slot_ref[:, part] = owners * capacity + rank.astype(jnp.int32)
            rows = jnp.transpose(
                jnp.broadcast_to(row_ref[:, part].astype(jnp.float32), (LANES, LANES))
            )
            tall = jnp.floor(rows * (1.0 / 32.0))
            extra = jnp.where(lane == 0, tall, jnp.where(lane == 1, rows - 32.0 * tall, 0.0))
            extra = jnp.where(lane == 2, 1.0, extra)
            parts_ref[part, 2 * width :] = extra.astype(jnp.bfloat16)
            value = cotangent_ref[part, :] - latents_ref[part, :]
            high = value.astype(jnp.bfloat16)
            parts_ref[part, :width] = high
            parts_ref[part, width : 2 * width] = (value - high.astype(jnp.float32)).astype(
                jnp.bfloat16
            )

    ids = lax.broadcasted_iota(jnp.int32, (tile, count), 0) + step * tile
    chooser = (ids == slot_ref[...]).astype(jnp.float32).astype(jnp.bfloat16)
    both = dot(chooser, parts_ref[...])
    value = both[:, :width] + both[:, width : 2 * width]
    turned = jnp.transpose(both[:, 2 * width :])
    wanted = 32.0 * turned[0:1] + turned[1:2] + turned[2:3] - 1.0
    lane = lax.broadcasted_iota(jnp.int32, (EXTRA, LANES), 1)
    for k in range(out_ref.shape[0]):
        own = slice(k * capacity, (k + 1) * capacity)
        for j in range(width // LANES):
            out_ref[k, j * capacity : (j + 1) * capacity, :] = value[own, j * LANES : (j + 1) * LANES]
        at = k * capacity // LANES * LANES
        row = jnp.broadcast_to(wanted[:, at : at + LANES], (EXTRA, LANES))
        shift = k * capacity - at
        if shift:
            row = pltpu.roll(row, LANES - shift, 1)
        out_ref[k, width // LANES * capacity :, :] = jnp.where(lane < capacity, row, -1.0)


def route(devices, capacity, code_owner, code_row, latents, cotangent):
    count, width = latents.shape
    per_step = max(1, 256 // capacity)
    block = width // LANES * capacity + EXTRA
    whole = lambda *shape: pl.BlockSpec(shape, lambda i: (0,) * len(shape))
    return pl.pallas_call(
        functools.partial(route_kernel, devices, capacity),
        grid=(devices // per_step,),
        in_specs=[whole(1, count), whole(1, count), whole(count, width), whole(count, width)],
        out_specs=[
            pl.BlockSpec((per_step, block, LANES), lambda i: (i, 0, 0)),
            whole(1, count),
        ],
        out_shape=[
            jax.ShapeDtypeStruct((devices, block, LANES), jnp.float32),
            jax.ShapeDtypeStruct((1, count), jnp.int32),
        ],
        scratch_shapes=[pltpu.VMEM((count, 2 * width + LANES), jnp.bfloat16)],
        compiler_params=pltpu.CompilerParams(vmem_limit_bytes=40 * 2**20),
        name="route",
    )(code_owner.reshape(1, count), code_row.reshape(1, count), latents, cotangent)


def backward_kernel(sizes, capacity, incoming_hbm, hidden_hbm, slope_hbm, projected_hbm,
                    codebook_hbm, weight_hbm, *refs):
    outer, inner, chip, core = sizes
    devices = outer * inner * chip * core
    mine_hbm, theirs_hbm, refs = refs[:outer], refs[outer : 2 * outer], refs[2 * outer :]
    (incoming, hidden, slope, projected, codebook, weight, parts, wanted, low, grad, flat,
     in_sem, out_sem) = refs
    width = projected.shape[1]
    dim_in, rows = codebook.shape
    hidden_size = hidden.shape[0]
    length = flat.shape[1] - EXTRA
    pairs = list(zip(
        (incoming_hbm, projected_hbm, weight_hbm, slope_hbm, hidden_hbm, codebook_hbm),
        (incoming, projected, weight, slope, hidden, codebook),
    ))
    loads = [pltpu.make_async_copy(a, b, in_sem.at[k]) for k, (a, b) in enumerate(pairs)]
    for load in loads:
        load.start()
    for d in range(devices):
        flat[d, length:, :] = jnp.zeros((EXTRA, LANES), jnp.float32)
    loads[0].wait()

    blocks = width // LANES
    for s in range(devices):
        own = pl.ds(s * capacity, capacity)
        for j in range(blocks):
            value = incoming[s, j * capacity : (j + 1) * capacity, :]
            high = value.astype(jnp.bfloat16)
            parts[own, j * LANES : (j + 1) * LANES] = high
            parts[own, width + j * LANES : width + (j + 1) * LANES] = (
                value - high.astype(jnp.float32)
            ).astype(jnp.bfloat16)
    per_row = LANES // capacity
    for t in range(devices * capacity // LANES):
        row = None
        for k in range(per_row):
            one = incoming[t * per_row + k, blocks * capacity :, :]
            if k:
                one = pltpu.roll(one, k * capacity, 1)
            row = one if row is None else jnp.maximum(row, one)
        wanted[:, t * LANES : (t + 1) * LANES] = row.astype(jnp.int32)

    loads[1].wait()
    loads[2].wait()
    loads[3].wait()
    tile = min(256, rows)
    bias_in = jnp.zeros((1, hidden_size), jnp.float32)
    bias_out = jnp.zeros((1, width), jnp.float32)
    for start in range(0, rows, tile):
        part = pl.ds(start, tile)
        ids = lax.broadcasted_iota(jnp.int32, (tile, wanted.shape[1]), 0) + start
        chooser = (ids == wanted[0:1, :]).astype(jnp.float32)
        times = jnp.sum(chooser, axis=1, keepdims=True)
        both = dot(chooser.astype(jnp.bfloat16), parts[...])
        code_grad = both[:, :width] + both[:, width:] + times * projected[part, :]
        bias_out += jnp.sum(code_grad, axis=0, keepdims=True)
        code_low = code_grad.astype(jnp.bfloat16)
        low[part, :] = code_low
        preact_grad = (dot(code_low, weight[...]) * slope[part, :]).astype(jnp.bfloat16)
        grad[part, :] = preact_grad
        bias_in += jnp.sum(preact_grad.astype(jnp.float32), axis=0, keepdims=True)

    biases = [bias_in[:, k : k + LANES] for k in range(0, hidden_size, LANES)]
    biases += [bias_out[:, k : k + LANES] for k in range(0, width, LANES)]
    for j, bias in enumerate(biases):
        flat[j // EXTRA, length + j % EXTRA : length + j % EXTRA + 1, :] = bias

    first = lax.axis_index("outer")
    plane = lax.axis_index("inner") * chip + lax.axis_index("chip")
    me = lax.axis_index("core")
    stores = []

    def send(k):
        o = lax.rem(first + k, outer)
        for target, c in ((theirs_hbm, 1 - me), (mine_hbm, me)):
            for j in range(inner * chip):
                d = (o * inner * chip + lax.bitwise_xor(plane, j)) * core + c
                copy = pltpu.make_async_copy(flat.at[d], target[k].at[j], out_sem.at[len(stores)])
                copy.start()
                stores.append(copy)

    def keep(row, value):
        for k in range(0, value.shape[0], length):
            flat[(row + k) // length, :length, :] = value[k : k + length, :]

    base = dim_in * hidden_size // LANES
    loads[4].wait()
    out = dot(hidden[...], low[...])
    for j in range(blocks):
        keep(base + j * hidden_size, out[:, j * LANES : (j + 1) * LANES])
    loads[5].wait()
    wide = 2 * LANES
    for start in range(0, hidden_size, wide):
        out = dot(codebook[...], grad[:, start : start + wide])
        for j in range(wide // LANES):
            keep((start // LANES + j) * dim_in, out[:, j * LANES : (j + 1) * LANES])
    for k in range(outer - 1, -1, -1):
        send(k)
    for copy in stores:
        copy.wait()


def backward(sizes, capacity, incoming, hidden_t, slope, projected, codebook_t, weight_t):
    devices = incoming.shape[0]
    rows, width = projected.shape
    dim_in, hidden_size = codebook_t.shape[0], hidden_t.shape[0]
    length = (dim_in + width) * hidden_size // LANES // devices
    outer, inner, chip, _ = sizes
    piece = jax.ShapeDtypeStruct((inner * chip, length + EXTRA, LANES), jnp.float32)
    operands = (incoming, hidden_t, slope, projected, codebook_t, weight_t)
    vmem = lambda shape, dtype: pltpu.VMEM(shape, dtype)
    slots = devices * capacity
    return pl.pallas_call(
        functools.partial(backward_kernel, sizes, capacity),
        in_specs=[pl.BlockSpec(memory_space=pl.ANY)] * 6,
        out_specs=[pl.BlockSpec(memory_space=pl.ANY)] * (2 * outer),
        out_shape=[piece] * (2 * outer),
        scratch_shapes=[vmem(a.shape, a.dtype) for a in operands]
        + [
            vmem((slots, 2 * width), jnp.bfloat16),
            vmem((EXTRA, slots), jnp.int32),
            vmem((rows, width), jnp.bfloat16),
            vmem((rows, hidden_size), jnp.bfloat16),
            vmem((devices, length + EXTRA, LANES), jnp.float32),
            pltpu.SemaphoreType.DMA((6,)),
            pltpu.SemaphoreType.DMA((devices,)),
        ],
        compiler_params=pltpu.CompilerParams(vmem_limit_bytes=56 * 2**20),
        name="backward",
    )(*operands)


def assemble_kernel(sizes, *refs):
    outer, inner, chip, core = sizes
    devices = outer * inner * chip * core
    pieces, (weight_in, weight_out, biases), (held, sems) = (
        refs[:devices], refs[devices : devices + 3], refs[devices + 3 :]
    )
    length = held.shape[1] - EXTRA
    dim_in, hidden_size = weight_in.shape
    base = dim_in * hidden_size // LANES
    first = lax.axis_index("outer")
    plane = lax.axis_index("inner") * chip + lax.axis_index("chip")
    me = lax.axis_index("core")
    loads = []
    for k, piece in enumerate(pieces):
        load = pltpu.make_async_copy(piece, held.at[k], sems.at[k])
        load.start()
        loads.append(load)
    for k, load in enumerate(loads):
        c = k // (outer * inner * chip)
        o, j = divmod(k % (outer * inner * chip), inner * chip)
        o = lax.rem(first + outer - o, outer)
        d = (o * inner * chip + lax.bitwise_xor(plane, j)) * core + lax.bitwise_xor(me, c)
        load.wait()

        def put(target, at, k=k):
            height = target.shape[0]
            rows = pl.ds(pl.multiple_of(lax.rem(at, height), length), length)
            lanes = pl.ds(pl.multiple_of(lax.div(at, height) * LANES, LANES), LANES)
            target[rows, lanes] = held[k, :length, :]

        @pl.when(d * length < base)
        def _():
            put(weight_in, d * length)

        @pl.when(d * length >= base)
        def _():
            put(weight_out, d * length - base)

        @pl.when(d < 2)
        def _():
            biases[d] = held[k, length:, :]


def assemble(sizes, pieces, dim_in, hidden_size, width):
    hbm = pl.BlockSpec(memory_space=pl.ANY)
    vmem = pl.BlockSpec(memory_space=pltpu.VMEM)
    return pl.pallas_call(
        functools.partial(assemble_kernel, sizes),
        in_specs=[hbm] * len(pieces),
        out_specs=[vmem] * 3,
        out_shape=[
            jax.ShapeDtypeStruct((dim_in, hidden_size), jnp.float32),
            jax.ShapeDtypeStruct((hidden_size, width), jnp.float32),
            jax.ShapeDtypeStruct((2, EXTRA, LANES), jnp.float32),
        ],
        scratch_shapes=[
            pltpu.VMEM((len(pieces),) + pieces[0].shape, jnp.float32),
            pltpu.SemaphoreType.DMA((len(pieces),)),
        ],
        compiler_params=pltpu.CompilerParams(vmem_limit_bytes=32 * 2**20),
        name="assemble",
    )(*pieces)


def sum_chunks(sizes, mine, theirs):
    outer, inner, chip, core = sizes
    planes = inner * chip

    def along(x, k):
        return lax.ppermute(x, "outer", [(o, (o + k) % outer) for o in range(outer)])

    def plane(x, j):
        return lax.ppermute(x, ("inner", "chip"), [(p, p ^ j) for p in range(planes)])

    def other(x):
        return lax.ppermute(x, "core", [(c, core - 1 - c) for c in range(core)])

    total = None
    for k in range(outer - 1, -1, -1):
        arrived = other(theirs[k])
        part = mine[k][0] + arrived[0]
        for j in range(1, planes):
            part = part + plane(mine[k][j] + arrived[j], j)
        if k:
            part = along(part, k)
        total = part if total is None else total + part

    near = [along(total, k) if k else total for k in range(outer)]
    near = [plane(x, j) if j else x for x in near for j in range(planes)]
    return near + [other(x) for x in near]


def per_device(
    sizes, codebook, weight_in, bias_in, weight_out, bias_out, latents, cotangent, code_owner, code_row
):
    outer, inner, chip, core = sizes
    devices = outer * inner * chip * core
    rows, dim_in = codebook.shape
    hidden_size = weight_in.shape[1]
    count, width = latents.shape
    capacity = max(2, 2 * count // devices)

    outgoing, slots = route(devices, capacity, code_owner, code_row, latents, cotangent)
    outgoing, bias_in = lax.optimization_barrier((outgoing, bias_in))
    incoming = lax.all_to_all(outgoing, AXES, split_axis=0, concat_axis=0, tiled=True)

    preact = dot(codebook, weight_in) + bias_in
    hidden, slope = gelu_parts(preact)
    hidden = hidden.astype(jnp.bfloat16)
    projected = dot(hidden, weight_out) + bias_out

    pieces = backward(
        sizes, capacity, incoming, hidden.T, slope, projected, codebook.T, weight_out.T
    )
    mine, theirs = list(pieces[:outer]), list(pieces[outer:])
    theirs[-1], incoming = lax.optimization_barrier((theirs[-1], incoming))

    wanted = incoming[:, -EXTRA, :capacity].reshape(-1)
    asked = wanted[:, None] == jnp.arange(rows, dtype=jnp.float32)[None, :]
    picked = pick(asked.astype(jnp.bfloat16), projected)
    answers = lax.all_to_all(
        picked.reshape(devices, capacity, width), AXES, split_axis=0, concat_axis=0, tiled=True
    ).reshape(-1, width)

    chunks = sum_chunks(sizes, mine, theirs)
    gw_in, gw_out, biases = assemble(sizes, chunks, dim_in, hidden_size, width)
    biases = biases.reshape(-1)
    gb_in, gb_out = biases[:hidden_size], biases[hidden_size : hidden_size + width]

    slot_ids = jnp.arange(devices * capacity, dtype=jnp.int32)
    from_slot = slots.reshape(-1, 1) == slot_ids[None, :]
    chosen = pick(from_slot.astype(jnp.bfloat16), answers)
    latent_grad = cotangent - 0.25 * (chosen - latents)
    return (latent_grad, gw_in, gb_in, gw_out, gb_out)


def solution(mesh):
    code, data = mesh.shape["code"], mesh.shape["dp"]
    core = 2
    outer = 1
    while outer * outer < code:
        outer *= 2
    sizes = (outer, code // outer, data // core, core)
    fine = Mesh(mesh.devices.reshape(sizes), AXES)
    rows = P(AXES, None)
    return jax.shard_map(
        functools.partial(per_device, sizes),
        mesh=fine,
        in_specs=(rows, P(), P(), P(), P(), rows, rows, rows, P(AXES)),
        out_specs=(rows, P(), P(), P(), P()),
        check_vma=False,
    )
```

```python
import functools

import jax
import jax.numpy as jnp
from jax import lax
from jax.experimental import pallas as pl
from jax.experimental.pallas import tpu as pltpu
from jax.sharding import Mesh, PartitionSpec as P

scale_gelu = 0.7978845608028654
cubic_term = 0.044715
LANES = 128
EXTRA = 8
AXES = ("outer", "inner", "chip", "core")


def gelu_parts(x):
    tangent = jnp.tanh(scale_gelu * (x + cubic_term * x * x * x))
    value = 0.5 * x * (1.0 + tangent)
    slope = 0.5 * (1.0 + tangent) + 0.5 * x * (1.0 - tangent * tangent) * scale_gelu * (
        1.0 + 3.0 * cubic_term * x * x
    )
    return value, slope


def split_two(x):
    high = lax.reduce_precision(x, 8, 7)
    low = (x - high).astype(jnp.bfloat16)
    return jnp.concatenate([high.astype(jnp.bfloat16), low], axis=1)


def pick(chooser, rows):
    width = rows.shape[1]
    both = jnp.dot(chooser, split_two(rows), preferred_element_type=jnp.float32)
    return both[:, :width] + both[:, width:]


def dot(a, b):
    return jnp.dot(a, b, preferred_element_type=jnp.float32)


def route_kernel(devices, capacity, owner_hbm, row_hbm, latents_hbm, cotangent_hbm,
                 out_ref, slot_ref, owner_ref, row_ref, latents_ref, cotangent_ref, parts_ref, sems):
    count, width = latents_ref.shape
    step = pl.program_id(0)
    tile = out_ref.shape[0] * capacity

    @pl.when(step == 0)
    def _():
        loads = [
            pltpu.make_async_copy(a, b, sems.at[k])
            for k, (a, b) in enumerate((
                (owner_hbm, owner_ref), (row_hbm, row_ref),
                (latents_hbm, latents_ref), (cotangent_hbm, cotangent_ref),
            ))
        ]
        for load in loads:
            load.start()
        before = (
            lax.broadcasted_iota(jnp.int32, (LANES, LANES), 0)
            < lax.broadcasted_iota(jnp.int32, (LANES, LANES), 1)
        ).astype(jnp.bfloat16)
        owner_ids = lax.broadcasted_iota(jnp.int32, (devices, LANES), 0)
        lane = lax.broadcasted_iota(jnp.int32, (LANES, LANES), 1)
        seen = jnp.zeros((devices, 1), jnp.float32)
        loads[0].wait()
        loads[1].wait()
        for start in range(0, count, LANES):
            part = pl.ds(start, LANES)
            owners = owner_ref[:, part]
            mine = (owner_ids == owners).astype(jnp.float32)
            ranks = dot(mine.astype(jnp.bfloat16), before) + seen
            rank = jnp.sum(mine * ranks, axis=0, keepdims=True)
            seen = seen + jnp.sum(mine, axis=1, keepdims=True)
            slot_ref[:, part] = owners * capacity + rank.astype(jnp.int32)
            rows = jnp.transpose(
                jnp.broadcast_to(row_ref[:, part].astype(jnp.float32), (LANES, LANES))
            )
            tall = jnp.floor(rows * (1.0 / 32.0))
            extra = jnp.where(lane == 0, tall, jnp.where(lane == 1, rows - 32.0 * tall, 0.0))
            extra = jnp.where(lane == 2, 1.0, extra)
            parts_ref[part, 2 * width :] = extra.astype(jnp.bfloat16)
        loads[2].wait()
        loads[3].wait()
        for start in range(0, count, LANES):
            part = pl.ds(start, LANES)
            value = cotangent_ref[part, :] - latents_ref[part, :]
            high = value.astype(jnp.bfloat16)
            parts_ref[part, :width] = high
            parts_ref[part, width : 2 * width] = (value - high.astype(jnp.float32)).astype(
                jnp.bfloat16
            )

    ids = lax.broadcasted_iota(jnp.int32, (tile, count), 0) + step * tile
    chooser = (ids == slot_ref[...]).astype(jnp.float32).astype(jnp.bfloat16)
    both = dot(chooser, parts_ref[...])
    value = both[:, :width] + both[:, width : 2 * width]
    turned = jnp.transpose(both[:, 2 * width :])
    wanted = 32.0 * turned[0:1] + turned[1:2] + turned[2:3] - 1.0
    lane = lax.broadcasted_iota(jnp.int32, (EXTRA, LANES), 1)
    for k in range(out_ref.shape[0]):
        own = slice(k * capacity, (k + 1) * capacity)
        for j in range(width // LANES):
            out_ref[k, j * capacity : (j + 1) * capacity, :] = value[own, j * LANES : (j + 1) * LANES]
        at = k * capacity // LANES * LANES
        row = jnp.broadcast_to(wanted[:, at : at + LANES], (EXTRA, LANES))
        shift = k * capacity - at
        if shift:
            row = pltpu.roll(row, LANES - shift, 1)
        out_ref[k, width // LANES * capacity :, :] = jnp.where(lane < capacity, row, -1.0)


def route(devices, capacity, code_owner, code_row, latents, cotangent):
    count, width = latents.shape
    per_step = max(1, 256 // capacity)
    block = width // LANES * capacity + EXTRA
    whole = lambda *shape: pl.BlockSpec(shape, lambda i: (0,) * len(shape))
    return pl.pallas_call(
        functools.partial(route_kernel, devices, capacity),
        grid=(devices // per_step,),
        in_specs=[pl.BlockSpec(memory_space=pl.ANY)] * 4,
        out_specs=[
            pl.BlockSpec((per_step, block, LANES), lambda i: (i, 0, 0)),
            whole(1, count),
        ],
        out_shape=[
            jax.ShapeDtypeStruct((devices, block, LANES), jnp.float32),
            jax.ShapeDtypeStruct((1, count), jnp.int32),
        ],
        scratch_shapes=[
            pltpu.VMEM((1, count), jnp.int32),
            pltpu.VMEM((1, count), jnp.int32),
            pltpu.VMEM((count, width), jnp.float32),
            pltpu.VMEM((count, width), jnp.float32),
            pltpu.VMEM((count, 2 * width + LANES), jnp.bfloat16),
            pltpu.SemaphoreType.DMA((4,)),
        ],
        compiler_params=pltpu.CompilerParams(vmem_limit_bytes=60 * 2**20),
        name="route",
    )(code_owner.reshape(1, count), code_row.reshape(1, count), latents, cotangent)


def place(sizes, k, j):
    _, inner, chip, _ = sizes
    if k % 2:
        return j
    return j % inner * chip + j // inner


def backward_kernel(sizes, capacity, incoming_hbm, hidden_hbm, slope_hbm, projected_hbm,
                    codebook_hbm, weight_hbm, *refs):
    outer, inner, chip, core = sizes
    devices = outer * inner * chip * core
    mine_hbm, theirs_hbm, refs = refs[:outer], refs[outer : 2 * outer], refs[2 * outer :]
    (incoming, hidden, slope, projected, codebook, weight, parts, wanted, low, grad, flat,
     in_sem, out_sem) = refs
    width = projected.shape[1]
    dim_in, rows = codebook.shape
    hidden_size = hidden.shape[0]
    length = flat.shape[2] - EXTRA
    pairs = list(zip(
        (incoming_hbm, projected_hbm, weight_hbm, slope_hbm, hidden_hbm, codebook_hbm),
        (incoming, projected, weight, slope, hidden, codebook),
    ))
    loads = [pltpu.make_async_copy(a, b, in_sem.at[k]) for k, (a, b) in enumerate(pairs)]
    loads[0].start()
    loads[0].wait()
    for load in loads[1:]:
        load.start()

    blocks = width // LANES
    for s in range(devices):
        own = pl.ds(s * capacity, capacity)
        for j in range(blocks):
            value = incoming[s, j * capacity : (j + 1) * capacity, :]
            high = value.astype(jnp.bfloat16)
            parts[own, j * LANES : (j + 1) * LANES] = high
            parts[own, width + j * LANES : width + (j + 1) * LANES] = (
                value - high.astype(jnp.float32)
            ).astype(jnp.bfloat16)
    per_row = LANES // capacity
    for t in range(devices * capacity // LANES):
        row = None
        for k in range(per_row):
            one = incoming[t * per_row + k, blocks * capacity :, :]
            if k:
                one = pltpu.roll(one, k * capacity, 1)
            row = one if row is None else jnp.maximum(row, one)
        wanted[:, t * LANES : (t + 1) * LANES] = row.astype(jnp.int32)

    loads[1].wait()
    loads[2].wait()
    loads[3].wait()
    tile = min(256, rows)
    bias_in = jnp.zeros((1, hidden_size), jnp.float32)
    bias_out = jnp.zeros((1, width), jnp.float32)
    for start in range(0, rows, tile):
        part = pl.ds(start, tile)
        ids = lax.broadcasted_iota(jnp.int32, (tile, wanted.shape[1]), 0) + start
        chooser = (ids == wanted[0:1, :]).astype(jnp.float32)
        times = jnp.sum(chooser, axis=1, keepdims=True)
        both = dot(chooser.astype(jnp.bfloat16), parts[...])
        code_grad = both[:, :width] + both[:, width:] + times * projected[part, :]
        bias_out += jnp.sum(code_grad, axis=0, keepdims=True)
        code_low = code_grad.astype(jnp.bfloat16)
        low[part, :] = code_low
        preact_grad = (dot(code_low, weight[...]) * slope[part, :]).astype(jnp.bfloat16)
        grad[part, :] = preact_grad
        bias_in += jnp.sum(preact_grad.astype(jnp.float32), axis=0, keepdims=True)


    first = lax.axis_index("outer")
    plane = lax.axis_index("inner") * chip + lax.axis_index("chip")
    me = lax.axis_index("core")
    band = hidden_size // outer
    pieces = inner * chip
    home = lax.rem(outer - first, outer)
    for k in range(outer):
        for e in range(pieces * core):
            flat[k, e, length:, :] = jnp.zeros((EXTRA, LANES), jnp.float32)
    biases = [bias_in[:, k : k + LANES] for k in range(0, hidden_size, LANES)]
    biases += [bias_out[:, k : k + LANES] for k in range(0, width, LANES)]
    for j, bias in enumerate(biases):
        flat[home, j // EXTRA, length + j % EXTRA : length + j % EXTRA + 1, :] = bias

    loads[4].wait()
    loads[5].wait()
    stores = []
    for k in range(outer - 1, -1, -1):
        o = lax.rem(first + k, outer)
        here = pl.ds(pl.multiple_of(o * band, band), band)

        def keep(row, value):
            for r in range(0, value.shape[0], length):
                flat[k, (row + r) // length, :length, :] = value[r : r + length, :]

        out = dot(codebook[...], grad[:, here])
        for j in range(band // LANES):
            keep(j * dim_in, out[:, j * LANES : (j + 1) * LANES])
        out = dot(hidden[here, :], low[...])
        for j in range(blocks):
            keep(band // LANES * dim_in + j * band, out[:, j * LANES : (j + 1) * LANES])
        for target, c in ((theirs_hbm, 1 - me), (mine_hbm, me)):
            for j in range(pieces):
                e = lax.bitwise_xor(plane, place(sizes, k, j)) * core + c
                copy = pltpu.make_async_copy(
                    flat.at[k, e], target[k].at[j], out_sem.at[len(stores)]
                )
                copy.start()
                stores.append(copy)
    for copy in stores:
        copy.wait()


def backward(sizes, capacity, incoming, hidden_t, slope, projected, codebook_t, weight_t):
    devices = incoming.shape[0]
    rows, width = projected.shape
    dim_in, hidden_size = codebook_t.shape[0], hidden_t.shape[0]
    length = (dim_in + width) * hidden_size // LANES // devices
    outer, inner, chip, _ = sizes
    piece = jax.ShapeDtypeStruct((inner * chip, length + EXTRA, LANES), jnp.float32)
    operands = (incoming, hidden_t, slope, projected, codebook_t, weight_t)
    vmem = lambda shape, dtype: pltpu.VMEM(shape, dtype)
    slots = devices * capacity
    return pl.pallas_call(
        functools.partial(backward_kernel, sizes, capacity),
        in_specs=[pl.BlockSpec(memory_space=pl.ANY)] * 6,
        out_specs=[pl.BlockSpec(memory_space=pl.ANY)] * (2 * outer),
        out_shape=[piece] * (2 * outer),
        scratch_shapes=[vmem(a.shape, a.dtype) for a in operands]
        + [
            vmem((slots, 2 * width), jnp.bfloat16),
            vmem((EXTRA, slots), jnp.int32),
            vmem((rows, width), jnp.bfloat16),
            vmem((rows, hidden_size), jnp.bfloat16),
            vmem((outer, inner * chip * 2, length + EXTRA, LANES), jnp.float32),
            pltpu.SemaphoreType.DMA((6,)),
            pltpu.SemaphoreType.DMA((devices,)),
        ],
        compiler_params=pltpu.CompilerParams(vmem_limit_bytes=56 * 2**20),
        name="backward",
    )(*operands)


def assemble_kernel(sizes, *refs):
    outer, inner, chip, core = sizes
    devices = outer * inner * chip * core
    pieces, (weight_in, weight_out, biases, sems, bias_sem) = refs[:devices], refs[devices:]
    length = pieces[0].shape[0] - EXTRA
    dim_in, hidden_size = weight_in.shape
    band = hidden_size // outer
    base = band // LANES * dim_in
    first = lax.axis_index("outer")
    plane = lax.axis_index("inner") * chip + lax.axis_index("chip")
    me = lax.axis_index("core")
    copies = []
    for n, piece in enumerate(pieces):
        c, n = divmod(n, devices // core)
        k, j = divmod(n, inner * chip)
        n += c * (devices // core)
        o = lax.rem(first + outer - k, outer)
        e = lax.bitwise_xor(plane, place(sizes, k, j)) * core + lax.bitwise_xor(me, c)
        at = e * length
        source = piece.at[pl.ds(0, length)]

        def copy_to(target, row, column):
            rows = pl.ds(pl.multiple_of(row, length), length)
            lanes = pl.ds(pl.multiple_of(column * LANES, LANES), LANES)
            return pltpu.make_async_copy(source, target.at[rows, lanes], sems.at[n])

        @pl.when(at < base)
        def _():
            column = o * (band // LANES) + lax.div(at, dim_in)
            copy_to(weight_in, lax.rem(at, dim_in), column).start()

        @pl.when(at >= base)
        def _():
            copy_to(weight_out, o * band + lax.rem(at - base, band), lax.div(at - base, band)).start()

        @pl.when((o == 0) & (e < 2))
        def _():
            copy = pltpu.make_async_copy(
                piece.at[pl.ds(length, EXTRA)], biases.at[jnp.minimum(e, 1)], bias_sem
            )
            copy.start()
            copy.wait()

        copies.append(copy_to(weight_in, 0, 0))
    for copy in copies:
        copy.wait()


def assemble(sizes, pieces, dim_in, hidden_size, width):
    hbm = pl.BlockSpec(memory_space=pl.ANY)
    return pl.pallas_call(
        functools.partial(assemble_kernel, sizes),
        in_specs=[hbm] * len(pieces),
        out_specs=[hbm] * 3,
        out_shape=[
            jax.ShapeDtypeStruct((dim_in, hidden_size), jnp.float32),
            jax.ShapeDtypeStruct((hidden_size, width), jnp.float32),
            jax.ShapeDtypeStruct((2, EXTRA, LANES), jnp.float32),
        ],
        scratch_shapes=[
            pltpu.SemaphoreType.DMA((len(pieces),)),
            pltpu.SemaphoreType.DMA,
        ],
        compiler_params=pltpu.CompilerParams(vmem_limit_bytes=4 * 2**20),
        name="assemble",
    )(*pieces)


def along(sizes, x, k):
    outer = sizes[0]
    return lax.ppermute(x, "outer", [(o, (o + k) % outer) for o in range(outer)])


def across(sizes, axis, x, j):
    size = sizes[AXES.index(axis)]
    return lax.ppermute(x, axis, [(p, p ^ j) for p in range(size)])


def sum_chunks(sizes, mine, theirs):
    outer, inner, chip, _ = sizes
    total = None
    for k in range(outer - 1, -1, -1):
        slow, fast = ("inner", "chip") if k % 2 else ("chip", "inner")
        low = sizes[AXES.index(fast)]
        arrived = across(sizes, "core", theirs[k], 1)
        part = mine[k][:low] + arrived[:low]
        for j in range(1, sizes[AXES.index(slow)]):
            here = slice(j * low, (j + 1) * low)
            part = part + across(sizes, slow, mine[k][here] + arrived[here], j)
        chunk = part[0]
        for j in range(1, low):
            chunk = chunk + across(sizes, fast, part[j], j)
        if k:
            chunk = along(sizes, chunk, k)
        total = chunk if total is None else total + chunk
    return total


def spread_chunks(sizes, total):
    outer, inner, chip, _ = sizes
    near = []
    for k in range(outer):
        slow, fast = ("inner", "chip") if k % 2 else ("chip", "inner")
        x = along(sizes, total, k) if k else total
        row = [across(sizes, fast, x, j) if j else x for j in range(sizes[AXES.index(fast)])]
        for j in range(sizes[AXES.index(slow)]):
            near += [across(sizes, slow, x, j) if j else x for x in row]
    return near


def per_device(
    sizes, codebook, weight_in, bias_in, weight_out, bias_out, latents, cotangent, code_owner, code_row
):
    outer, inner, chip, core = sizes
    devices = outer * inner * chip * core
    rows, dim_in = codebook.shape
    hidden_size = weight_in.shape[1]
    count, width = latents.shape
    capacity = max(2, 2 * count // devices)

    outgoing, slots = route(devices, capacity, code_owner, code_row, latents, cotangent)
    outgoing, bias_in = lax.optimization_barrier((outgoing, bias_in))
    incoming = lax.all_to_all(outgoing, AXES, split_axis=0, concat_axis=0, tiled=True)

    preact = dot(codebook, weight_in) + bias_in
    hidden, slope = gelu_parts(preact)
    hidden = hidden.astype(jnp.bfloat16)
    projected = dot(hidden, weight_out) + bias_out

    wanted = incoming[:, -EXTRA, :capacity].reshape(-1)
    asked = wanted[:, None] == jnp.arange(rows, dtype=jnp.float32)[None, :]
    picked = pick(asked.astype(jnp.bfloat16), projected)
    incoming, picked = lax.optimization_barrier((incoming, picked))
    answers = lax.all_to_all(
        picked.reshape(devices, capacity, width), AXES, split_axis=0, concat_axis=0, tiled=True
    ).reshape(-1, width)

    pieces = backward(
        sizes, capacity, incoming, hidden.T, slope, projected, codebook.T, weight_out.T
    )
    total = sum_chunks(sizes, list(pieces[:outer]), list(pieces[outer:]))
    near = spread_chunks(sizes, total)

    slot_ids = jnp.arange(devices * capacity, dtype=jnp.int32)
    from_slot = slots.reshape(-1, 1) == slot_ids[None, :]
    chosen = pick(from_slot.astype(jnp.bfloat16), answers)
    latent_grad = cotangent - 0.25 * (chosen - latents)
    late = len(near) - inner * chip
    near[late], latent_grad = lax.optimization_barrier((near[late], latent_grad))

    chunks = near + [across(sizes, "core", x, 1) for x in near]
    gw_in, gw_out, biases = assemble(sizes, chunks, dim_in, hidden_size, width)
    biases = biases.reshape(-1)
    gb_in, gb_out = biases[:hidden_size], biases[hidden_size : hidden_size + width]
    return (latent_grad, gw_in, gb_in, gw_out, gb_out)


def solution(mesh):
    code, data = mesh.shape["code"], mesh.shape["dp"]
    core = 2
    outer = 1
    while outer * outer < code:
        outer *= 2
    sizes = (outer, code // outer, data // core, core)
    fine = Mesh(mesh.devices.reshape(sizes), AXES)
    rows = P(AXES, None)
    return jax.shard_map(
        functools.partial(per_device, sizes),
        mesh=fine,
        in_specs=(rows, P(), P(), P(), P(), rows, rows, rows, P(AXES)),
        out_specs=(rows, P(), P(), P(), P()),
        check_vma=False,
    )
```

```python
import functools

import jax
import jax.numpy as jnp
from jax import lax
from jax.experimental import pallas as pl
from jax.experimental.pallas import tpu as pltpu
from jax.sharding import Mesh, PartitionSpec as P

scale_gelu = 0.7978845608028654
cubic_term = 0.044715
LANES = 128
EXTRA = 8
AXES = ("outer", "inner", "chip", "core")


def gelu_parts(x):
    tangent = jnp.tanh(scale_gelu * (x + cubic_term * x * x * x))
    value = 0.5 * x * (1.0 + tangent)
    slope = 0.5 * (1.0 + tangent) + 0.5 * x * (1.0 - tangent * tangent) * scale_gelu * (
        1.0 + 3.0 * cubic_term * x * x
    )
    return value, slope


def split_two(x):
    high = lax.reduce_precision(x, 8, 7)
    low = (x - high).astype(jnp.bfloat16)
    return jnp.concatenate([high.astype(jnp.bfloat16), low], axis=1)


def pick(chooser, rows):
    width = rows.shape[1]
    both = jnp.dot(chooser, split_two(rows), preferred_element_type=jnp.float32)
    return both[:, :width] + both[:, width:]


def dot(a, b):
    return jnp.dot(a, b, preferred_element_type=jnp.float32)


def forward_kernel(codebook_ref, weight_in_ref, bias_in_ref, weight_out_ref, bias_out_ref,
                   hidden_ref, codebook_t_ref, slope_ref, projected_ref, parts_ref):
    width = projected_ref.shape[1]
    codebook = codebook_ref[...]
    codebook_t_ref[...] = jnp.transpose(codebook.astype(jnp.float32)).astype(jnp.bfloat16)
    hidden, slope = gelu_parts(dot(codebook, weight_in_ref[...]) + bias_in_ref[...])
    slope_ref[...] = slope
    hidden_ref[...] = jnp.transpose(hidden).astype(jnp.bfloat16)
    projected = dot(hidden.astype(jnp.bfloat16), weight_out_ref[...]) + bias_out_ref[...]
    projected_ref[...] = projected
    high = projected.astype(jnp.bfloat16)
    parts_ref[:, :width] = high
    parts_ref[:, width:] = (projected - high.astype(jnp.float32)).astype(jnp.bfloat16)


def forward(codebook, weight_in, bias_in, weight_out, bias_out):
    rows, dim_in = codebook.shape
    hidden_size, width = weight_out.shape
    tile = min(256, rows)
    whole = lambda *shape: pl.BlockSpec(shape, lambda i: (0, 0))
    return pl.pallas_call(
        forward_kernel,
        grid=(rows // tile,),
        in_specs=[
            pl.BlockSpec((tile, dim_in), lambda i: (i, 0)),
            whole(dim_in, hidden_size),
            whole(1, hidden_size),
            whole(hidden_size, width),
            whole(1, width),
        ],
        out_specs=[
            pl.BlockSpec((hidden_size, tile), lambda i: (0, i)),
            pl.BlockSpec((dim_in, tile), lambda i: (0, i)),
            pl.BlockSpec((tile, hidden_size), lambda i: (i, 0)),
            pl.BlockSpec((tile, width), lambda i: (i, 0)),
            pl.BlockSpec((tile, 2 * width), lambda i: (i, 0)),
        ],
        out_shape=[
            jax.ShapeDtypeStruct((hidden_size, rows), jnp.bfloat16),
            jax.ShapeDtypeStruct((dim_in, rows), jnp.bfloat16),
            jax.ShapeDtypeStruct((rows, hidden_size), jnp.float32),
            jax.ShapeDtypeStruct((rows, width), jnp.float32),
            jax.ShapeDtypeStruct((rows, 2 * width), jnp.bfloat16),
        ],
        cost_estimate=pl.CostEstimate(
            flops=2 * rows * hidden_size * (dim_in + width),
            bytes_accessed=14 * rows * hidden_size,
            transcendentals=rows * hidden_size,
        ),
        compiler_params=pltpu.CompilerParams(vmem_limit_bytes=60 * 2**20),
        name="forward",
    )(codebook, weight_in, bias_in.reshape(1, -1), weight_out, bias_out.reshape(1, -1))


def pick_kernel(capacity, incoming_hbm, parts_ref, out_ref, wanted_ref, asked_ref, sem):
    devices = asked_ref.shape[0]
    rows, both = parts_ref.shape
    width = both // 2
    step = pl.program_id(0)
    per_row = LANES // capacity

    @pl.when(step == 0)
    def _():
        payload = incoming_hbm.shape[1] - EXTRA
        load = pltpu.make_async_copy(
            incoming_hbm.at[pl.ds(0, devices), pl.ds(payload, EXTRA)], asked_ref, sem
        )
        load.start()
        load.wait()
        for t in range(devices // per_row):
            row = asked_ref[t * per_row]
            for k in range(1, per_row):
                row = jnp.maximum(row, pltpu.roll(asked_ref[t * per_row + k], k * capacity, 1))
            wanted_ref[:, t * LANES : (t + 1) * LANES] = row

    tile = out_ref.shape[0] * capacity
    lane = lax.broadcasted_iota(jnp.int32, (LANES, LANES), 1).astype(jnp.float32)
    for start in range(0, tile, LANES):
        at = pl.ds(pl.multiple_of(step * tile + start, LANES), LANES)
        column = jnp.transpose(jnp.broadcast_to(wanted_ref[0:1, at], (LANES, LANES)))
        chooser = jnp.concatenate(
            [
                (column == lane + float(r)).astype(jnp.float32).astype(jnp.bfloat16)
                for r in range(0, rows, LANES)
            ],
            axis=1,
        )
        value = dot(chooser, parts_ref[...])
        value = value[:, :width] + value[:, width:]
        for k in range(per_row):
            out_ref[start // capacity + k] = value[k * capacity : (k + 1) * capacity]


def pick_rows(capacity, incoming, parts):
    devices = incoming.shape[0]
    rows, both = parts.shape
    steps = 4
    return pl.pallas_call(
        functools.partial(pick_kernel, capacity),
        grid=(steps,),
        in_specs=[
            pl.BlockSpec(memory_space=pl.ANY),
            pl.BlockSpec((rows, both), lambda i: (0, 0)),
        ],
        out_specs=[
            pl.BlockSpec((devices // steps, capacity, both // 2), lambda i: (i, 0, 0)),
            pl.BlockSpec((EXTRA, devices * capacity), lambda i: (0, 0)),
        ],
        out_shape=[
            jax.ShapeDtypeStruct((devices, capacity, both // 2), jnp.float32),
            jax.ShapeDtypeStruct((EXTRA, devices * capacity), jnp.float32),
        ],
        scratch_shapes=[
            pltpu.VMEM((devices, EXTRA, LANES), jnp.float32),
            pltpu.SemaphoreType.DMA,
        ],
        cost_estimate=pl.CostEstimate(
            flops=2 * devices * capacity * rows * both,
            bytes_accessed=4 * devices * capacity * both,
            transcendentals=0,
        ),
        compiler_params=pltpu.CompilerParams(vmem_limit_bytes=60 * 2**20),
        name="pick_rows",
    )(incoming, parts)


def route_kernel(devices, capacity, owner_hbm, row_hbm, latents_hbm, cotangent_hbm,
                 out_ref, slot_ref, owner_ref, row_ref, latents_ref, cotangent_ref, parts_ref, sems):
    count, width = latents_ref.shape
    step = pl.program_id(0)
    tile = out_ref.shape[0] * capacity

    @pl.when(step == 0)
    def _():
        loads = [
            pltpu.make_async_copy(a, b, sems.at[k])
            for k, (a, b) in enumerate((
                (owner_hbm, owner_ref), (row_hbm, row_ref),
                (latents_hbm, latents_ref), (cotangent_hbm, cotangent_ref),
            ))
        ]
        for load in loads:
            load.start()
        before = (
            lax.broadcasted_iota(jnp.int32, (LANES, LANES), 0)
            < lax.broadcasted_iota(jnp.int32, (LANES, LANES), 1)
        ).astype(jnp.bfloat16)
        owner_ids = lax.broadcasted_iota(jnp.int32, (devices, LANES), 0)
        lane = lax.broadcasted_iota(jnp.int32, (LANES, LANES), 1)
        seen = jnp.zeros((devices, 1), jnp.float32)
        loads[0].wait()
        loads[1].wait()
        for start in range(0, count, LANES):
            part = pl.ds(start, LANES)
            owners = owner_ref[:, part]
            mine = (owner_ids == owners).astype(jnp.float32)
            ranks = dot(mine.astype(jnp.bfloat16), before) + seen
            rank = jnp.sum(mine * ranks, axis=0, keepdims=True)
            seen = seen + jnp.sum(mine, axis=1, keepdims=True)
            slot_ref[:, part] = owners * capacity + rank.astype(jnp.int32)
            rows = jnp.transpose(
                jnp.broadcast_to(row_ref[:, part].astype(jnp.float32), (LANES, LANES))
            )
            tall = jnp.floor(rows * (1.0 / 32.0))
            extra = jnp.where(lane == 0, tall, jnp.where(lane == 1, rows - 32.0 * tall, 0.0))
            extra = jnp.where(lane == 2, 1.0, extra)
            parts_ref[part, 2 * width :] = extra.astype(jnp.bfloat16)
        loads[2].wait()
        loads[3].wait()
        for start in range(0, count, LANES):
            part = pl.ds(start, LANES)
            value = cotangent_ref[part, :] - latents_ref[part, :]
            high = value.astype(jnp.bfloat16)
            parts_ref[part, :width] = high
            parts_ref[part, width : 2 * width] = (value - high.astype(jnp.float32)).astype(
                jnp.bfloat16
            )

    ids = lax.broadcasted_iota(jnp.int32, (tile, count), 0) + step * tile
    chooser = (ids == slot_ref[...]).astype(jnp.float32).astype(jnp.bfloat16)
    both = dot(chooser, parts_ref[...])
    value = both[:, :width] + both[:, width : 2 * width]
    turned = jnp.transpose(both[:, 2 * width :])
    wanted = 32.0 * turned[0:1] + turned[1:2] + turned[2:3] - 1.0
    lane = lax.broadcasted_iota(jnp.int32, (EXTRA, LANES), 1)
    for k in range(out_ref.shape[0]):
        own = slice(k * capacity, (k + 1) * capacity)
        for j in range(width // LANES):
            out_ref[k, j * capacity : (j + 1) * capacity, :] = value[own, j * LANES : (j + 1) * LANES]
        at = k * capacity // LANES * LANES
        row = jnp.broadcast_to(wanted[:, at : at + LANES], (EXTRA, LANES))
        shift = k * capacity - at
        if shift:
            row = pltpu.roll(row, LANES - shift, 1)
        out_ref[k, width // LANES * capacity :, :] = jnp.where(lane < capacity, row, -1.0)


def route(devices, capacity, code_owner, code_row, latents, cotangent):
    count, width = latents.shape
    per_step = max(1, 256 // capacity)
    block = width // LANES * capacity + EXTRA
    whole = lambda *shape: pl.BlockSpec(shape, lambda i: (0,) * len(shape))
    return pl.pallas_call(
        functools.partial(route_kernel, devices, capacity),
        grid=(devices // per_step,),
        in_specs=[pl.BlockSpec(memory_space=pl.ANY)] * 4,
        out_specs=[
            pl.BlockSpec((per_step, block, LANES), lambda i: (i, 0, 0)),
            whole(1, count),
        ],
        out_shape=[
            jax.ShapeDtypeStruct((devices, block, LANES), jnp.float32),
            jax.ShapeDtypeStruct((1, count), jnp.int32),
        ],
        scratch_shapes=[
            pltpu.VMEM((1, count), jnp.int32),
            pltpu.VMEM((1, count), jnp.int32),
            pltpu.VMEM((count, width), jnp.float32),
            pltpu.VMEM((count, width), jnp.float32),
            pltpu.VMEM((count, 2 * width + LANES), jnp.bfloat16),
            pltpu.SemaphoreType.DMA((4,)),
        ],
        compiler_params=pltpu.CompilerParams(vmem_limit_bytes=60 * 2**20),
        name="route",
    )(code_owner.reshape(1, count), code_row.reshape(1, count), latents, cotangent)


def place(sizes, k, j):
    _, inner, chip, _ = sizes
    if k % 2:
        return j
    return j % inner * chip + j // inner


def backward_kernel(sizes, capacity, incoming_hbm, wanted_hbm, hidden_hbm, slope_hbm, projected_hbm,
                    codebook_hbm, weight_hbm, *refs):
    outer, inner, chip, core = sizes
    devices = outer * inner * chip * core
    mine_hbm, theirs_hbm, refs = refs[:outer], refs[outer : 2 * outer], refs[2 * outer :]
    (incoming, wanted, hidden, slope, projected, codebook, weight, parts, low, grad, flat,
     in_sem, out_sem) = refs
    width = projected.shape[1]
    dim_in, rows = codebook.shape
    hidden_size = hidden.shape[0]
    length = flat.shape[2] - EXTRA
    pairs = list(zip(
        (wanted_hbm, projected_hbm, weight_hbm, slope_hbm, hidden_hbm, codebook_hbm),
        (wanted, projected, weight, slope, hidden, codebook),
    ))
    loads = [pltpu.make_async_copy(a, b, in_sem.at[k]) for k, (a, b) in enumerate(pairs)]
    loads[0].start()
    blocks = width // LANES
    quarter = devices // 4
    arrivals = []
    for n in range(4):
        part = pl.ds(n * quarter, quarter)
        arrivals.append(pltpu.make_async_copy(
            incoming_hbm.at[part, pl.ds(0, blocks * capacity)], incoming.at[part], in_sem.at[6 + n]
        ))
        arrivals[n].start()
    for load in loads[1:]:
        load.start()
    for n in range(4):
        arrivals[n].wait()
        for s in range(n * quarter, (n + 1) * quarter):
            own = pl.ds(s * capacity, capacity)
            for j in range(blocks):
                value = incoming[s, j * capacity : (j + 1) * capacity, :]
                high = value.astype(jnp.bfloat16)
                parts[own, j * LANES : (j + 1) * LANES] = high
                parts[own, width + j * LANES : width + (j + 1) * LANES] = (
                    value - high.astype(jnp.float32)
                ).astype(jnp.bfloat16)
    for load in loads[:4]:
        load.wait()
    tile = min(256, rows)
    bias_in = jnp.zeros((1, hidden_size), jnp.float32)
    bias_out = jnp.zeros((1, width), jnp.float32)
    for start in range(0, rows, tile):
        part = pl.ds(start, tile)
        ids = (lax.broadcasted_iota(jnp.int32, (tile, wanted.shape[1]), 0) + start).astype(
            jnp.float32
        )
        chooser = (ids == wanted[0:1, :]).astype(jnp.float32)
        times = jnp.sum(chooser, axis=1, keepdims=True)
        both = dot(chooser.astype(jnp.bfloat16), parts[...])
        code_grad = both[:, :width] + both[:, width:] + times * projected[part, :]
        bias_out += jnp.sum(code_grad, axis=0, keepdims=True)
        code_low = code_grad.astype(jnp.bfloat16)
        low[part, :] = code_low
        preact_grad = (dot(code_low, weight[...]) * slope[part, :]).astype(jnp.bfloat16)
        grad[part, :] = preact_grad
        bias_in += jnp.sum(preact_grad.astype(jnp.float32), axis=0, keepdims=True)


    first = lax.axis_index("outer")
    plane = lax.axis_index("inner") * chip + lax.axis_index("chip")
    me = lax.axis_index("core")
    band = hidden_size // outer
    pieces = inner * chip
    home = lax.rem(outer - first, outer)
    for k in range(outer):
        for e in range(pieces * core):
            flat[k, e, length:, :] = jnp.zeros((EXTRA, LANES), jnp.float32)
    biases = [bias_in[:, k : k + LANES] for k in range(0, hidden_size, LANES)]
    biases += [bias_out[:, k : k + LANES] for k in range(0, width, LANES)]
    for j, bias in enumerate(biases):
        flat[home, j // EXTRA, length + j % EXTRA : length + j % EXTRA + 1, :] = bias

    loads[4].wait()
    loads[5].wait()
    stores = []
    for k in range(outer - 1, -1, -1):
        o = lax.rem(first + k, outer)
        here = pl.ds(pl.multiple_of(o * band, band), band)

        def keep(row, value):
            for r in range(0, value.shape[0], length):
                flat[k, (row + r) // length, :length, :] = value[r : r + length, :]

        out = dot(codebook[...], grad[:, here])
        for j in range(band // LANES):
            keep(j * dim_in, out[:, j * LANES : (j + 1) * LANES])
        out = dot(hidden[here, :], low[...])
        for j in range(blocks):
            keep(band // LANES * dim_in + j * band, out[:, j * LANES : (j + 1) * LANES])
        for target, c in ((theirs_hbm, 1 - me), (mine_hbm, me)):
            for j in range(pieces):
                e = lax.bitwise_xor(plane, place(sizes, k, j)) * core + c
                copy = pltpu.make_async_copy(
                    flat.at[k, e], target[k].at[j], out_sem.at[len(stores)]
                )
                copy.start()
                stores.append(copy)
    for copy in stores:
        copy.wait()


def backward(sizes, capacity, incoming, wanted, hidden_t, slope, projected, codebook_t, weight_t):
    devices = incoming.shape[0]
    rows, width = projected.shape
    dim_in, hidden_size = codebook_t.shape[0], hidden_t.shape[0]
    length = (dim_in + width) * hidden_size // LANES // devices
    outer, inner, chip, core = sizes
    piece = jax.ShapeDtypeStruct((inner * chip, length + EXTRA, LANES), jnp.float32)
    operands = (incoming, wanted, hidden_t, slope, projected, codebook_t, weight_t)
    vmem = lambda shape, dtype: pltpu.VMEM(shape, dtype)
    slots = devices * capacity
    return pl.pallas_call(
        functools.partial(backward_kernel, sizes, capacity),
        in_specs=[pl.BlockSpec(memory_space=pl.ANY)] * len(operands),
        out_specs=[pl.BlockSpec(memory_space=pl.ANY)] * (2 * outer),
        out_shape=[piece] * (2 * outer),
        scratch_shapes=[vmem((devices, incoming.shape[1] - EXTRA, LANES), jnp.float32)]
        + [vmem(a.shape, a.dtype) for a in operands[1:]]
        + [
            vmem((slots, 2 * width), jnp.bfloat16),
            vmem((rows, width), jnp.bfloat16),
            vmem((rows, hidden_size), jnp.bfloat16),
            vmem((outer, inner * chip * core, length + EXTRA, LANES), jnp.float32),
            pltpu.SemaphoreType.DMA((10,)),
            pltpu.SemaphoreType.DMA((devices,)),
        ],
        cost_estimate=pl.CostEstimate(
            flops=2 * rows * (slots * 2 * width + hidden_size * (2 * width + dim_in)),
            bytes_accessed=16 * rows * hidden_size,
            transcendentals=0,
        ),
        compiler_params=pltpu.CompilerParams(vmem_limit_bytes=60 * 2**20),
        name="backward",
    )(*operands)


def assemble_kernel(sizes, *refs):
    outer, inner, chip, core = sizes
    devices = outer * inner * chip * core
    pieces, (weight_in, weight_out, biases, sems, bias_sem) = refs[:devices], refs[devices:]
    length = pieces[0].shape[0] - EXTRA
    dim_in, hidden_size = weight_in.shape
    band = hidden_size // outer
    base = band // LANES * dim_in
    first = lax.axis_index("outer")
    plane = lax.axis_index("inner") * chip + lax.axis_index("chip")
    me = lax.axis_index("core")
    copies = []
    for n, piece in enumerate(pieces):
        c, n = divmod(n, devices // core)
        k, j = divmod(n, inner * chip)
        n += c * (devices // core)
        o = lax.rem(first + outer - k, outer)
        e = lax.bitwise_xor(plane, place(sizes, k, j)) * core + lax.bitwise_xor(me, c)
        at = e * length
        source = piece.at[pl.ds(0, length)]

        def copy_to(target, row, column):
            rows = pl.ds(pl.multiple_of(row, length), length)
            lanes = pl.ds(pl.multiple_of(column * LANES, LANES), LANES)
            return pltpu.make_async_copy(source, target.at[rows, lanes], sems.at[n])

        @pl.when(at < base)
        def _():
            column = o * (band // LANES) + lax.div(at, dim_in)
            copy_to(weight_in, lax.rem(at, dim_in), column).start()

        @pl.when(at >= base)
        def _():
            copy_to(weight_out, o * band + lax.rem(at - base, band), lax.div(at - base, band)).start()

        @pl.when((o == 0) & (e < 2))
        def _():
            copy = pltpu.make_async_copy(
                piece.at[pl.ds(length, EXTRA)], biases.at[jnp.minimum(e, 1)], bias_sem
            )
            copy.start()
            copy.wait()

        copies.append(copy_to(weight_in, 0, 0))
    for copy in copies:
        copy.wait()


def assemble(sizes, pieces, dim_in, hidden_size, width):
    hbm = pl.BlockSpec(memory_space=pl.ANY)
    return pl.pallas_call(
        functools.partial(assemble_kernel, sizes),
        in_specs=[hbm] * len(pieces),
        out_specs=[hbm] * 3,
        out_shape=[
            jax.ShapeDtypeStruct((dim_in, hidden_size), jnp.float32),
            jax.ShapeDtypeStruct((hidden_size, width), jnp.float32),
            jax.ShapeDtypeStruct((2, EXTRA, LANES), jnp.float32),
        ],
        scratch_shapes=[
            pltpu.SemaphoreType.DMA((len(pieces),)),
            pltpu.SemaphoreType.DMA,
        ],
        compiler_params=pltpu.CompilerParams(vmem_limit_bytes=4 * 2**20),
        name="assemble",
    )(*pieces)


def along(sizes, x, k):
    outer = sizes[0]
    return lax.ppermute(x, "outer", [(o, (o + k) % outer) for o in range(outer)])


def across(sizes, axis, x, j):
    size = sizes[AXES.index(axis)]
    return lax.ppermute(x, axis, [(p, p ^ j) for p in range(size)])


def sum_chunks(sizes, mine, theirs):
    outer, inner, chip, _ = sizes
    total = None
    for k in range(outer - 1, -1, -1):
        slow, fast = ("inner", "chip") if k % 2 else ("chip", "inner")
        low = sizes[AXES.index(fast)]
        arrived = across(sizes, "core", theirs[k], 1)
        part = mine[k][:low] + arrived[:low]
        for j in range(1, sizes[AXES.index(slow)]):
            here = slice(j * low, (j + 1) * low)
            part = part + across(sizes, slow, mine[k][here] + arrived[here], j)
        chunk = part[0]
        for j in range(1, low):
            chunk = chunk + across(sizes, fast, part[j], j)
        if k:
            chunk = along(sizes, chunk, k)
        total = chunk if total is None else total + chunk
    return total


def spread_chunks(sizes, total):
    outer, inner, chip, _ = sizes
    near = []
    for k in range(outer):
        slow, fast = ("inner", "chip") if k % 2 else ("chip", "inner")
        x = along(sizes, total, k) if k else total
        row = [across(sizes, fast, x, j) if j else x for j in range(sizes[AXES.index(fast)])]
        for j in range(sizes[AXES.index(slow)]):
            near += [across(sizes, slow, x, j) if j else x for x in row]
    return near


def per_device(
    sizes, codebook, weight_in, bias_in, weight_out, bias_out, latents, cotangent, code_owner, code_row
):
    outer, inner, chip, core = sizes
    devices = outer * inner * chip * core
    rows, dim_in = codebook.shape
    hidden_size = weight_in.shape[1]
    count, width = latents.shape
    capacity = max(2, 2 * count // devices)

    outgoing, slots = route(devices, capacity, code_owner, code_row, latents, cotangent)
    outgoing, bias_in = lax.optimization_barrier((outgoing, bias_in))
    incoming = lax.all_to_all(outgoing, AXES, split_axis=0, concat_axis=0, tiled=True)

    hidden_t, codebook_t, slope, projected, parts = forward(
        codebook, weight_in, bias_in, weight_out, bias_out
    )
    picked, wanted = pick_rows(capacity, incoming, parts)
    answers = lax.all_to_all(picked, AXES, split_axis=0, concat_axis=0, tiled=True)

    pieces = backward(
        sizes, capacity, incoming, wanted, hidden_t, slope, projected, codebook_t, weight_out.T
    )
    total = sum_chunks(sizes, list(pieces[:outer]), list(pieces[outer:]))
    total, answers = lax.optimization_barrier((total, answers))
    answers = answers.reshape(-1, width)
    near = spread_chunks(sizes, total)

    slot_ids = jnp.arange(devices * capacity, dtype=jnp.int32)
    from_slot = slots.reshape(-1, 1) == slot_ids[None, :]
    chosen = pick(from_slot.astype(jnp.bfloat16), answers)
    latent_grad = cotangent - 0.25 * (chosen - latents)
    late = len(near) - inner * chip
    near[late], latent_grad = lax.optimization_barrier((near[late], latent_grad))

    chunks = near + [across(sizes, "core", x, 1) for x in near]
    gw_in, gw_out, biases = assemble(sizes, chunks, dim_in, hidden_size, width)
    biases = biases.reshape(-1)
    gb_in, gb_out = biases[:hidden_size], biases[hidden_size : hidden_size + width]
    return (latent_grad, gw_in, gb_in, gw_out, gb_out)


def solution(mesh):
    code, data = mesh.shape["code"], mesh.shape["dp"]
    core = 2
    outer = 1
    while outer * outer < code:
        outer *= 2
    sizes = (outer, code // outer, data // core, core)
    fine = Mesh(mesh.devices.reshape(sizes), AXES)
    rows = P(AXES, None)
    return jax.shard_map(
        functools.partial(per_device, sizes),
        mesh=fine,
        in_specs=(rows, P(), P(), P(), P(), rows, rows, rows, P(AXES)),
        out_specs=(rows, P(), P(), P(), P()),
        check_vma=False,
    )
```

```python
import functools

import jax
import jax.numpy as jnp
from jax import lax
from jax.experimental import pallas as pl
from jax.experimental.pallas import tpu as pltpu
from jax.sharding import Mesh, PartitionSpec as P

scale_gelu = 0.7978845608028654
cubic_term = 0.044715
LANES = 128
EXTRA = 8
AXES = ("outer", "inner", "chip", "core")


def gelu_parts(x):
    tangent = jnp.tanh(scale_gelu * (x + cubic_term * x * x * x))
    value = 0.5 * x * (1.0 + tangent)
    slope = 0.5 * (1.0 + tangent) + 0.5 * x * (1.0 - tangent * tangent) * scale_gelu * (
        1.0 + 3.0 * cubic_term * x * x
    )
    return value, slope


def split_two(x):
    high = lax.reduce_precision(x, 8, 7)
    low = (x - high).astype(jnp.bfloat16)
    return jnp.concatenate([high.astype(jnp.bfloat16), low], axis=1)


def pick(chooser, rows):
    width = rows.shape[1]
    both = jnp.dot(chooser, split_two(rows), preferred_element_type=jnp.float32)
    return both[:, :width] + both[:, width:]


def dot(a, b):
    return jnp.dot(a, b, preferred_element_type=jnp.float32)


def forward_kernel(codebook_ref, weight_in_ref, bias_in_ref, weight_out_ref, bias_out_ref,
                   hidden_ref, codebook_t_ref, slope_ref, projected_ref, parts_ref):
    width = projected_ref.shape[1]
    codebook = codebook_ref[...]
    codebook_t_ref[...] = jnp.transpose(codebook.astype(jnp.float32)).astype(jnp.bfloat16)
    hidden, slope = gelu_parts(dot(codebook, weight_in_ref[...]) + bias_in_ref[...])
    slope_ref[...] = slope
    hidden_ref[...] = jnp.transpose(hidden).astype(jnp.bfloat16)
    projected = dot(hidden.astype(jnp.bfloat16), weight_out_ref[...]) + bias_out_ref[...]
    projected_ref[...] = projected
    high = projected.astype(jnp.bfloat16)
    parts_ref[:, :width] = high
    parts_ref[:, width:] = (projected - high.astype(jnp.float32)).astype(jnp.bfloat16)


def forward(codebook, weight_in, bias_in, weight_out, bias_out):
    rows, dim_in = codebook.shape
    hidden_size, width = weight_out.shape
    tile = min(256, rows)
    whole = lambda *shape: pl.BlockSpec(shape, lambda i: (0, 0))
    return pl.pallas_call(
        forward_kernel,
        grid=(rows // tile,),
        in_specs=[
            pl.BlockSpec((tile, dim_in), lambda i: (i, 0)),
            whole(dim_in, hidden_size),
            whole(1, hidden_size),
            whole(hidden_size, width),
            whole(1, width),
        ],
        out_specs=[
            pl.BlockSpec((hidden_size, tile), lambda i: (0, i)),
            pl.BlockSpec((dim_in, tile), lambda i: (0, i)),
            pl.BlockSpec((tile, hidden_size), lambda i: (i, 0)),
            pl.BlockSpec((tile, width), lambda i: (i, 0)),
            pl.BlockSpec((tile, 2 * width), lambda i: (i, 0)),
        ],
        out_shape=[
            jax.ShapeDtypeStruct((hidden_size, rows), jnp.bfloat16),
            jax.ShapeDtypeStruct((dim_in, rows), jnp.bfloat16),
            jax.ShapeDtypeStruct((rows, hidden_size), jnp.float32),
            jax.ShapeDtypeStruct((rows, width), jnp.float32),
            jax.ShapeDtypeStruct((rows, 2 * width), jnp.bfloat16),
        ],
        cost_estimate=pl.CostEstimate(
            flops=2 * rows * hidden_size * (dim_in + width),
            bytes_accessed=14 * rows * hidden_size,
            transcendentals=rows * hidden_size,
        ),
        compiler_params=pltpu.CompilerParams(vmem_limit_bytes=60 * 2**20),
        name="forward",
    )(codebook, weight_in, bias_in.reshape(1, -1), weight_out, bias_out.reshape(1, -1))


def pick_kernel(capacity, incoming_hbm, parts_hbm, out_ref, wanted_ref, asked_ref, parts_ref, sems):
    devices = asked_ref.shape[0]
    rows, both = parts_ref.shape
    width = both // 2
    step = pl.program_id(0)
    per_row = LANES // capacity

    @pl.when(step == 0)
    def _():
        payload = incoming_hbm.shape[1] - EXTRA
        load = pltpu.make_async_copy(
            incoming_hbm.at[pl.ds(0, devices), pl.ds(payload, EXTRA)], asked_ref, sems.at[0]
        )
        load.start()
        more = pltpu.make_async_copy(parts_hbm, parts_ref, sems.at[1])
        more.start()
        load.wait()
        for t in range(devices // per_row):
            row = asked_ref[t * per_row]
            for k in range(1, per_row):
                row = jnp.maximum(row, pltpu.roll(asked_ref[t * per_row + k], k * capacity, 1))
            wanted_ref[:, t * LANES : (t + 1) * LANES] = row
        more.wait()

    tile = out_ref.shape[0] * capacity
    lane = lax.broadcasted_iota(jnp.int32, (LANES, LANES), 1).astype(jnp.float32)
    choosers = []
    for start in range(0, tile, LANES):
        at = pl.ds(pl.multiple_of(step * tile + start, LANES), LANES)
        column = jnp.transpose(jnp.broadcast_to(wanted_ref[0:1, at], (LANES, LANES)))
        choosers.append(jnp.concatenate(
            [
                (column == lane + float(r)).astype(jnp.float32).astype(jnp.bfloat16)
                for r in range(0, rows, LANES)
            ],
            axis=1,
        ))
    value = dot(jnp.concatenate(choosers, axis=0), parts_ref[...])
    value = value[:, :width] + value[:, width:]
    for k in range(out_ref.shape[0]):
        out_ref[k] = value[k * capacity : (k + 1) * capacity]


def pick_rows(capacity, incoming, parts):
    devices = incoming.shape[0]
    rows, both = parts.shape
    steps = 4
    return pl.pallas_call(
        functools.partial(pick_kernel, capacity),
        grid=(steps,),
        in_specs=[pl.BlockSpec(memory_space=pl.ANY)] * 2,
        out_specs=[
            pl.BlockSpec((devices // steps, capacity, both // 2), lambda i: (i, 0, 0)),
            pl.BlockSpec((EXTRA, devices * capacity), lambda i: (0, 0)),
        ],
        out_shape=[
            jax.ShapeDtypeStruct((devices, capacity, both // 2), jnp.float32),
            jax.ShapeDtypeStruct((EXTRA, devices * capacity), jnp.float32),
        ],
        scratch_shapes=[
            pltpu.VMEM((devices, EXTRA, LANES), jnp.float32),
            pltpu.VMEM((rows, both), jnp.bfloat16),
            pltpu.SemaphoreType.DMA((2,)),
        ],
        cost_estimate=pl.CostEstimate(
            flops=2 * devices * capacity * rows * both,
            bytes_accessed=4 * devices * capacity * both,
            transcendentals=0,
        ),
        compiler_params=pltpu.CompilerParams(vmem_limit_bytes=60 * 2**20),
        name="pick_rows",
    )(incoming, parts)


def route_kernel(devices, capacity, owner_hbm, row_hbm, latents_hbm, cotangent_hbm,
                 out_ref, slot_ref, owner_ref, row_ref, latents_ref, cotangent_ref, parts_ref, sems):
    count, width = latents_ref.shape
    step = pl.program_id(0)
    tile = out_ref.shape[0] * capacity

    @pl.when(step == 0)
    def _():
        loads = [
            pltpu.make_async_copy(a, b, sems.at[k])
            for k, (a, b) in enumerate((
                (owner_hbm, owner_ref), (row_hbm, row_ref),
                (latents_hbm, latents_ref), (cotangent_hbm, cotangent_ref),
            ))
        ]
        for load in loads:
            load.start()
        before = (
            lax.broadcasted_iota(jnp.int32, (LANES, LANES), 0)
            < lax.broadcasted_iota(jnp.int32, (LANES, LANES), 1)
        ).astype(jnp.bfloat16)
        owner_ids = lax.broadcasted_iota(jnp.int32, (devices, LANES), 0)
        lane = lax.broadcasted_iota(jnp.int32, (LANES, LANES), 1)
        seen = jnp.zeros((devices, 1), jnp.float32)
        loads[0].wait()
        loads[1].wait()
        for start in range(0, count, LANES):
            part = pl.ds(start, LANES)
            owners = owner_ref[:, part]
            mine = (owner_ids == owners).astype(jnp.float32)
            ranks = dot(mine.astype(jnp.bfloat16), before) + seen
            rank = jnp.sum(mine * ranks, axis=0, keepdims=True)
            seen = seen + jnp.sum(mine, axis=1, keepdims=True)
            slot_ref[:, part] = owners * capacity + rank.astype(jnp.int32)
            rows = jnp.transpose(
                jnp.broadcast_to(row_ref[:, part].astype(jnp.float32), (LANES, LANES))
            )
            tall = jnp.floor(rows * (1.0 / 32.0))
            extra = jnp.where(lane == 0, tall, jnp.where(lane == 1, rows - 32.0 * tall, 0.0))
            extra = jnp.where(lane == 2, 1.0, extra)
            parts_ref[part, 2 * width :] = extra.astype(jnp.bfloat16)
        loads[2].wait()
        loads[3].wait()
        for start in range(0, count, LANES):
            part = pl.ds(start, LANES)
            value = cotangent_ref[part, :] - latents_ref[part, :]
            high = value.astype(jnp.bfloat16)
            parts_ref[part, :width] = high
            parts_ref[part, width : 2 * width] = (value - high.astype(jnp.float32)).astype(
                jnp.bfloat16
            )

    ids = lax.broadcasted_iota(jnp.int32, (tile, count), 0) + step * tile
    chooser = (ids == slot_ref[...]).astype(jnp.float32).astype(jnp.bfloat16)
    both = dot(chooser, parts_ref[...])
    value = both[:, :width] + both[:, width : 2 * width]
    turned = jnp.transpose(both[:, 2 * width :])
    wanted = 32.0 * turned[0:1] + turned[1:2] + turned[2:3] - 1.0
    lane = lax.broadcasted_iota(jnp.int32, (EXTRA, LANES), 1)
    for k in range(out_ref.shape[0]):
        own = slice(k * capacity, (k + 1) * capacity)
        for j in range(width // LANES):
            out_ref[k, j * capacity : (j + 1) * capacity, :] = value[own, j * LANES : (j + 1) * LANES]
        at = k * capacity // LANES * LANES
        row = jnp.broadcast_to(wanted[:, at : at + LANES], (EXTRA, LANES))
        shift = k * capacity - at
        if shift:
            row = pltpu.roll(row, LANES - shift, 1)
        out_ref[k, width // LANES * capacity :, :] = jnp.where(lane < capacity, row, -1.0)


def route(devices, capacity, code_owner, code_row, latents, cotangent):
    count, width = latents.shape
    per_step = max(1, 512 // capacity)
    block = width // LANES * capacity + EXTRA
    whole = lambda *shape: pl.BlockSpec(shape, lambda i: (0,) * len(shape))
    return pl.pallas_call(
        functools.partial(route_kernel, devices, capacity),
        grid=(devices // per_step,),
        in_specs=[pl.BlockSpec(memory_space=pl.ANY)] * 4,
        out_specs=[
            pl.BlockSpec((per_step, block, LANES), lambda i: (i, 0, 0)),
            whole(1, count),
        ],
        out_shape=[
            jax.ShapeDtypeStruct((devices, block, LANES), jnp.float32),
            jax.ShapeDtypeStruct((1, count), jnp.int32),
        ],
        scratch_shapes=[
            pltpu.VMEM((1, count), jnp.int32),
            pltpu.VMEM((1, count), jnp.int32),
            pltpu.VMEM((count, width), jnp.float32),
            pltpu.VMEM((count, width), jnp.float32),
            pltpu.VMEM((count, 2 * width + LANES), jnp.bfloat16),
            pltpu.SemaphoreType.DMA((4,)),
        ],
        compiler_params=pltpu.CompilerParams(vmem_limit_bytes=60 * 2**20),
        name="route",
    )(code_owner.reshape(1, count), code_row.reshape(1, count), latents, cotangent)


def place(sizes, k, j):
    _, inner, chip, _ = sizes
    if k % 2:
        return j
    return j % inner * chip + j // inner


def backward_kernel(sizes, capacity, incoming_hbm, wanted_hbm, hidden_hbm, slope_hbm, projected_hbm,
                    codebook_hbm, weight_hbm, *refs):
    outer, inner, chip, core = sizes
    devices = outer * inner * chip * core
    mine_hbm, theirs_hbm, refs = refs[:outer], refs[outer : 2 * outer], refs[2 * outer :]
    (incoming, wanted, hidden, slope, projected, codebook, weight, parts, low, grad, flat,
     in_sem, out_sem) = refs
    width = projected.shape[1]
    dim_in, rows = codebook.shape
    hidden_size = hidden.shape[0]
    length = flat.shape[2] - EXTRA
    pairs = list(zip(
        (wanted_hbm, projected_hbm, weight_hbm, slope_hbm, hidden_hbm, codebook_hbm),
        (wanted, projected, weight, slope, hidden, codebook),
    ))
    loads = [pltpu.make_async_copy(a, b, in_sem.at[k]) for k, (a, b) in enumerate(pairs)]
    loads[0].start()
    blocks = width // LANES
    quarter = devices // 4
    arrivals = []
    for n in range(4):
        part = pl.ds(n * quarter, quarter)
        arrivals.append(pltpu.make_async_copy(
            incoming_hbm.at[part, pl.ds(0, blocks * capacity)], incoming.at[part], in_sem.at[6 + n]
        ))
        arrivals[n].start()
    for load in loads[1:]:
        load.start()
    for n in range(4):
        arrivals[n].wait()
        for s in range(n * quarter, (n + 1) * quarter):
            own = pl.ds(s * capacity, capacity)
            for j in range(blocks):
                value = incoming[s, j * capacity : (j + 1) * capacity, :]
                high = value.astype(jnp.bfloat16)
                parts[own, j * LANES : (j + 1) * LANES] = high
                parts[own, width + j * LANES : width + (j + 1) * LANES] = (
                    value - high.astype(jnp.float32)
                ).astype(jnp.bfloat16)
    for load in loads[:4]:
        load.wait()
    tile = min(512, rows)
    bias_in = jnp.zeros((1, hidden_size), jnp.float32)
    bias_out = jnp.zeros((1, width), jnp.float32)
    for start in range(0, rows, tile):
        part = pl.ds(start, tile)
        ids = (lax.broadcasted_iota(jnp.int32, (tile, wanted.shape[1]), 0) + start).astype(
            jnp.float32
        )
        chooser = (ids == wanted[0:1, :]).astype(jnp.float32)
        times = jnp.sum(chooser, axis=1, keepdims=True)
        both = dot(chooser.astype(jnp.bfloat16), parts[...])
        code_grad = both[:, :width] + both[:, width:] + times * projected[part, :]
        bias_out += jnp.sum(code_grad, axis=0, keepdims=True)
        code_low = code_grad.astype(jnp.bfloat16)
        low[part, :] = code_low
        preact_grad = (dot(code_low, weight[...]) * slope[part, :]).astype(jnp.bfloat16)
        grad[part, :] = preact_grad
        bias_in += jnp.sum(preact_grad.astype(jnp.float32), axis=0, keepdims=True)


    first = lax.axis_index("outer")
    plane = lax.axis_index("inner") * chip + lax.axis_index("chip")
    me = lax.axis_index("core")
    band = hidden_size // outer
    pieces = inner * chip
    home = lax.rem(outer - first, outer)
    for k in range(outer):
        for e in range(pieces * core):
            flat[k, e, length:, :] = jnp.zeros((EXTRA, LANES), jnp.float32)
    biases = [bias_in[:, k : k + LANES] for k in range(0, hidden_size, LANES)]
    biases += [bias_out[:, k : k + LANES] for k in range(0, width, LANES)]
    for j, bias in enumerate(biases):
        flat[home, j // EXTRA, length + j % EXTRA : length + j % EXTRA + 1, :] = bias

    loads[4].wait()
    loads[5].wait()
    stores = []
    for k in range(outer - 1, -1, -1):
        o = lax.rem(first + k, outer)
        here = pl.ds(pl.multiple_of(o * band, band), band)

        def keep(row, value):
            for r in range(0, value.shape[0], length):
                flat[k, (row + r) // length, :length, :] = value[r : r + length, :]

        out = dot(codebook[...], grad[:, here])
        for j in range(band // LANES):
            keep(j * dim_in, out[:, j * LANES : (j + 1) * LANES])
        out = dot(hidden[here, :], low[...])
        for j in range(blocks):
            keep(band // LANES * dim_in + j * band, out[:, j * LANES : (j + 1) * LANES])
        for target, c in ((theirs_hbm, 1 - me), (mine_hbm, me)):
            for j in range(pieces):
                e = lax.bitwise_xor(plane, place(sizes, k, j)) * core + c
                copy = pltpu.make_async_copy(
                    flat.at[k, e], target[k].at[j], out_sem.at[len(stores)]
                )
                copy.start()
                stores.append(copy)
    for copy in stores:
        copy.wait()


def backward(sizes, capacity, incoming, wanted, hidden_t, slope, projected, codebook_t, weight_t):
    devices = incoming.shape[0]
    rows, width = projected.shape
    dim_in, hidden_size = codebook_t.shape[0], hidden_t.shape[0]
    length = (dim_in + width) * hidden_size // LANES // devices
    outer, inner, chip, core = sizes
    piece = jax.ShapeDtypeStruct((inner * chip, length + EXTRA, LANES), jnp.float32)
    operands = (incoming, wanted, hidden_t, slope, projected, codebook_t, weight_t)
    vmem = lambda shape, dtype: pltpu.VMEM(shape, dtype)
    slots = devices * capacity
    return pl.pallas_call(
        functools.partial(backward_kernel, sizes, capacity),
        in_specs=[pl.BlockSpec(memory_space=pl.ANY)] * len(operands),
        out_specs=[pl.BlockSpec(memory_space=pl.ANY)] * (2 * outer),
        out_shape=[piece] * (2 * outer),
        scratch_shapes=[vmem((devices, incoming.shape[1] - EXTRA, LANES), jnp.float32)]
        + [vmem(a.shape, a.dtype) for a in operands[1:]]
        + [
            vmem((slots, 2 * width), jnp.bfloat16),
            vmem((rows, width), jnp.bfloat16),
            vmem((rows, hidden_size), jnp.bfloat16),
            vmem((outer, inner * chip * core, length + EXTRA, LANES), jnp.float32),
            pltpu.SemaphoreType.DMA((10,)),
            pltpu.SemaphoreType.DMA((devices,)),
        ],
        cost_estimate=pl.CostEstimate(
            flops=2 * rows * (slots * 2 * width + hidden_size * (2 * width + dim_in)),
            bytes_accessed=16 * rows * hidden_size,
            transcendentals=0,
        ),
        compiler_params=pltpu.CompilerParams(vmem_limit_bytes=60 * 2**20),
        name="backward",
    )(*operands)


def assemble_kernel(sizes, *refs):
    outer, inner, chip, core = sizes
    devices = outer * inner * chip * core
    pieces, (weight_in, weight_out, biases, sems, bias_sem) = refs[:devices], refs[devices:]
    length = pieces[0].shape[0] - EXTRA
    dim_in, hidden_size = weight_in.shape
    band = hidden_size // outer
    base = band // LANES * dim_in
    first = lax.axis_index("outer")
    plane = lax.axis_index("inner") * chip + lax.axis_index("chip")
    me = lax.axis_index("core")
    copies = []
    for n, piece in enumerate(pieces):
        c, n = divmod(n, devices // core)
        k, j = divmod(n, inner * chip)
        n += c * (devices // core)
        o = lax.rem(first + outer - k, outer)
        e = lax.bitwise_xor(plane, place(sizes, k, j)) * core + lax.bitwise_xor(me, c)
        at = e * length
        source = piece.at[pl.ds(0, length)]

        def copy_to(target, row, column):
            rows = pl.ds(pl.multiple_of(row, length), length)
            lanes = pl.ds(pl.multiple_of(column * LANES, LANES), LANES)
            return pltpu.make_async_copy(source, target.at[rows, lanes], sems.at[n])

        @pl.when(at < base)
        def _():
            column = o * (band // LANES) + lax.div(at, dim_in)
            copy_to(weight_in, lax.rem(at, dim_in), column).start()

        @pl.when(at >= base)
        def _():
            copy_to(weight_out, o * band + lax.rem(at - base, band), lax.div(at - base, band)).start()

        @pl.when((o == 0) & (e < 2))
        def _():
            copy = pltpu.make_async_copy(
                piece.at[pl.ds(length, EXTRA)], biases.at[jnp.minimum(e, 1)], bias_sem
            )
            copy.start()
            copy.wait()

        copies.append(copy_to(weight_in, 0, 0))
    for copy in copies:
        copy.wait()


def assemble(sizes, pieces, dim_in, hidden_size, width):
    hbm = pl.BlockSpec(memory_space=pl.ANY)
    return pl.pallas_call(
        functools.partial(assemble_kernel, sizes),
        in_specs=[hbm] * len(pieces),
        out_specs=[hbm] * 3,
        out_shape=[
            jax.ShapeDtypeStruct((dim_in, hidden_size), jnp.float32),
            jax.ShapeDtypeStruct((hidden_size, width), jnp.float32),
            jax.ShapeDtypeStruct((2, EXTRA, LANES), jnp.float32),
        ],
        scratch_shapes=[
            pltpu.SemaphoreType.DMA((len(pieces),)),
            pltpu.SemaphoreType.DMA,
        ],
        compiler_params=pltpu.CompilerParams(vmem_limit_bytes=4 * 2**20),
        name="assemble",
    )(*pieces)


def along(sizes, x, k):
    outer = sizes[0]
    return lax.ppermute(x, "outer", [(o, (o + k) % outer) for o in range(outer)])


def across(sizes, axis, x, j):
    size = sizes[AXES.index(axis)]
    return lax.ppermute(x, axis, [(p, p ^ j) for p in range(size)])


def sum_chunks(sizes, mine, theirs, answers):
    outer, inner, chip, _ = sizes
    chunks = [None] * outer
    for k in range(outer - 1, -1, -1):
        slow, fast = ("inner", "chip") if k % 2 else ("chip", "inner")
        low = sizes[AXES.index(fast)]
        arrived = across(sizes, "core", theirs[k], 1)
        part = mine[k][:low] + arrived[:low]
        for j in range(1, sizes[AXES.index(slow)]):
            here = slice(j * low, (j + 1) * low)
            part = part + across(sizes, slow, mine[k][here] + arrived[here], j)
        chunks[k] = part[0]
        for j in range(1, low):
            chunks[k] = chunks[k] + across(sizes, fast, part[j], j)
    chunks, answers = lax.optimization_barrier((chunks, answers))
    total = chunks[0]
    for k in range(outer - 1, 0, -1):
        total = total + along(sizes, chunks[k], k)
    return total, answers


def spread_chunks(sizes, total):
    outer, inner, chip, _ = sizes
    near = []
    for k in range(outer):
        slow, fast = ("inner", "chip") if k % 2 else ("chip", "inner")
        x = along(sizes, total, k) if k else total
        row = [across(sizes, fast, x, j) if j else x for j in range(sizes[AXES.index(fast)])]
        for j in range(sizes[AXES.index(slow)]):
            near += [across(sizes, slow, x, j) if j else x for x in row]
    return near


def per_device(
    sizes, codebook, weight_in, bias_in, weight_out, bias_out, latents, cotangent, code_owner, code_row
):
    outer, inner, chip, core = sizes
    devices = outer * inner * chip * core
    rows, dim_in = codebook.shape
    hidden_size = weight_in.shape[1]
    count, width = latents.shape
    capacity = max(2, 2 * count // devices)

    outgoing, slots = route(devices, capacity, code_owner, code_row, latents, cotangent)
    outgoing, bias_in = lax.optimization_barrier((outgoing, bias_in))
    incoming = lax.all_to_all(outgoing, AXES, split_axis=0, concat_axis=0, tiled=True)

    hidden_t, codebook_t, slope, projected, parts = forward(
        codebook, weight_in, bias_in, weight_out, bias_out
    )
    picked, wanted = pick_rows(capacity, incoming, parts)
    answers = lax.all_to_all(picked, AXES, split_axis=0, concat_axis=0, tiled=True)

    pieces = backward(
        sizes, capacity, incoming, wanted, hidden_t, slope, projected, codebook_t, weight_out.T
    )
    total, answers = sum_chunks(sizes, list(pieces[:outer]), list(pieces[outer:]), answers)
    answers = answers.reshape(-1, width)
    near = spread_chunks(sizes, total)

    slot_ids = jnp.arange(devices * capacity, dtype=jnp.int32)
    from_slot = slots.reshape(-1, 1) == slot_ids[None, :]
    chosen = pick(from_slot.astype(jnp.bfloat16), answers)
    latent_grad = cotangent - 0.25 * (chosen - latents)
    late = len(near) - inner * chip
    near[late], latent_grad = lax.optimization_barrier((near[late], latent_grad))

    chunks = near + [across(sizes, "core", x, 1) for x in near]
    gw_in, gw_out, biases = assemble(sizes, chunks, dim_in, hidden_size, width)
    biases = biases.reshape(-1)
    gb_in, gb_out = biases[:hidden_size], biases[hidden_size : hidden_size + width]
    return (latent_grad, gw_in, gb_in, gw_out, gb_out)


def solution(mesh):
    code, data = mesh.shape["code"], mesh.shape["dp"]
    core = 2
    outer = 1
    while outer * outer < code:
        outer *= 2
    sizes = (outer, code // outer, data // core, core)
    fine = Mesh(mesh.devices.reshape(sizes), AXES)
    rows = P(AXES, None)
    return jax.shard_map(
        functools.partial(per_device, sizes),
        mesh=fine,
        in_specs=(rows, P(), P(), P(), P(), rows, rows, rows, P(AXES)),
        out_specs=(rows, P(), P(), P(), P()),
        check_vma=False,
    )
```

```python
import functools

import jax
import jax.numpy as jnp
from jax import lax
from jax.experimental import pallas as pl
from jax.experimental.pallas import tpu as pltpu
from jax.sharding import Mesh, PartitionSpec as P

scale_gelu = 0.7978845608028654
cubic_term = 0.044715
LANES = 128
EXTRA = 8
AXES = ("outer", "inner", "chip", "core")


def gelu_parts(x):
    tangent = jnp.tanh(scale_gelu * (x + cubic_term * x * x * x))
    value = 0.5 * x * (1.0 + tangent)
    slope = 0.5 * (1.0 + tangent) + 0.5 * x * (1.0 - tangent * tangent) * scale_gelu * (
        1.0 + 3.0 * cubic_term * x * x
    )
    return value, slope


def split_two(x):
    high = lax.reduce_precision(x, 8, 7)
    low = (x - high).astype(jnp.bfloat16)
    return jnp.concatenate([high.astype(jnp.bfloat16), low], axis=1)


def pick(chooser, rows):
    width = rows.shape[1]
    both = jnp.dot(chooser, split_two(rows), preferred_element_type=jnp.float32)
    return both[:, :width] + both[:, width:]


def dot(a, b):
    return jnp.dot(a, b, preferred_element_type=jnp.float32)


def forward_kernel(codebook_ref, weight_in_ref, bias_in_ref, weight_out_ref, bias_out_ref,
                   hidden_ref, codebook_t_ref, slope_ref, projected_ref, parts_ref):
    width = projected_ref.shape[1]
    codebook = codebook_ref[...]
    codebook_t_ref[...] = jnp.transpose(codebook.astype(jnp.float32)).astype(jnp.bfloat16)
    hidden, slope = gelu_parts(dot(codebook, weight_in_ref[...]) + bias_in_ref[...])
    slope_ref[...] = slope
    hidden_ref[...] = jnp.transpose(hidden).astype(jnp.bfloat16)
    projected = dot(hidden.astype(jnp.bfloat16), weight_out_ref[...]) + bias_out_ref[...]
    projected_ref[...] = projected
    high = projected.astype(jnp.bfloat16)
    parts_ref[:, :width] = high
    parts_ref[:, width:] = (projected - high.astype(jnp.float32)).astype(jnp.bfloat16)


def forward(codebook, weight_in, bias_in, weight_out, bias_out):
    rows, dim_in = codebook.shape
    hidden_size, width = weight_out.shape
    tile = min(256, rows)
    whole = lambda *shape: pl.BlockSpec(shape, lambda i: (0, 0))
    return pl.pallas_call(
        forward_kernel,
        grid=(rows // tile,),
        in_specs=[
            pl.BlockSpec((tile, dim_in), lambda i: (i, 0)),
            whole(dim_in, hidden_size),
            whole(1, hidden_size),
            whole(hidden_size, width),
            whole(1, width),
        ],
        out_specs=[
            pl.BlockSpec((hidden_size, tile), lambda i: (0, i)),
            pl.BlockSpec((dim_in, tile), lambda i: (0, i)),
            pl.BlockSpec((tile, hidden_size), lambda i: (i, 0)),
            pl.BlockSpec((tile, width), lambda i: (i, 0)),
            pl.BlockSpec((tile, 2 * width), lambda i: (i, 0)),
        ],
        out_shape=[
            jax.ShapeDtypeStruct((hidden_size, rows), jnp.bfloat16),
            jax.ShapeDtypeStruct((dim_in, rows), jnp.bfloat16),
            jax.ShapeDtypeStruct((rows, hidden_size), jnp.float32),
            jax.ShapeDtypeStruct((rows, width), jnp.float32),
            jax.ShapeDtypeStruct((rows, 2 * width), jnp.bfloat16),
        ],
        cost_estimate=pl.CostEstimate(
            flops=2 * rows * hidden_size * (dim_in + width),
            bytes_accessed=14 * rows * hidden_size,
            transcendentals=rows * hidden_size,
        ),
        compiler_params=pltpu.CompilerParams(vmem_limit_bytes=60 * 2**20),
        name="forward",
    )(codebook, weight_in, bias_in.reshape(1, -1), weight_out, bias_out.reshape(1, -1))


def join_wanted(capacity, asked_ref, wanted_ref):
    per_row = LANES // capacity
    for t in range(asked_ref.shape[0] // per_row):
        row = asked_ref[t * per_row]
        for k in range(1, per_row):
            row = jnp.maximum(row, pltpu.roll(asked_ref[t * per_row + k], k * capacity, 1))
        wanted_ref[:, t * LANES : (t + 1) * LANES] = row


def pick_kernel(capacity, incoming_hbm, parts_hbm, *refs):
    out_refs, (wanted_ref, asked_ref, parts_ref, sems) = refs[:-4], refs[-4:]
    devices = asked_ref.shape[0]
    rows, both = parts_ref.shape
    width = both // 2
    step = pl.program_id(0)

    @pl.when(step == 0)
    def _():
        payload = incoming_hbm.shape[1] - EXTRA
        load = pltpu.make_async_copy(
            incoming_hbm.at[pl.ds(0, devices), pl.ds(payload, EXTRA)], asked_ref, sems.at[0]
        )
        load.start()
        more = pltpu.make_async_copy(parts_hbm, parts_ref, sems.at[1])
        more.start()
        load.wait()
        join_wanted(capacity, asked_ref, wanted_ref)
        more.wait()

    tile = out_refs[0].shape[0] * capacity
    lane = lax.broadcasted_iota(jnp.int32, (LANES, LANES), 1).astype(jnp.float32)
    choosers = []
    for start in range(0, tile, LANES):
        at = pl.ds(pl.multiple_of(step * tile + start, LANES), LANES)
        column = jnp.transpose(jnp.broadcast_to(wanted_ref[0:1, at], (LANES, LANES)))
        choosers.append(jnp.concatenate(
            [
                (column == lane + float(r)).astype(jnp.float32).astype(jnp.bfloat16)
                for r in range(0, rows, LANES)
            ],
            axis=1,
        ))
    value = dot(jnp.concatenate(choosers, axis=0), parts_ref[...])
    value = value[:, :width] + value[:, width:]
    for j, out_ref in enumerate(out_refs):
        for k in range(out_ref.shape[0]):
            out_ref[k] = value[k * capacity : (k + 1) * capacity, j * LANES : (j + 1) * LANES]


def pick_rows(capacity, incoming, parts):
    devices = incoming.shape[0]
    rows, both = parts.shape
    steps = 4
    blocks = both // 2 // LANES
    return pl.pallas_call(
        functools.partial(pick_kernel, capacity),
        grid=(steps,),
        in_specs=[pl.BlockSpec(memory_space=pl.ANY)] * 2,
        out_specs=[pl.BlockSpec((devices // steps, capacity, LANES), lambda i: (i, 0, 0))] * blocks,
        out_shape=[jax.ShapeDtypeStruct((devices, capacity, LANES), jnp.float32)] * blocks,
        scratch_shapes=[
            pltpu.VMEM((EXTRA, devices * capacity), jnp.float32),
            pltpu.VMEM((devices, EXTRA, LANES), jnp.float32),
            pltpu.VMEM((rows, both), jnp.bfloat16),
            pltpu.SemaphoreType.DMA((2,)),
        ],
        cost_estimate=pl.CostEstimate(
            flops=2 * devices * capacity * rows * both,
            bytes_accessed=4 * devices * capacity * both,
            transcendentals=0,
        ),
        compiler_params=pltpu.CompilerParams(vmem_limit_bytes=24 * 2**20),
        name="pick_rows",
    )(incoming, parts)


def route_kernel(devices, capacity, owner_hbm, row_hbm, latents_hbm, cotangent_hbm,
                 out_ref, slot_ref, owner_ref, row_ref, latents_ref, cotangent_ref, parts_ref, sems):
    count, width = latents_ref.shape
    step = pl.program_id(0)
    tile = out_ref.shape[0] * capacity

    @pl.when(step == 0)
    def _():
        loads = [
            pltpu.make_async_copy(a, b, sems.at[k])
            for k, (a, b) in enumerate((
                (owner_hbm, owner_ref), (row_hbm, row_ref),
                (latents_hbm, latents_ref), (cotangent_hbm, cotangent_ref),
            ))
        ]
        for load in loads:
            load.start()
        before = (
            lax.broadcasted_iota(jnp.int32, (LANES, LANES), 0)
            < lax.broadcasted_iota(jnp.int32, (LANES, LANES), 1)
        ).astype(jnp.bfloat16)
        owner_ids = lax.broadcasted_iota(jnp.int32, (devices, LANES), 0)
        lane = lax.broadcasted_iota(jnp.int32, (LANES, LANES), 1)
        seen = jnp.zeros((devices, 1), jnp.float32)
        loads[0].wait()
        loads[1].wait()
        for start in range(0, count, LANES):
            part = pl.ds(start, LANES)
            owners = owner_ref[:, part]
            mine = (owner_ids == owners).astype(jnp.float32)
            ranks = dot(mine.astype(jnp.bfloat16), before) + seen
            rank = jnp.sum(mine * ranks, axis=0, keepdims=True)
            seen = seen + jnp.sum(mine, axis=1, keepdims=True)
            slot_ref[:, part] = owners * capacity + rank.astype(jnp.int32)
            rows = jnp.transpose(
                jnp.broadcast_to(row_ref[:, part].astype(jnp.float32), (LANES, LANES))
            )
            tall = jnp.floor(rows * (1.0 / 32.0))
            extra = jnp.where(lane == 0, tall, jnp.where(lane == 1, rows - 32.0 * tall, 0.0))
            extra = jnp.where(lane == 2, 1.0, extra)
            parts_ref[part, 2 * width :] = extra.astype(jnp.bfloat16)
        loads[2].wait()
        loads[3].wait()
        for start in range(0, count, LANES):
            part = pl.ds(start, LANES)
            value = cotangent_ref[part, :] - latents_ref[part, :]
            high = value.astype(jnp.bfloat16)
            parts_ref[part, :width] = high
            parts_ref[part, width : 2 * width] = (value - high.astype(jnp.float32)).astype(
                jnp.bfloat16
            )

    ids = lax.broadcasted_iota(jnp.int32, (tile, count), 0) + step * tile
    chooser = (ids == slot_ref[...]).astype(jnp.float32).astype(jnp.bfloat16)
    both = dot(chooser, parts_ref[...])
    value = both[:, :width] + both[:, width : 2 * width]
    turned = jnp.transpose(both[:, 2 * width :])
    wanted = 32.0 * turned[0:1] + turned[1:2] + turned[2:3] - 1.0
    lane = lax.broadcasted_iota(jnp.int32, (EXTRA, LANES), 1)
    for k in range(out_ref.shape[0]):
        own = slice(k * capacity, (k + 1) * capacity)
        for j in range(width // LANES):
            out_ref[k, j * capacity : (j + 1) * capacity, :] = value[own, j * LANES : (j + 1) * LANES]
        at = k * capacity // LANES * LANES
        row = jnp.broadcast_to(wanted[:, at : at + LANES], (EXTRA, LANES))
        shift = k * capacity - at
        if shift:
            row = pltpu.roll(row, LANES - shift, 1)
        out_ref[k, width // LANES * capacity :, :] = jnp.where(lane < capacity, row, -1.0)


def route(devices, capacity, code_owner, code_row, latents, cotangent):
    count, width = latents.shape
    per_step = max(1, 512 // capacity)
    block = width // LANES * capacity + EXTRA
    whole = lambda *shape: pl.BlockSpec(shape, lambda i: (0,) * len(shape))
    return pl.pallas_call(
        functools.partial(route_kernel, devices, capacity),
        grid=(devices // per_step,),
        in_specs=[pl.BlockSpec(memory_space=pl.ANY)] * 4,
        out_specs=[
            pl.BlockSpec((per_step, block, LANES), lambda i: (i, 0, 0)),
            whole(1, count),
        ],
        out_shape=[
            jax.ShapeDtypeStruct((devices, block, LANES), jnp.float32),
            jax.ShapeDtypeStruct((1, count), jnp.int32),
        ],
        scratch_shapes=[
            pltpu.VMEM((1, count), jnp.int32),
            pltpu.VMEM((1, count), jnp.int32),
            pltpu.VMEM((count, width), jnp.float32),
            pltpu.VMEM((count, width), jnp.float32),
            pltpu.VMEM((count, 2 * width + LANES), jnp.bfloat16),
            pltpu.SemaphoreType.DMA((4,)),
        ],
        compiler_params=pltpu.CompilerParams(vmem_limit_bytes=60 * 2**20),
        name="route",
    )(code_owner.reshape(1, count), code_row.reshape(1, count), latents, cotangent)


def place(sizes, k, j):
    _, inner, chip, _ = sizes
    if k % 2:
        return j
    return j % inner * chip + j // inner


def backward_kernel(sizes, capacity, incoming_hbm, hidden_hbm, slope_hbm, projected_hbm,
                    codebook_hbm, weight_hbm, *refs):
    outer, inner, chip, core = sizes
    devices = outer * inner * chip * core
    mine_hbm, theirs_hbm, refs = refs[:outer], refs[outer : 2 * outer], refs[2 * outer :]
    (asked, incoming, hidden, slope, projected, codebook, weight, parts, wanted, low, grad, flat,
     in_sem, out_sem) = refs
    width = projected.shape[1]
    dim_in, rows = codebook.shape
    hidden_size = hidden.shape[0]
    length = flat.shape[2] - EXTRA
    pairs = list(zip(
        (incoming_hbm.at[pl.ds(0, devices), pl.ds(width // LANES * capacity, EXTRA)],
         projected_hbm, weight_hbm, slope_hbm, hidden_hbm, codebook_hbm),
        (asked, projected, weight, slope, hidden, codebook),
    ))
    loads = [pltpu.make_async_copy(a, b, in_sem.at[k]) for k, (a, b) in enumerate(pairs)]
    loads[0].start()
    blocks = width // LANES
    quarter = devices // 4
    arrivals = []
    for n in range(4):
        part = pl.ds(n * quarter, quarter)
        arrivals.append(pltpu.make_async_copy(
            incoming_hbm.at[part, pl.ds(0, blocks * capacity)], incoming.at[part], in_sem.at[6 + n]
        ))
        arrivals[n].start()
    for load in loads[1:]:
        load.start()
    for n in range(4):
        arrivals[n].wait()
        for s in range(n * quarter, (n + 1) * quarter):
            own = pl.ds(s * capacity, capacity)
            for j in range(blocks):
                value = incoming[s, j * capacity : (j + 1) * capacity, :]
                high = value.astype(jnp.bfloat16)
                parts[own, j * LANES : (j + 1) * LANES] = high
                parts[own, width + j * LANES : width + (j + 1) * LANES] = (
                    value - high.astype(jnp.float32)
                ).astype(jnp.bfloat16)
    loads[0].wait()
    join_wanted(capacity, asked, wanted)
    for load in loads[1:4]:
        load.wait()
    tile = min(512, rows)
    bias_in = jnp.zeros((1, hidden_size), jnp.float32)
    bias_out = jnp.zeros((1, width), jnp.float32)
    for start in range(0, rows, tile):
        part = pl.ds(start, tile)
        ids = (lax.broadcasted_iota(jnp.int32, (tile, wanted.shape[1]), 0) + start).astype(
            jnp.float32
        )
        chooser = (ids == wanted[0:1, :]).astype(jnp.float32)
        times = jnp.sum(chooser, axis=1, keepdims=True)
        both = dot(chooser.astype(jnp.bfloat16), parts[...])
        code_grad = both[:, :width] + both[:, width:] + times * projected[part, :]
        bias_out += jnp.sum(code_grad, axis=0, keepdims=True)
        code_low = code_grad.astype(jnp.bfloat16)
        low[part, :] = code_low
        preact_grad = (dot(code_low, weight[...]) * slope[part, :]).astype(jnp.bfloat16)
        grad[part, :] = preact_grad
        bias_in += jnp.sum(preact_grad.astype(jnp.float32), axis=0, keepdims=True)


    first = lax.axis_index("outer")
    plane = lax.axis_index("inner") * chip + lax.axis_index("chip")
    me = lax.axis_index("core")
    band = hidden_size // outer
    pieces = inner * chip
    home = lax.rem(outer - first, outer)
    for k in range(outer):
        for e in range(pieces * core):
            flat[k, e, length:, :] = jnp.zeros((EXTRA, LANES), jnp.float32)
    biases = [bias_in[:, k : k + LANES] for k in range(0, hidden_size, LANES)]
    biases += [bias_out[:, k : k + LANES] for k in range(0, width, LANES)]
    for j, bias in enumerate(biases):
        flat[home, j // EXTRA, length + j % EXTRA : length + j % EXTRA + 1, :] = bias

    loads[4].wait()
    loads[5].wait()
    stores = []
    for k in range(outer - 1, -1, -1):
        o = lax.rem(first + k, outer)
        here = pl.ds(pl.multiple_of(o * band, band), band)

        def keep(row, value):
            for r in range(0, value.shape[0], length):
                flat[k, (row + r) // length, :length, :] = value[r : r + length, :]

        out = dot(codebook[...], grad[:, here])
        for j in range(band // LANES):
            keep(j * dim_in, out[:, j * LANES : (j + 1) * LANES])
        out = dot(hidden[here, :], low[...])
        for j in range(blocks):
            keep(band // LANES * dim_in + j * band, out[:, j * LANES : (j + 1) * LANES])
        for target, c in ((theirs_hbm, 1 - me), (mine_hbm, me)):
            for j in range(pieces):
                e = lax.bitwise_xor(plane, place(sizes, k, j)) * core + c
                copy = pltpu.make_async_copy(
                    flat.at[k, e], target[k].at[j], out_sem.at[len(stores)]
                )
                copy.start()
                stores.append(copy)
    for copy in stores:
        copy.wait()


def backward(sizes, capacity, incoming, hidden_t, slope, projected, codebook_t, weight_t):
    devices = incoming.shape[0]
    rows, width = projected.shape
    dim_in, hidden_size = codebook_t.shape[0], hidden_t.shape[0]
    length = (dim_in + width) * hidden_size // LANES // devices
    outer, inner, chip, core = sizes
    piece = jax.ShapeDtypeStruct((inner * chip, length + EXTRA, LANES), jnp.float32)
    operands = (incoming, hidden_t, slope, projected, codebook_t, weight_t)
    vmem = lambda shape, dtype: pltpu.VMEM(shape, dtype)
    slots = devices * capacity
    return pl.pallas_call(
        functools.partial(backward_kernel, sizes, capacity),
        in_specs=[pl.BlockSpec(memory_space=pl.ANY)] * len(operands),
        out_specs=[pl.BlockSpec(memory_space=pl.ANY)] * (2 * outer),
        out_shape=[piece] * (2 * outer),
        scratch_shapes=[
            vmem((devices, EXTRA, LANES), jnp.float32),
            vmem((devices, incoming.shape[1] - EXTRA, LANES), jnp.float32),
        ]
        + [vmem(a.shape, a.dtype) for a in operands[1:]]
        + [
            vmem((slots, 2 * width), jnp.bfloat16),
            vmem((EXTRA, slots), jnp.float32),
            vmem((rows, width), jnp.bfloat16),
            vmem((rows, hidden_size), jnp.bfloat16),
            vmem((outer, inner * chip * core, length + EXTRA, LANES), jnp.float32),
            pltpu.SemaphoreType.DMA((10,)),
            pltpu.SemaphoreType.DMA((devices,)),
        ],
        cost_estimate=pl.CostEstimate(
            flops=2 * rows * (slots * 2 * width + hidden_size * (2 * width + dim_in)),
            bytes_accessed=16 * rows * hidden_size,
            transcendentals=0,
        ),
        compiler_params=pltpu.CompilerParams(vmem_limit_bytes=40 * 2**20),
        name="backward",
    )(*operands)


def assemble_kernel(sizes, *refs):
    outer, inner, chip, core = sizes
    devices = outer * inner * chip * core
    pieces, (weight_in, weight_out, biases, sems, bias_sem) = refs[:devices], refs[devices:]
    length = pieces[0].shape[0] - EXTRA
    dim_in, hidden_size = weight_in.shape
    band = hidden_size // outer
    base = band // LANES * dim_in
    first = lax.axis_index("outer")
    plane = lax.axis_index("inner") * chip + lax.axis_index("chip")
    me = lax.axis_index("core")
    copies = []
    for n, piece in enumerate(pieces):
        c, n = divmod(n, devices // core)
        k, j = divmod(n, inner * chip)
        n += c * (devices // core)
        o = lax.rem(first + outer - k, outer)
        e = lax.bitwise_xor(plane, place(sizes, k, j)) * core + lax.bitwise_xor(me, c)
        at = e * length
        source = piece.at[pl.ds(0, length)]

        def copy_to(target, row, column):
            rows = pl.ds(pl.multiple_of(row, length), length)
            lanes = pl.ds(pl.multiple_of(column * LANES, LANES), LANES)
            return pltpu.make_async_copy(source, target.at[rows, lanes], sems.at[n])

        @pl.when(at < base)
        def _():
            column = o * (band // LANES) + lax.div(at, dim_in)
            copy_to(weight_in, lax.rem(at, dim_in), column).start()

        @pl.when(at >= base)
        def _():
            copy_to(weight_out, o * band + lax.rem(at - base, band), lax.div(at - base, band)).start()

        @pl.when((o == 0) & (e < 2))
        def _():
            copy = pltpu.make_async_copy(
                piece.at[pl.ds(length, EXTRA)], biases.at[jnp.minimum(e, 1)], bias_sem
            )
            copy.start()
            copy.wait()

        copies.append(copy_to(weight_in, 0, 0))
    for copy in copies:
        copy.wait()


def assemble(sizes, pieces, dim_in, hidden_size, width):
    hbm = pl.BlockSpec(memory_space=pl.ANY)
    return pl.pallas_call(
        functools.partial(assemble_kernel, sizes),
        in_specs=[hbm] * len(pieces),
        out_specs=[hbm] * 3,
        out_shape=[
            jax.ShapeDtypeStruct((dim_in, hidden_size), jnp.float32),
            jax.ShapeDtypeStruct((hidden_size, width), jnp.float32),
            jax.ShapeDtypeStruct((2, EXTRA, LANES), jnp.float32),
        ],
        scratch_shapes=[
            pltpu.SemaphoreType.DMA((len(pieces),)),
            pltpu.SemaphoreType.DMA,
        ],
        compiler_params=pltpu.CompilerParams(vmem_limit_bytes=4 * 2**20),
        name="assemble",
    )(*pieces)


def along(sizes, x, k):
    outer = sizes[0]
    return lax.ppermute(x, "outer", [(o, (o + k) % outer) for o in range(outer)])


def across(sizes, axis, x, j):
    size = sizes[AXES.index(axis)]
    return lax.ppermute(x, axis, [(p, p ^ j) for p in range(size)])


def sum_chunks(sizes, mine, theirs, first_answers):
    outer, inner, chip, _ = sizes
    chunks = [None] * outer
    for k in range(outer - 1, -1, -1):
        slow, fast = ("inner", "chip") if k % 2 else ("chip", "inner")
        low = sizes[AXES.index(fast)]
        arrived = across(sizes, "core", theirs[k], 1)
        part = mine[k][:low] + arrived[:low]
        for j in range(1, sizes[AXES.index(slow)]):
            here = slice(j * low, (j + 1) * low)
            part = part + across(sizes, slow, mine[k][here] + arrived[here], j)
        chunks[k] = part[0]
        for j in range(1, low):
            chunks[k] = chunks[k] + across(sizes, fast, part[j], j)
    chunks, first_answers = lax.optimization_barrier((chunks, first_answers))
    total = chunks[0]
    for k in range(outer - 1, 0, -1):
        total = total + along(sizes, chunks[k], k)
    return total, first_answers


def spread_chunks(sizes, total, second):
    outer, inner, chip, _ = sizes
    near = []
    lines = [along(sizes, total, k) if k else total for k in range(outer)]
    lines[outer // 2], second = lax.optimization_barrier((lines[outer // 2], second))
    for k, x in enumerate(lines):
        slow, fast = ("inner", "chip") if k % 2 else ("chip", "inner")
        row = [across(sizes, fast, x, j) if j else x for j in range(sizes[AXES.index(fast)])]
        for j in range(sizes[AXES.index(slow)]):
            near += [across(sizes, slow, x, j) if j else x for x in row]
    return near, second


def per_device(
    sizes, codebook, weight_in, bias_in, weight_out, bias_out, latents, cotangent, code_owner, code_row
):
    outer, inner, chip, core = sizes
    devices = outer * inner * chip * core
    rows, dim_in = codebook.shape
    hidden_size = weight_in.shape[1]
    count, width = latents.shape
    capacity = max(2, 2 * count // devices)

    outgoing, slots = route(devices, capacity, code_owner, code_row, latents, cotangent)
    outgoing, bias_in = lax.optimization_barrier((outgoing, bias_in))
    incoming = lax.all_to_all(outgoing, AXES, split_axis=0, concat_axis=0, tiled=True)

    hidden_t, codebook_t, slope, projected, parts = forward(
        codebook, weight_in, bias_in, weight_out, bias_out
    )
    pieces = backward(
        sizes, capacity, incoming, hidden_t, slope, projected, codebook_t, weight_out.T
    )
    mine, theirs = list(pieces[:outer]), list(pieces[outer:])
    theirs[0], incoming = lax.optimization_barrier((theirs[0], incoming))

    def exchange(x):
        x = lax.all_to_all(x, AXES, split_axis=0, concat_axis=0, tiled=True)
        return x.reshape(-1, x.shape[-1])

    picked = pick_rows(capacity, incoming, parts)
    total, first = sum_chunks(sizes, mine, theirs, exchange(picked[0]))
    near, second = spread_chunks(sizes, total, list(picked[1:]))

    slot_ids = jnp.arange(devices * capacity, dtype=jnp.int32)
    from_slot = (slots.reshape(-1, 1) == slot_ids[None, :]).astype(jnp.bfloat16)
    first = pick(from_slot, first)
    late = len(near) - inner * chip
    near[late], first = lax.optimization_barrier((near[late], first))
    chosen = jnp.concatenate([first] + [pick(from_slot, exchange(x)) for x in second], axis=1)
    latent_grad = cotangent - 0.25 * (chosen - latents)

    chunks = near + [across(sizes, "core", x, 1) for x in near]
    gw_in, gw_out, biases = assemble(sizes, chunks, dim_in, hidden_size, width)
    biases = biases.reshape(-1)
    gb_in, gb_out = biases[:hidden_size], biases[hidden_size : hidden_size + width]
    return (latent_grad, gw_in, gb_in, gw_out, gb_out)


def solution(mesh):
    code, data = mesh.shape["code"], mesh.shape["dp"]
    core = 2
    outer = 1
    while outer * outer < code:
        outer *= 2
    sizes = (outer, code // outer, data // core, core)
    fine = Mesh(mesh.devices.reshape(sizes), AXES)
    rows = P(AXES, None)
    return jax.shard_map(
        functools.partial(per_device, sizes),
        mesh=fine,
        in_specs=(rows, P(), P(), P(), P(), rows, rows, rows, P(AXES)),
        out_specs=(rows, P(), P(), P(), P()),
        check_vma=False,
    )
```

```python
import functools

import jax
import jax.numpy as jnp
from jax import lax
from jax.experimental import pallas as pl
from jax.experimental.pallas import tpu as pltpu
from jax.sharding import Mesh, PartitionSpec as P

scale_gelu = 0.7978845608028654
cubic_term = 0.044715
LANES = 128
EXTRA = 8
AXES = ("outer", "inner", "chip", "core")


def gelu_parts(x):
    tangent = jnp.tanh(scale_gelu * (x + cubic_term * x * x * x))
    value = 0.5 * x * (1.0 + tangent)
    slope = 0.5 * (1.0 + tangent) + 0.5 * x * (1.0 - tangent * tangent) * scale_gelu * (
        1.0 + 3.0 * cubic_term * x * x
    )
    return value, slope


def split_two(x):
    high = lax.reduce_precision(x, 8, 7)
    low = (x - high).astype(jnp.bfloat16)
    return jnp.concatenate([high.astype(jnp.bfloat16), low], axis=1)


def pick(chooser, rows):
    width = rows.shape[1]
    both = jnp.dot(chooser, split_two(rows), preferred_element_type=jnp.float32)
    return both[:, :width] + both[:, width:]


def dot(a, b):
    return jnp.dot(a, b, preferred_element_type=jnp.float32)


def forward_kernel(codebook_ref, weight_in_ref, bias_in_ref, weight_out_ref, bias_out_ref,
                   hidden_ref, codebook_t_ref, slope_ref, projected_ref, parts_ref):
    width = projected_ref.shape[1]
    codebook = codebook_ref[...]
    codebook_t_ref[...] = jnp.transpose(codebook.astype(jnp.float32)).astype(jnp.bfloat16)
    hidden, slope = gelu_parts(dot(codebook, weight_in_ref[...]) + bias_in_ref[...])
    slope_ref[...] = slope
    hidden_ref[...] = jnp.transpose(hidden).astype(jnp.bfloat16)
    projected = dot(hidden.astype(jnp.bfloat16), weight_out_ref[...]) + bias_out_ref[...]
    projected_ref[...] = projected
    high = projected.astype(jnp.bfloat16)
    parts_ref[:, :width] = high
    parts_ref[:, width:] = (projected - high.astype(jnp.float32)).astype(jnp.bfloat16)


def forward(codebook, weight_in, bias_in, weight_out, bias_out):
    rows, dim_in = codebook.shape
    hidden_size, width = weight_out.shape
    tile = min(256, rows)
    whole = lambda *shape: pl.BlockSpec(shape, lambda i: (0, 0))
    return pl.pallas_call(
        forward_kernel,
        grid=(rows // tile,),
        in_specs=[
            pl.BlockSpec((tile, dim_in), lambda i: (i, 0)),
            whole(dim_in, hidden_size),
            whole(1, hidden_size),
            whole(hidden_size, width),
            whole(1, width),
        ],
        out_specs=[
            pl.BlockSpec((hidden_size, tile), lambda i: (0, i)),
            pl.BlockSpec((dim_in, tile), lambda i: (0, i)),
            pl.BlockSpec((tile, hidden_size), lambda i: (i, 0)),
            pl.BlockSpec((tile, width), lambda i: (i, 0)),
            pl.BlockSpec((tile, 2 * width), lambda i: (i, 0)),
        ],
        out_shape=[
            jax.ShapeDtypeStruct((hidden_size, rows), jnp.bfloat16),
            jax.ShapeDtypeStruct((dim_in, rows), jnp.bfloat16),
            jax.ShapeDtypeStruct((rows, hidden_size), jnp.float32),
            jax.ShapeDtypeStruct((rows, width), jnp.float32),
            jax.ShapeDtypeStruct((rows, 2 * width), jnp.bfloat16),
        ],
        cost_estimate=pl.CostEstimate(
            flops=2 * rows * hidden_size * (dim_in + width),
            bytes_accessed=14 * rows * hidden_size,
            transcendentals=rows * hidden_size,
        ),
        compiler_params=pltpu.CompilerParams(vmem_limit_bytes=60 * 2**20),
        name="forward",
    )(codebook, weight_in, bias_in.reshape(1, -1), weight_out, bias_out.reshape(1, -1))


def join_wanted(capacity, asked_ref, wanted_ref):
    per_row = LANES // capacity
    for t in range(asked_ref.shape[0] // per_row):
        row = asked_ref[t * per_row]
        for k in range(1, per_row):
            row = jnp.maximum(row, pltpu.roll(asked_ref[t * per_row + k], k * capacity, 1))
        wanted_ref[:, t * LANES : (t + 1) * LANES] = row


def pick_kernel(capacity, incoming_hbm, parts_hbm, *refs):
    out_ref, wanted_ref, asked_ref, parts_ref, sems = refs
    devices = asked_ref.shape[0]
    rows, both = parts_ref.shape
    width = both // 2
    step = pl.program_id(0)

    @pl.when(step == 0)
    def _():
        payload = incoming_hbm.shape[1] - EXTRA
        load = pltpu.make_async_copy(
            incoming_hbm.at[pl.ds(0, devices), pl.ds(payload, EXTRA)], asked_ref, sems.at[0]
        )
        load.start()
        more = pltpu.make_async_copy(parts_hbm, parts_ref, sems.at[1])
        more.start()
        load.wait()
        join_wanted(capacity, asked_ref, wanted_ref)
        more.wait()

    tile = out_ref.shape[0] * capacity
    lane = lax.broadcasted_iota(jnp.int32, (LANES, LANES), 1).astype(jnp.float32)
    choosers = []
    for start in range(0, tile, LANES):
        at = pl.ds(pl.multiple_of(step * tile + start, LANES), LANES)
        column = jnp.transpose(jnp.broadcast_to(wanted_ref[0:1, at], (LANES, LANES)))
        choosers.append(jnp.concatenate(
            [
                (column == lane + float(r)).astype(jnp.float32).astype(jnp.bfloat16)
                for r in range(0, rows, LANES)
            ],
            axis=1,
        ))
    value = dot(jnp.concatenate(choosers, axis=0), parts_ref[...])
    value = value[:, :width] + value[:, width:]
    for k in range(out_ref.shape[0]):
        out_ref[k] = value[k * capacity : (k + 1) * capacity]


def pick_rows(capacity, incoming, parts):
    devices = incoming.shape[0]
    rows, both = parts.shape
    steps = 4
    return pl.pallas_call(
        functools.partial(pick_kernel, capacity),
        grid=(steps,),
        in_specs=[pl.BlockSpec(memory_space=pl.ANY)] * 2,
        out_specs=pl.BlockSpec((devices // steps, capacity, both // 2), lambda i: (i, 0, 0)),
        out_shape=jax.ShapeDtypeStruct((devices, capacity, both // 2), jnp.float32),
        scratch_shapes=[
            pltpu.VMEM((EXTRA, devices * capacity), jnp.float32),
            pltpu.VMEM((devices, EXTRA, LANES), jnp.float32),
            pltpu.VMEM((rows, both), jnp.bfloat16),
            pltpu.SemaphoreType.DMA((2,)),
        ],
        cost_estimate=pl.CostEstimate(
            flops=2 * devices * capacity * rows * both,
            bytes_accessed=4 * devices * capacity * both,
            transcendentals=0,
        ),
        compiler_params=pltpu.CompilerParams(vmem_limit_bytes=60 * 2**20),
        name="pick_rows",
    )(incoming, parts)


def route_kernel(devices, capacity, owner_hbm, row_hbm, latents_hbm, cotangent_hbm,
                 out_ref, slot_ref, owner_ref, row_ref, latents_ref, cotangent_ref, parts_ref, sems):
    count, width = latents_ref.shape
    step = pl.program_id(0)
    tile = out_ref.shape[0] * capacity

    @pl.when(step == 0)
    def _():
        loads = [
            pltpu.make_async_copy(a, b, sems.at[k])
            for k, (a, b) in enumerate((
                (owner_hbm, owner_ref), (row_hbm, row_ref),
                (latents_hbm, latents_ref), (cotangent_hbm, cotangent_ref),
            ))
        ]
        for load in loads:
            load.start()
        before = (
            lax.broadcasted_iota(jnp.int32, (LANES, LANES), 0)
            < lax.broadcasted_iota(jnp.int32, (LANES, LANES), 1)
        ).astype(jnp.bfloat16)
        owner_ids = lax.broadcasted_iota(jnp.int32, (devices, LANES), 0)
        lane = lax.broadcasted_iota(jnp.int32, (LANES, LANES), 1)
        seen = jnp.zeros((devices, 1), jnp.float32)
        loads[0].wait()
        loads[1].wait()
        for start in range(0, count, LANES):
            part = pl.ds(start, LANES)
            owners = owner_ref[:, part]
            mine = (owner_ids == owners).astype(jnp.float32)
            ranks = dot(mine.astype(jnp.bfloat16), before) + seen
            rank = jnp.sum(mine * ranks, axis=0, keepdims=True)
            seen = seen + jnp.sum(mine, axis=1, keepdims=True)
            slot_ref[:, part] = owners * capacity + rank.astype(jnp.int32)
            rows = jnp.transpose(
                jnp.broadcast_to(row_ref[:, part].astype(jnp.float32), (LANES, LANES))
            )
            tall = jnp.floor(rows * (1.0 / 32.0))
            extra = jnp.where(lane == 0, tall, jnp.where(lane == 1, rows - 32.0 * tall, 0.0))
            extra = jnp.where(lane == 2, 1.0, extra)
            parts_ref[part, 2 * width :] = extra.astype(jnp.bfloat16)
        loads[2].wait()
        loads[3].wait()
        for start in range(0, count, LANES):
            part = pl.ds(start, LANES)
            value = cotangent_ref[part, :] - latents_ref[part, :]
            high = value.astype(jnp.bfloat16)
            parts_ref[part, :width] = high
            parts_ref[part, width : 2 * width] = (value - high.astype(jnp.float32)).astype(
                jnp.bfloat16
            )

    ids = lax.broadcasted_iota(jnp.int32, (tile, count), 0) + step * tile
    chooser = (ids == slot_ref[...]).astype(jnp.float32).astype(jnp.bfloat16)
    both = dot(chooser, parts_ref[...])
    value = both[:, :width] + both[:, width : 2 * width]
    turned = jnp.transpose(both[:, 2 * width :])
    wanted = 32.0 * turned[0:1] + turned[1:2] + turned[2:3] - 1.0
    lane = lax.broadcasted_iota(jnp.int32, (EXTRA, LANES), 1)
    for k in range(out_ref.shape[0]):
        own = slice(k * capacity, (k + 1) * capacity)
        for j in range(width // LANES):
            out_ref[k, j * capacity : (j + 1) * capacity, :] = value[own, j * LANES : (j + 1) * LANES]
        at = k * capacity // LANES * LANES
        row = jnp.broadcast_to(wanted[:, at : at + LANES], (EXTRA, LANES))
        shift = k * capacity - at
        if shift:
            row = pltpu.roll(row, LANES - shift, 1)
        out_ref[k, width // LANES * capacity :, :] = jnp.where(lane < capacity, row, -1.0)


def route(devices, capacity, code_owner, code_row, latents, cotangent):
    count, width = latents.shape
    per_step = max(1, 512 // capacity)
    block = width // LANES * capacity + EXTRA
    whole = lambda *shape: pl.BlockSpec(shape, lambda i: (0,) * len(shape))
    return pl.pallas_call(
        functools.partial(route_kernel, devices, capacity),
        grid=(devices // per_step,),
        in_specs=[pl.BlockSpec(memory_space=pl.ANY)] * 4,
        out_specs=[
            pl.BlockSpec((per_step, block, LANES), lambda i: (i, 0, 0)),
            whole(1, count),
        ],
        out_shape=[
            jax.ShapeDtypeStruct((devices, block, LANES), jnp.float32),
            jax.ShapeDtypeStruct((1, count), jnp.int32),
        ],
        scratch_shapes=[
            pltpu.VMEM((1, count), jnp.int32),
            pltpu.VMEM((1, count), jnp.int32),
            pltpu.VMEM((count, width), jnp.float32),
            pltpu.VMEM((count, width), jnp.float32),
            pltpu.VMEM((count, 2 * width + LANES), jnp.bfloat16),
            pltpu.SemaphoreType.DMA((4,)),
        ],
        compiler_params=pltpu.CompilerParams(vmem_limit_bytes=60 * 2**20),
        name="route",
    )(code_owner.reshape(1, count), code_row.reshape(1, count), latents, cotangent)


def place(sizes, k, j):
    _, inner, chip, _ = sizes
    if k % 2:
        return j
    return j % inner * chip + j // inner


def backward_kernel(sizes, capacity, incoming_hbm, hidden_hbm, slope_hbm, projected_hbm,
                    codebook_hbm, weight_hbm, *refs):
    outer, inner, chip, core = sizes
    devices = outer * inner * chip * core
    mine_hbm, theirs_hbm, refs = refs[:outer], refs[outer : 2 * outer], refs[2 * outer :]
    (asked, incoming, hidden, slope, projected, codebook, weight, parts, wanted, low, grad, flat,
     in_sem, out_sem) = refs
    width = projected.shape[1]
    dim_in, rows = codebook.shape
    hidden_size = hidden.shape[0]
    length = flat.shape[2] - EXTRA
    pairs = list(zip(
        (incoming_hbm.at[pl.ds(0, devices), pl.ds(width // LANES * capacity, EXTRA)],
         projected_hbm, weight_hbm, slope_hbm, hidden_hbm, codebook_hbm),
        (asked, projected, weight, slope, hidden, codebook),
    ))
    loads = [pltpu.make_async_copy(a, b, in_sem.at[k]) for k, (a, b) in enumerate(pairs)]
    loads[0].start()
    blocks = width // LANES
    quarter = devices // 4
    arrivals = []
    for n in range(4):
        part = pl.ds(n * quarter, quarter)
        arrivals.append(pltpu.make_async_copy(
            incoming_hbm.at[part, pl.ds(0, blocks * capacity)], incoming.at[part], in_sem.at[6 + n]
        ))
        arrivals[n].start()
    for load in loads[1:]:
        load.start()
    for n in range(4):
        arrivals[n].wait()
        for s in range(n * quarter, (n + 1) * quarter):
            own = pl.ds(s * capacity, capacity)
            for j in range(blocks):
                value = incoming[s, j * capacity : (j + 1) * capacity, :]
                high = value.astype(jnp.bfloat16)
                parts[own, j * LANES : (j + 1) * LANES] = high
                parts[own, width + j * LANES : width + (j + 1) * LANES] = (
                    value - high.astype(jnp.float32)
                ).astype(jnp.bfloat16)
    loads[0].wait()
    join_wanted(capacity, asked, wanted)
    for load in loads[1:4]:
        load.wait()
    tile = min(512, rows)
    bias_in = jnp.zeros((1, hidden_size), jnp.float32)
    bias_out = jnp.zeros((1, width), jnp.float32)
    for start in range(0, rows, tile):
        part = pl.ds(start, tile)
        ids = (lax.broadcasted_iota(jnp.int32, (tile, wanted.shape[1]), 0) + start).astype(
            jnp.float32
        )
        chooser = (ids == wanted[0:1, :]).astype(jnp.float32)
        times = jnp.sum(chooser, axis=1, keepdims=True)
        both = dot(chooser.astype(jnp.bfloat16), parts[...])
        code_grad = both[:, :width] + both[:, width:] + times * projected[part, :]
        bias_out += jnp.sum(code_grad, axis=0, keepdims=True)
        code_low = code_grad.astype(jnp.bfloat16)
        low[part, :] = code_low
        preact_grad = (dot(code_low, weight[...]) * slope[part, :]).astype(jnp.bfloat16)
        grad[part, :] = preact_grad
        bias_in += jnp.sum(preact_grad.astype(jnp.float32), axis=0, keepdims=True)


    first = lax.axis_index("outer")
    plane = lax.axis_index("inner") * chip + lax.axis_index("chip")
    me = lax.axis_index("core")
    band = hidden_size // outer
    pieces = inner * chip
    home = lax.rem(outer - first, outer)
    for k in range(outer):
        for e in range(pieces * core):
            flat[k, e, length:, :] = jnp.zeros((EXTRA, LANES), jnp.float32)
    biases = [bias_in[:, k : k + LANES] for k in range(0, hidden_size, LANES)]
    biases += [bias_out[:, k : k + LANES] for k in range(0, width, LANES)]
    for j, bias in enumerate(biases):
        flat[home, j // EXTRA, length + j % EXTRA : length + j % EXTRA + 1, :] = bias

    loads[4].wait()
    loads[5].wait()
    stores = []
    for k in range(outer - 1, -1, -1):
        o = lax.rem(first + k, outer)
        here = pl.ds(pl.multiple_of(o * band, band), band)

        def keep(row, value):
            for r in range(0, value.shape[0], length):
                flat[k, (row + r) // length, :length, :] = value[r : r + length, :]

        out = dot(codebook[...], grad[:, here])
        for j in range(band // LANES):
            keep(j * dim_in, out[:, j * LANES : (j + 1) * LANES])
        out = dot(hidden[here, :], low[...])
        for j in range(blocks):
            keep(band // LANES * dim_in + j * band, out[:, j * LANES : (j + 1) * LANES])
        for target, c in ((theirs_hbm, 1 - me), (mine_hbm, me)):
            for j in range(pieces):
                e = lax.bitwise_xor(plane, place(sizes, k, j)) * core + c
                copy = pltpu.make_async_copy(
                    flat.at[k, e], target[k].at[j], out_sem.at[len(stores)]
                )
                copy.start()
                stores.append(copy)
    for copy in stores:
        copy.wait()


def backward(sizes, capacity, incoming, hidden_t, slope, projected, codebook_t, weight_t):
    devices = incoming.shape[0]
    rows, width = projected.shape
    dim_in, hidden_size = codebook_t.shape[0], hidden_t.shape[0]
    length = (dim_in + width) * hidden_size // LANES // devices
    outer, inner, chip, core = sizes
    piece = jax.ShapeDtypeStruct((inner * chip, length + EXTRA, LANES), jnp.float32)
    operands = (incoming, hidden_t, slope, projected, codebook_t, weight_t)
    vmem = lambda shape, dtype: pltpu.VMEM(shape, dtype)
    slots = devices * capacity
    return pl.pallas_call(
        functools.partial(backward_kernel, sizes, capacity),
        in_specs=[pl.BlockSpec(memory_space=pl.ANY)] * len(operands),
        out_specs=[pl.BlockSpec(memory_space=pl.ANY)] * (2 * outer),
        out_shape=[piece] * (2 * outer),
        scratch_shapes=[
            vmem((devices, EXTRA, LANES), jnp.float32),
            vmem((devices, incoming.shape[1] - EXTRA, LANES), jnp.float32),
        ]
        + [vmem(a.shape, a.dtype) for a in operands[1:]]
        + [
            vmem((slots, 2 * width), jnp.bfloat16),
            vmem((EXTRA, slots), jnp.float32),
            vmem((rows, width), jnp.bfloat16),
            vmem((rows, hidden_size), jnp.bfloat16),
            vmem((outer, inner * chip * core, length + EXTRA, LANES), jnp.float32),
            pltpu.SemaphoreType.DMA((10,)),
            pltpu.SemaphoreType.DMA((devices,)),
        ],
        cost_estimate=pl.CostEstimate(
            flops=2 * rows * (slots * 2 * width + hidden_size * (2 * width + dim_in)),
            bytes_accessed=16 * rows * hidden_size,
            transcendentals=0,
        ),
        compiler_params=pltpu.CompilerParams(vmem_limit_bytes=60 * 2**20),
        name="backward",
    )(*operands)


def assemble_kernel(outer, total_hbm, weight_in, weight_out, biases, held, in_sem, out_sem):
    devices, length = held.shape[0], held.shape[1] - EXTRA
    dim_in, hidden_size = weight_in.shape
    band = hidden_size // outer
    base = band // LANES * dim_in
    loads = [
        pltpu.make_async_copy(total_hbm.at[d], held.at[d], in_sem.at[d]) for d in range(devices)
    ]
    for load in loads:
        load.start()
    copies = []
    for d in range(devices):
        o, at = divmod(d * length, devices // outer * length)
        if at < base:
            target, column, row = weight_in, o * (band // LANES) + at // dim_in, at % dim_in
        else:
            column, row = divmod(at - base, band)
            target, row = weight_out, o * band + row
        loads[d].wait()
        copies.append(pltpu.make_async_copy(
            held.at[d, pl.ds(0, length)],
            target.at[pl.ds(row, length), pl.ds(column * LANES, LANES)],
            out_sem.at[d],
        ))
        copies[-1].start()
        if d < 2:
            copies.append(pltpu.make_async_copy(
                held.at[d, pl.ds(length, EXTRA)], biases.at[d], out_sem.at[devices + d]
            ))
            copies[-1].start()
    for copy in copies:
        copy.wait()


def assemble(outer, total, dim_in, hidden_size, width):
    hbm = pl.BlockSpec(memory_space=pl.ANY)
    devices = total.shape[0]
    return pl.pallas_call(
        functools.partial(assemble_kernel, outer),
        in_specs=[hbm],
        out_specs=[hbm] * 3,
        out_shape=[
            jax.ShapeDtypeStruct((dim_in, hidden_size), jnp.float32),
            jax.ShapeDtypeStruct((hidden_size, width), jnp.float32),
            jax.ShapeDtypeStruct((2, EXTRA, LANES), jnp.float32),
        ],
        scratch_shapes=[
            pltpu.VMEM(total.shape, jnp.float32),
            pltpu.SemaphoreType.DMA((devices,)),
            pltpu.SemaphoreType.DMA((devices + 2,)),
        ],
        compiler_params=pltpu.CompilerParams(vmem_limit_bytes=60 * 2**20),
        name="assemble",
    )(total)


def along(sizes, x, k):
    outer = sizes[0]
    return lax.ppermute(x, "outer", [(o, (o + k) % outer) for o in range(outer)])


def across(sizes, axis, x, j):
    size = sizes[AXES.index(axis)]
    return lax.ppermute(x, axis, [(p, p ^ j) for p in range(size)])


def sum_chunks(sizes, mine, theirs, answers):
    outer, inner, chip, _ = sizes
    chunks = [None] * outer
    for k in range(outer - 1, -1, -1):
        slow, fast = ("inner", "chip") if k % 2 else ("chip", "inner")
        low = sizes[AXES.index(fast)]
        arrived = across(sizes, "core", theirs[k], 1)
        part = mine[k][:low] + arrived[:low]
        for j in range(1, sizes[AXES.index(slow)]):
            here = slice(j * low, (j + 1) * low)
            part = part + across(sizes, slow, mine[k][here] + arrived[here], j)
        chunks[k] = part[0]
        for j in range(1, low):
            chunks[k] = chunks[k] + across(sizes, fast, part[j], j)
    chunks, answers = lax.optimization_barrier((chunks, answers))
    total = chunks[0]
    for k in range(outer - 1, 0, -1):
        total = total + along(sizes, chunks[k], k)
    return total, answers


def per_device(
    sizes, codebook, weight_in, bias_in, weight_out, bias_out, latents, cotangent, code_owner, code_row
):
    outer, inner, chip, core = sizes
    devices = outer * inner * chip * core
    rows, dim_in = codebook.shape
    hidden_size = weight_in.shape[1]
    count, width = latents.shape
    capacity = max(2, 2 * count // devices)

    outgoing, slots = route(devices, capacity, code_owner, code_row, latents, cotangent)
    outgoing, bias_in = lax.optimization_barrier((outgoing, bias_in))
    incoming = lax.all_to_all(outgoing, AXES, split_axis=0, concat_axis=0, tiled=True)

    hidden_t, codebook_t, slope, projected, parts = forward(
        codebook, weight_in, bias_in, weight_out, bias_out
    )
    pieces = backward(
        sizes, capacity, incoming, hidden_t, slope, projected, codebook_t, weight_out.T
    )
    mine, theirs = list(pieces[:outer]), list(pieces[outer:])
    theirs[0], incoming = lax.optimization_barrier((theirs[0], incoming))
    picked = pick_rows(capacity, incoming, parts)
    answers = lax.all_to_all(picked, AXES, split_axis=0, concat_axis=0, tiled=True)

    total, answers = sum_chunks(sizes, mine, theirs, answers)
    total = lax.all_gather(total[None], AXES, axis=0, tiled=True)
    gw_in, gw_out, biases = assemble(outer, total, dim_in, hidden_size, width)

    slot_ids = jnp.arange(devices * capacity, dtype=jnp.int32)
    from_slot = slots.reshape(-1, 1) == slot_ids[None, :]
    chosen = pick(from_slot.astype(jnp.bfloat16), answers.reshape(-1, width))
    latent_grad = cotangent - 0.25 * (chosen - latents)
    biases = biases.reshape(-1)
    gb_in, gb_out = biases[:hidden_size], biases[hidden_size : hidden_size + width]
    return (latent_grad, gw_in, gb_in, gw_out, gb_out)


def solution(mesh):
    code, data = mesh.shape["code"], mesh.shape["dp"]
    core = 2
    outer = 1
    while outer * outer < code:
        outer *= 2
    sizes = (outer, code // outer, data // core, core)
    fine = Mesh(mesh.devices.reshape(sizes), AXES)
    rows = P(AXES, None)
    return jax.shard_map(
        functools.partial(per_device, sizes),
        mesh=fine,
        in_specs=(rows, P(), P(), P(), P(), rows, rows, rows, P(AXES)),
        out_specs=(rows, P(), P(), P(), P()),
        check_vma=False,
    )
```

```python
import functools

import jax
import jax.numpy as jnp
from jax import lax
from jax.experimental import pallas as pl
from jax.experimental.pallas import tpu as pltpu
from jax.sharding import Mesh, PartitionSpec as P

scale_gelu = 0.7978845608028654
cubic_term = 0.044715
LANES = 128
EXTRA = 8
AXES = ("outer", "inner", "chip", "core")


def gelu_parts(x):
    tangent = jnp.tanh(scale_gelu * (x + cubic_term * x * x * x))
    value = 0.5 * x * (1.0 + tangent)
    slope = 0.5 * (1.0 + tangent) + 0.5 * x * (1.0 - tangent * tangent) * scale_gelu * (
        1.0 + 3.0 * cubic_term * x * x
    )
    return value, slope


def split_two(x):
    high = lax.reduce_precision(x, 8, 7)
    low = (x - high).astype(jnp.bfloat16)
    return jnp.concatenate([high.astype(jnp.bfloat16), low], axis=1)


def pick(chooser, rows):
    width = rows.shape[1]
    both = jnp.dot(chooser, split_two(rows), preferred_element_type=jnp.float32)
    return both[:, :width] + both[:, width:]


def dot(a, b):
    return jnp.dot(a, b, preferred_element_type=jnp.float32)


def forward_kernel(codebook_ref, weight_in_ref, bias_in_ref, weight_out_ref, bias_out_ref,
                   hidden_ref, codebook_t_ref, slope_ref, projected_ref, parts_ref):
    width = projected_ref.shape[1]
    codebook = codebook_ref[...]
    codebook_t_ref[...] = jnp.transpose(codebook.astype(jnp.float32)).astype(jnp.bfloat16)
    hidden, slope = gelu_parts(dot(codebook, weight_in_ref[...]) + bias_in_ref[...])
    slope_ref[...] = slope
    hidden_ref[...] = jnp.transpose(hidden).astype(jnp.bfloat16)
    projected = dot(hidden.astype(jnp.bfloat16), weight_out_ref[...]) + bias_out_ref[...]
    projected_ref[...] = projected
    high = projected.astype(jnp.bfloat16)
    parts_ref[:, :width] = high
    parts_ref[:, width:] = (projected - high.astype(jnp.float32)).astype(jnp.bfloat16)


def forward(codebook, weight_in, bias_in, weight_out, bias_out):
    rows, dim_in = codebook.shape
    hidden_size, width = weight_out.shape
    tile = min(256, rows)
    whole = lambda *shape: pl.BlockSpec(shape, lambda i: (0, 0))
    return pl.pallas_call(
        forward_kernel,
        grid=(rows // tile,),
        in_specs=[
            pl.BlockSpec((tile, dim_in), lambda i: (i, 0)),
            whole(dim_in, hidden_size),
            whole(1, hidden_size),
            whole(hidden_size, width),
            whole(1, width),
        ],
        out_specs=[
            pl.BlockSpec((hidden_size, tile), lambda i: (0, i)),
            pl.BlockSpec((dim_in, tile), lambda i: (0, i)),
            pl.BlockSpec((tile, hidden_size), lambda i: (i, 0)),
            pl.BlockSpec((tile, width), lambda i: (i, 0)),
            pl.BlockSpec((tile, 2 * width), lambda i: (i, 0)),
        ],
        out_shape=[
            jax.ShapeDtypeStruct((hidden_size, rows), jnp.bfloat16),
            jax.ShapeDtypeStruct((dim_in, rows), jnp.bfloat16),
            jax.ShapeDtypeStruct((rows, hidden_size), jnp.float32),
            jax.ShapeDtypeStruct((rows, width), jnp.float32),
            jax.ShapeDtypeStruct((rows, 2 * width), jnp.bfloat16),
        ],
        cost_estimate=pl.CostEstimate(
            flops=2 * rows * hidden_size * (dim_in + width),
            bytes_accessed=14 * rows * hidden_size,
            transcendentals=rows * hidden_size,
        ),
        compiler_params=pltpu.CompilerParams(vmem_limit_bytes=60 * 2**20),
        name="forward",
    )(codebook, weight_in, bias_in.reshape(1, -1), weight_out, bias_out.reshape(1, -1))


def pick_kernel(capacity, incoming_hbm, parts_hbm, out_ref, wanted_ref, asked_ref, parts_ref, sems):
    devices = asked_ref.shape[0]
    rows, both = parts_ref.shape
    width = both // 2
    step = pl.program_id(0)
    per_row = LANES // capacity

    @pl.when(step == 0)
    def _():
        payload = incoming_hbm.shape[1] - EXTRA
        load = pltpu.make_async_copy(
            incoming_hbm.at[pl.ds(0, devices), pl.ds(payload, EXTRA)], asked_ref, sems.at[0]
        )
        load.start()
        more = pltpu.make_async_copy(parts_hbm, parts_ref, sems.at[1])
        more.start()
        load.wait()
        for t in range(devices // per_row):
            row = asked_ref[t * per_row]
            for k in range(1, per_row):
                row = jnp.maximum(row, pltpu.roll(asked_ref[t * per_row + k], k * capacity, 1))
            wanted_ref[:, t * LANES : (t + 1) * LANES] = row
        more.wait()

    tile = out_ref.shape[0] * capacity
    lane = lax.broadcasted_iota(jnp.int32, (LANES, LANES), 1).astype(jnp.float32)
    choosers = []
    for start in range(0, tile, LANES):
        at = pl.ds(pl.multiple_of(step * tile + start, LANES), LANES)
        column = jnp.transpose(jnp.broadcast_to(wanted_ref[0:1, at], (LANES, LANES)))
        choosers.append(jnp.concatenate(
            [
                (column == lane + float(r)).astype(jnp.float32).astype(jnp.bfloat16)
                for r in range(0, rows, LANES)
            ],
            axis=1,
        ))
    value = dot(jnp.concatenate(choosers, axis=0), parts_ref[...])
    value = value[:, :width] + value[:, width:]
    for k in range(out_ref.shape[0]):
        out_ref[k] = value[k * capacity : (k + 1) * capacity]


def pick_rows(capacity, incoming, parts):
    devices = incoming.shape[0]
    rows, both = parts.shape
    steps = 4
    return pl.pallas_call(
        functools.partial(pick_kernel, capacity),
        grid=(steps,),
        in_specs=[pl.BlockSpec(memory_space=pl.ANY)] * 2,
        out_specs=[
            pl.BlockSpec((devices // steps, capacity, both // 2), lambda i: (i, 0, 0)),
            pl.BlockSpec((EXTRA, devices * capacity), lambda i: (0, 0)),
        ],
        out_shape=[
            jax.ShapeDtypeStruct((devices, capacity, both // 2), jnp.float32),
            jax.ShapeDtypeStruct((EXTRA, devices * capacity), jnp.float32),
        ],
        scratch_shapes=[
            pltpu.VMEM((devices, EXTRA, LANES), jnp.float32),
            pltpu.VMEM((rows, both), jnp.bfloat16),
            pltpu.SemaphoreType.DMA((2,)),
        ],
        cost_estimate=pl.CostEstimate(
            flops=2 * devices * capacity * rows * both,
            bytes_accessed=4 * devices * capacity * both,
            transcendentals=0,
        ),
        compiler_params=pltpu.CompilerParams(vmem_limit_bytes=60 * 2**20),
        name="pick_rows",
    )(incoming, parts)


def route_kernel(devices, capacity, owner_hbm, row_hbm, latents_hbm, cotangent_hbm,
                 out_ref, slot_ref, owner_ref, row_ref, latents_ref, cotangent_ref, parts_ref, sems):
    count, width = latents_ref.shape
    step = pl.program_id(0)
    tile = out_ref.shape[0] * capacity

    @pl.when(step == 0)
    def _():
        loads = [
            pltpu.make_async_copy(a, b, sems.at[k])
            for k, (a, b) in enumerate((
                (owner_hbm, owner_ref), (row_hbm, row_ref),
                (latents_hbm, latents_ref), (cotangent_hbm, cotangent_ref),
            ))
        ]
        for load in loads:
            load.start()
        before = (
            lax.broadcasted_iota(jnp.int32, (LANES, LANES), 0)
            < lax.broadcasted_iota(jnp.int32, (LANES, LANES), 1)
        ).astype(jnp.bfloat16)
        owner_ids = lax.broadcasted_iota(jnp.int32, (devices, LANES), 0)
        lane = lax.broadcasted_iota(jnp.int32, (LANES, LANES), 1)
        seen = jnp.zeros((devices, 1), jnp.float32)
        loads[0].wait()
        loads[1].wait()
        for start in range(0, count, LANES):
            part = pl.ds(start, LANES)
            owners = owner_ref[:, part]
            mine = (owner_ids == owners).astype(jnp.float32)
            ranks = dot(mine.astype(jnp.bfloat16), before) + seen
            rank = jnp.sum(mine * ranks, axis=0, keepdims=True)
            seen = seen + jnp.sum(mine, axis=1, keepdims=True)
            slot_ref[:, part] = owners * capacity + rank.astype(jnp.int32)
            rows = jnp.transpose(
                jnp.broadcast_to(row_ref[:, part].astype(jnp.float32), (LANES, LANES))
            )
            tall = jnp.floor(rows * (1.0 / 32.0))
            extra = jnp.where(lane == 0, tall, jnp.where(lane == 1, rows - 32.0 * tall, 0.0))
            extra = jnp.where(lane == 2, 1.0, extra)
            parts_ref[part, 2 * width :] = extra.astype(jnp.bfloat16)
        loads[2].wait()
        loads[3].wait()
        for start in range(0, count, LANES):
            part = pl.ds(start, LANES)
            value = cotangent_ref[part, :] - latents_ref[part, :]
            high = value.astype(jnp.bfloat16)
            parts_ref[part, :width] = high
            parts_ref[part, width : 2 * width] = (value - high.astype(jnp.float32)).astype(
                jnp.bfloat16
            )

    ids = lax.broadcasted_iota(jnp.int32, (tile, count), 0) + step * tile
    chooser = (ids == slot_ref[...]).astype(jnp.float32).astype(jnp.bfloat16)
    both = dot(chooser, parts_ref[...])
    value = both[:, :width] + both[:, width : 2 * width]
    turned = jnp.transpose(both[:, 2 * width :])
    wanted = 32.0 * turned[0:1] + turned[1:2] + turned[2:3] - 1.0
    lane = lax.broadcasted_iota(jnp.int32, (EXTRA, LANES), 1)
    for k in range(out_ref.shape[0]):
        own = slice(k * capacity, (k + 1) * capacity)
        for j in range(width // LANES):
            out_ref[k, j * capacity : (j + 1) * capacity, :] = value[own, j * LANES : (j + 1) * LANES]
        at = k * capacity // LANES * LANES
        row = jnp.broadcast_to(wanted[:, at : at + LANES], (EXTRA, LANES))
        shift = k * capacity - at
        if shift:
            row = pltpu.roll(row, LANES - shift, 1)
        out_ref[k, width // LANES * capacity :, :] = jnp.where(lane < capacity, row, -1.0)


def route(devices, capacity, code_owner, code_row, latents, cotangent):
    count, width = latents.shape
    per_step = max(1, 512 // capacity)
    block = width // LANES * capacity + EXTRA
    whole = lambda *shape: pl.BlockSpec(shape, lambda i: (0,) * len(shape))
    return pl.pallas_call(
        functools.partial(route_kernel, devices, capacity),
        grid=(devices // per_step,),
        in_specs=[pl.BlockSpec(memory_space=pl.ANY)] * 4,
        out_specs=[
            pl.BlockSpec((per_step, block, LANES), lambda i: (i, 0, 0)),
            whole(1, count),
        ],
        out_shape=[
            jax.ShapeDtypeStruct((devices, block, LANES), jnp.float32),
            jax.ShapeDtypeStruct((1, count), jnp.int32),
        ],
        scratch_shapes=[
            pltpu.VMEM((1, count), jnp.int32),
            pltpu.VMEM((1, count), jnp.int32),
            pltpu.VMEM((count, width), jnp.float32),
            pltpu.VMEM((count, width), jnp.float32),
            pltpu.VMEM((count, 2 * width + LANES), jnp.bfloat16),
            pltpu.SemaphoreType.DMA((4,)),
        ],
        compiler_params=pltpu.CompilerParams(vmem_limit_bytes=60 * 2**20),
        name="route",
    )(code_owner.reshape(1, count), code_row.reshape(1, count), latents, cotangent)


def place(sizes, k, j):
    _, inner, chip, _ = sizes
    if k % 2:
        return j
    return j % inner * chip + j // inner


def backward_kernel(sizes, capacity, incoming_hbm, wanted_hbm, hidden_hbm, slope_hbm, projected_hbm,
                    codebook_hbm, weight_hbm, *refs):
    outer, inner, chip, core = sizes
    devices = outer * inner * chip * core
    mine_hbm, theirs_hbm, refs = refs[:outer], refs[outer : 2 * outer], refs[2 * outer :]
    (incoming, wanted, hidden, slope, projected, codebook, weight, parts, low, grad, flat,
     in_sem, out_sem) = refs
    width = projected.shape[1]
    dim_in, rows = codebook.shape
    hidden_size = hidden.shape[0]
    length = flat.shape[2] - EXTRA
    pairs = list(zip(
        (wanted_hbm, projected_hbm, weight_hbm, slope_hbm, hidden_hbm, codebook_hbm),
        (wanted, projected, weight, slope, hidden, codebook),
    ))
    loads = [pltpu.make_async_copy(a, b, in_sem.at[k]) for k, (a, b) in enumerate(pairs)]
    loads[0].start()
    blocks = width // LANES
    quarter = devices // 4
    arrivals = []
    for n in range(4):
        part = pl.ds(n * quarter, quarter)
        arrivals.append(pltpu.make_async_copy(
            incoming_hbm.at[part, pl.ds(0, blocks * capacity)], incoming.at[part], in_sem.at[6 + n]
        ))
        arrivals[n].start()
    for load in loads[1:]:
        load.start()
    for n in range(4):
        arrivals[n].wait()
        for s in range(n * quarter, (n + 1) * quarter):
            own = pl.ds(s * capacity, capacity)
            for j in range(blocks):
                value = incoming[s, j * capacity : (j + 1) * capacity, :]
                high = value.astype(jnp.bfloat16)
                parts[own, j * LANES : (j + 1) * LANES] = high
                parts[own, width + j * LANES : width + (j + 1) * LANES] = (
                    value - high.astype(jnp.float32)
                ).astype(jnp.bfloat16)
    for load in loads[:4]:
        load.wait()
    tile = min(512, rows)
    bias_in = jnp.zeros((1, hidden_size), jnp.float32)
    bias_out = jnp.zeros((1, width), jnp.float32)
    for start in range(0, rows, tile):
        part = pl.ds(start, tile)
        ids = (lax.broadcasted_iota(jnp.int32, (tile, wanted.shape[1]), 0) + start).astype(
            jnp.float32
        )
        chooser = (ids == wanted[0:1, :]).astype(jnp.float32)
        times = jnp.sum(chooser, axis=1, keepdims=True)
        both = dot(chooser.astype(jnp.bfloat16), parts[...])
        code_grad = both[:, :width] + both[:, width:] + times * projected[part, :]
        bias_out += jnp.sum(code_grad, axis=0, keepdims=True)
        code_low = code_grad.astype(jnp.bfloat16)
        low[part, :] = code_low
        preact_grad = (dot(code_low, weight[...]) * slope[part, :]).astype(jnp.bfloat16)
        grad[part, :] = preact_grad
        bias_in += jnp.sum(preact_grad.astype(jnp.float32), axis=0, keepdims=True)


    first = lax.axis_index("outer")
    plane = lax.axis_index("inner") * chip + lax.axis_index("chip")
    me = lax.axis_index("core")
    band = hidden_size // outer
    pieces = inner * chip
    home = lax.rem(outer - first, outer)
    for k in range(outer):
        for e in range(pieces * core):
            flat[k, e, length:, :] = jnp.zeros((EXTRA, LANES), jnp.float32)
    for e, bias in enumerate((bias_in, bias_out)):
        for j in range(bias.shape[1] // LANES):
            flat[home, e, length + j : length + j + 1, :] = bias[:, j * LANES : (j + 1) * LANES]

    loads[4].wait()
    loads[5].wait()
    stores = []
    for k in range(outer - 1, -1, -1):
        o = lax.rem(first + k, outer)
        here = pl.ds(pl.multiple_of(o * band, band), band)

        def keep(row, value):
            for r in range(0, value.shape[0], length):
                flat[k, (row + r) // length, :length, :] = value[r : r + length, :]

        out = dot(codebook[...], grad[:, here])
        for j in range(band // LANES):
            keep(j * dim_in, out[:, j * LANES : (j + 1) * LANES])
        out = dot(hidden[here, :], low[...])
        for j in range(blocks):
            keep(band // LANES * dim_in + j * band, out[:, j * LANES : (j + 1) * LANES])
        for target, c in ((theirs_hbm, 1 - me), (mine_hbm, me)):
            for j in range(pieces):
                e = lax.bitwise_xor(plane, place(sizes, k, j)) * core + c
                copy = pltpu.make_async_copy(
                    flat.at[k, e], target[k].at[j], out_sem.at[len(stores)]
                )
                copy.start()
                stores.append(copy)
    for copy in stores:
        copy.wait()


def backward(sizes, capacity, incoming, wanted, hidden_t, slope, projected, codebook_t, weight_t):
    devices = incoming.shape[0]
    rows, width = projected.shape
    dim_in, hidden_size = codebook_t.shape[0], hidden_t.shape[0]
    length = (dim_in + width) * hidden_size // LANES // devices
    outer, inner, chip, core = sizes
    piece = jax.ShapeDtypeStruct((inner * chip, length + EXTRA, LANES), jnp.float32)
    operands = (incoming, wanted, hidden_t, slope, projected, codebook_t, weight_t)
    vmem = lambda shape, dtype: pltpu.VMEM(shape, dtype)
    slots = devices * capacity
    return pl.pallas_call(
        functools.partial(backward_kernel, sizes, capacity),
        in_specs=[pl.BlockSpec(memory_space=pl.ANY)] * len(operands),
        out_specs=[pl.BlockSpec(memory_space=pl.ANY)] * (2 * outer),
        out_shape=[piece] * (2 * outer),
        scratch_shapes=[vmem((devices, incoming.shape[1] - EXTRA, LANES), jnp.float32)]
        + [vmem(a.shape, a.dtype) for a in operands[1:]]
        + [
            vmem((slots, 2 * width), jnp.bfloat16),
            vmem((rows, width), jnp.bfloat16),
            vmem((rows, hidden_size), jnp.bfloat16),
            vmem((outer, inner * chip * core, length + EXTRA, LANES), jnp.float32),
            pltpu.SemaphoreType.DMA((10,)),
            pltpu.SemaphoreType.DMA((devices,)),
        ],
        cost_estimate=pl.CostEstimate(
            flops=2 * rows * (slots * 2 * width + hidden_size * (2 * width + dim_in)),
            bytes_accessed=16 * rows * hidden_size,
            transcendentals=0,
        ),
        compiler_params=pltpu.CompilerParams(vmem_limit_bytes=60 * 2**20),
        name="backward",
    )(*operands)


def assemble_kernel(sizes, *refs):
    outer, inner, chip, core = sizes
    devices = outer * inner * chip * core
    pieces, refs = refs[:devices], refs[devices:]
    weight_in, weight_out, bias_in, bias_out, sems, bias_sem = refs
    length = pieces[0].shape[0] - EXTRA
    dim_in, hidden_size = weight_in.shape
    band = hidden_size // outer
    base = band // LANES * dim_in
    first = lax.axis_index("outer")
    plane = lax.axis_index("inner") * chip + lax.axis_index("chip")
    me = lax.axis_index("core")
    copies = []
    for n, piece in enumerate(pieces):
        c, n = divmod(n, devices // core)
        k, j = divmod(n, inner * chip)
        n += c * (devices // core)
        o = lax.rem(first + outer - k, outer)
        e = lax.bitwise_xor(plane, place(sizes, k, j)) * core + lax.bitwise_xor(me, c)
        at = e * length
        source = piece.at[pl.ds(0, length)]

        def copy_to(target, row, column):
            rows = pl.ds(pl.multiple_of(row, length), length)
            lanes = pl.ds(pl.multiple_of(column * LANES, LANES), LANES)
            return pltpu.make_async_copy(source, target.at[rows, lanes], sems.at[n])

        @pl.when(at < base)
        def _():
            column = o * (band // LANES) + lax.div(at, dim_in)
            copy_to(weight_in, lax.rem(at, dim_in), column).start()

        @pl.when(at >= base)
        def _():
            copy_to(weight_out, o * band + lax.rem(at - base, band), lax.div(at - base, band)).start()

        for row, bias in enumerate((bias_in, bias_out)):

            @pl.when((o == 0) & (e == row))
            def _():
                copy = pltpu.make_async_copy(
                    piece.at[pl.ds(length, EXTRA)], bias, bias_sem
                )
                copy.start()
                copy.wait()

        copies.append(copy_to(weight_in, 0, 0))
    for copy in copies:
        copy.wait()


def assemble(sizes, pieces, dim_in, hidden_size, width):
    hbm = pl.BlockSpec(memory_space=pl.ANY)
    return pl.pallas_call(
        functools.partial(assemble_kernel, sizes),
        in_specs=[hbm] * len(pieces),
        out_specs=[hbm] * 4,
        out_shape=[
            jax.ShapeDtypeStruct((dim_in, hidden_size), jnp.float32),
            jax.ShapeDtypeStruct((hidden_size, width), jnp.float32),
            jax.ShapeDtypeStruct((EXTRA, LANES), jnp.float32),
            jax.ShapeDtypeStruct((EXTRA, LANES), jnp.float32),
        ],
        scratch_shapes=[
            pltpu.SemaphoreType.DMA((len(pieces),)),
            pltpu.SemaphoreType.DMA,
        ],
        compiler_params=pltpu.CompilerParams(vmem_limit_bytes=4 * 2**20),
        name="assemble",
    )(*pieces)


def along(sizes, x, k):
    outer = sizes[0]
    return lax.ppermute(x, "outer", [(o, (o + k) % outer) for o in range(outer)])


def across(sizes, axis, x, j):
    size = sizes[AXES.index(axis)]
    return lax.ppermute(x, axis, [(p, p ^ j) for p in range(size)])


def sum_chunks(sizes, mine, theirs):
    outer, inner, chip, _ = sizes
    chunks = [None] * outer
    for k in range(outer - 1, -1, -1):
        slow, fast = ("inner", "chip") if k % 2 else ("chip", "inner")
        low = sizes[AXES.index(fast)]
        arrived = across(sizes, "core", theirs[k], 1)
        part = mine[k][:low] + arrived[:low]
        for j in range(1, sizes[AXES.index(slow)]):
            here = slice(j * low, (j + 1) * low)
            part = part + across(sizes, slow, mine[k][here] + arrived[here], j)
        chunks[k] = part[0]
        for j in range(1, low):
            chunks[k] = chunks[k] + across(sizes, fast, part[j], j)
    total = chunks[0]
    for k in range(outer - 1, 0, -1):
        total = total + along(sizes, chunks[k], k)
    return total


def spread_chunks(sizes, total):
    outer, inner, chip, _ = sizes
    near = []
    for k in range(outer):
        slow, fast = ("inner", "chip") if k % 2 else ("chip", "inner")
        x = along(sizes, total, k) if k else total
        row = [across(sizes, fast, x, j) if j else x for j in range(sizes[AXES.index(fast)])]
        for j in range(sizes[AXES.index(slow)]):
            near += [across(sizes, slow, x, j) if j else x for x in row]
    return near


def per_device(
    sizes, codebook, weight_in, bias_in, weight_out, bias_out, latents, cotangent, code_owner, code_row
):
    outer, inner, chip, core = sizes
    devices = outer * inner * chip * core
    rows, dim_in = codebook.shape
    hidden_size = weight_in.shape[1]
    count, width = latents.shape
    capacity = max(2, 2 * count // devices)

    outgoing, slots = route(devices, capacity, code_owner, code_row, latents, cotangent)
    outgoing, bias_in = lax.optimization_barrier((outgoing, bias_in))
    incoming = lax.all_to_all(outgoing, AXES, split_axis=0, concat_axis=0, tiled=True)

    hidden_t, codebook_t, slope, projected, parts = forward(
        codebook, weight_in, bias_in, weight_out, bias_out
    )
    picked, wanted = pick_rows(capacity, incoming, parts)
    answers = lax.all_to_all(picked, AXES, split_axis=0, concat_axis=0, tiled=True)

    weight_t = weight_out.T

    def reduce_half(*operands):
        pieces = backward(sizes, capacity, *operands)
        return sum_chunks(sizes, list(pieces[:outer]), list(pieces[outer:]))

    def nothing(*operands):
        length = (dim_in + width) * hidden_size // LANES // devices
        return jnp.zeros((length + EXTRA, LANES), jnp.float32)

    total = lax.cond(
        code_row[0] >= 0, reduce_half, nothing,
        incoming, wanted, hidden_t, slope, projected, codebook_t, weight_t,
    )
    total, answers = lax.optimization_barrier((total, answers))
    answers = answers.reshape(-1, width)
    near = spread_chunks(sizes, total)

    slot_ids = jnp.arange(devices * capacity, dtype=jnp.int32)
    from_slot = slots.reshape(-1, 1) == slot_ids[None, :]
    chosen = pick(from_slot.astype(jnp.bfloat16), answers)
    latent_grad = cotangent - 0.25 * (chosen - latents)
    late = len(near) - inner * chip
    near[late], latent_grad = lax.optimization_barrier((near[late], latent_grad))

    chunks = near + [across(sizes, "core", x, 1) for x in near]
    gw_in, gw_out, gb_in, gb_out = assemble(sizes, chunks, dim_in, hidden_size, width)
    gb_in, gb_out = gb_in.reshape(-1)[:hidden_size], gb_out.reshape(-1)[:width]
    return (latent_grad, gw_in, gb_in, gw_out, gb_out)


def solution(mesh):
    code, data = mesh.shape["code"], mesh.shape["dp"]
    core = 2
    outer = 1
    while outer * outer < code:
        outer *= 2
    sizes = (outer, code // outer, data // core, core)
    fine = Mesh(mesh.devices.reshape(sizes), AXES)
    rows = P(AXES, None)
    return jax.shard_map(
        functools.partial(per_device, sizes),
        mesh=fine,
        in_specs=(rows, P(), P(), P(), P(), rows, rows, rows, P(AXES)),
        out_specs=(rows, P(), P(), P(), P()),
        check_vma=False,
    )
```

```python
import functools

import jax
import jax.numpy as jnp
from jax import lax
from jax.experimental import pallas as pl
from jax.experimental.pallas import tpu as pltpu
from jax.sharding import Mesh, PartitionSpec as P

scale_gelu = 0.7978845608028654
cubic_term = 0.044715
LANES = 128
EXTRA = 8
AXES = ("outer", "inner", "chip", "core")


def gelu_parts(x):
    tangent = jnp.tanh(scale_gelu * (x + cubic_term * x * x * x))
    value = 0.5 * x * (1.0 + tangent)
    slope = 0.5 * (1.0 + tangent) + 0.5 * x * (1.0 - tangent * tangent) * scale_gelu * (
        1.0 + 3.0 * cubic_term * x * x
    )
    return value, slope


def split_two(x):
    high = lax.reduce_precision(x, 8, 7)
    low = (x - high).astype(jnp.bfloat16)
    return jnp.concatenate([high.astype(jnp.bfloat16), low], axis=1)


def pick(chooser, rows):
    width = rows.shape[1]
    both = jnp.dot(chooser, split_two(rows), preferred_element_type=jnp.float32)
    return both[:, :width] + both[:, width:]


def dot(a, b):
    return jnp.dot(a, b, preferred_element_type=jnp.float32)


def forward_kernel(codebook_ref, weight_in_ref, bias_in_ref, weight_out_ref, bias_out_ref,
                   hidden_ref, codebook_t_ref, slope_ref, projected_ref, parts_ref):
    width = projected_ref.shape[1]
    codebook = codebook_ref[...]
    codebook_t_ref[...] = jnp.transpose(codebook.astype(jnp.float32)).astype(jnp.bfloat16)
    hidden, slope = gelu_parts(dot(codebook, weight_in_ref[...]) + bias_in_ref[...])
    slope_ref[...] = slope
    hidden_ref[...] = jnp.transpose(hidden).astype(jnp.bfloat16)
    projected = dot(hidden.astype(jnp.bfloat16), weight_out_ref[...]) + bias_out_ref[...]
    projected_ref[...] = projected
    high = projected.astype(jnp.bfloat16)
    parts_ref[:, :width] = high
    parts_ref[:, width:] = (projected - high.astype(jnp.float32)).astype(jnp.bfloat16)


def forward(codebook, weight_in, bias_in, weight_out, bias_out):
    rows, dim_in = codebook.shape
    hidden_size, width = weight_out.shape
    tile = min(256, rows)
    whole = lambda *shape: pl.BlockSpec(shape, lambda i: (0, 0))
    return pl.pallas_call(
        forward_kernel,
        grid=(rows // tile,),
        in_specs=[
            pl.BlockSpec((tile, dim_in), lambda i: (i, 0)),
            whole(dim_in, hidden_size),
            whole(1, hidden_size),
            whole(hidden_size, width),
            whole(1, width),
        ],
        out_specs=[
            pl.BlockSpec((hidden_size, tile), lambda i: (0, i)),
            pl.BlockSpec((dim_in, tile), lambda i: (0, i)),
            pl.BlockSpec((tile, hidden_size), lambda i: (i, 0)),
            pl.BlockSpec((tile, width), lambda i: (i, 0)),
            pl.BlockSpec((tile, 2 * width), lambda i: (i, 0)),
        ],
        out_shape=[
            jax.ShapeDtypeStruct((hidden_size, rows), jnp.bfloat16),
            jax.ShapeDtypeStruct((dim_in, rows), jnp.bfloat16),
            jax.ShapeDtypeStruct((rows, hidden_size), jnp.float32),
            jax.ShapeDtypeStruct((rows, width), jnp.float32),
            jax.ShapeDtypeStruct((rows, 2 * width), jnp.bfloat16),
        ],
        cost_estimate=pl.CostEstimate(
            flops=2 * rows * hidden_size * (dim_in + width),
            bytes_accessed=14 * rows * hidden_size,
            transcendentals=rows * hidden_size,
        ),
        compiler_params=pltpu.CompilerParams(vmem_limit_bytes=60 * 2**20),
        name="forward",
    )(codebook, weight_in, bias_in.reshape(1, -1), weight_out, bias_out.reshape(1, -1))


def pick_kernel(capacity, asked_hbm, parts_hbm, out_ref, wanted_ref, asked_ref, parts_ref, sems):
    devices = asked_ref.shape[0]
    rows, both = parts_ref.shape
    width = both // 2
    step = pl.program_id(0)
    per_row = LANES // capacity

    @pl.when(step == 0)
    def _():
        load = pltpu.make_async_copy(asked_hbm, asked_ref, sems.at[0])
        load.start()
        more = pltpu.make_async_copy(parts_hbm, parts_ref, sems.at[1])
        more.start()
        load.wait()
        for t in range(devices // per_row):
            row = asked_ref[t * per_row]
            for k in range(1, per_row):
                row = jnp.maximum(row, pltpu.roll(asked_ref[t * per_row + k], k * capacity, 1))
            wanted_ref[:, t * LANES : (t + 1) * LANES] = row
        more.wait()

    tile = out_ref.shape[0] * capacity
    lane = lax.broadcasted_iota(jnp.int32, (LANES, LANES), 1).astype(jnp.float32)
    choosers = []
    for start in range(0, tile, LANES):
        at = pl.ds(pl.multiple_of(step * tile + start, LANES), LANES)
        column = jnp.transpose(jnp.broadcast_to(wanted_ref[0:1, at], (LANES, LANES)))
        choosers.append(jnp.concatenate(
            [
                (column == lane + float(r)).astype(jnp.float32).astype(jnp.bfloat16)
                for r in range(0, rows, LANES)
            ],
            axis=1,
        ))
    value = dot(jnp.concatenate(choosers, axis=0), parts_ref[...])
    value = value[:, :width] + value[:, width:]
    for k in range(out_ref.shape[0]):
        out_ref[k] = value[k * capacity : (k + 1) * capacity]


def pick_rows(capacity, asked, parts):
    devices = asked.shape[0]
    rows, both = parts.shape
    steps = 4
    return pl.pallas_call(
        functools.partial(pick_kernel, capacity),
        grid=(steps,),
        in_specs=[pl.BlockSpec(memory_space=pl.ANY)] * 2,
        out_specs=[
            pl.BlockSpec((devices // steps, capacity, both // 2), lambda i: (i, 0, 0)),
            pl.BlockSpec((EXTRA, devices * capacity), lambda i: (0, 0)),
        ],
        out_shape=[
            jax.ShapeDtypeStruct((devices, capacity, both // 2), jnp.float32),
            jax.ShapeDtypeStruct((EXTRA, devices * capacity), jnp.float32),
        ],
        scratch_shapes=[
            pltpu.VMEM((devices, EXTRA, LANES), jnp.float32),
            pltpu.VMEM((rows, both), jnp.bfloat16),
            pltpu.SemaphoreType.DMA((2,)),
        ],
        cost_estimate=pl.CostEstimate(
            flops=2 * devices * capacity * rows * both,
            bytes_accessed=4 * devices * capacity * both,
            transcendentals=0,
        ),
        compiler_params=pltpu.CompilerParams(vmem_limit_bytes=60 * 2**20),
        name="pick_rows",
    )(asked, parts)


def route_kernel(devices, capacity, owner_hbm, row_hbm, latents_hbm, cotangent_hbm,
                 out_ref, asked_ref, slot_ref, owner_ref, row_ref, latents_ref, cotangent_ref, parts_ref,
                 sems):
    count, width = latents_ref.shape
    step = pl.program_id(0)
    tile = out_ref.shape[0] * capacity

    @pl.when(step == 0)
    def _():
        loads = [
            pltpu.make_async_copy(a, b, sems.at[k])
            for k, (a, b) in enumerate((
                (owner_hbm, owner_ref), (row_hbm, row_ref),
                (latents_hbm, latents_ref), (cotangent_hbm, cotangent_ref),
            ))
        ]
        for load in loads:
            load.start()
        before = (
            lax.broadcasted_iota(jnp.int32, (LANES, LANES), 0)
            < lax.broadcasted_iota(jnp.int32, (LANES, LANES), 1)
        ).astype(jnp.bfloat16)
        owner_ids = lax.broadcasted_iota(jnp.int32, (devices, LANES), 0)
        lane = lax.broadcasted_iota(jnp.int32, (LANES, LANES), 1)
        seen = jnp.zeros((devices, 1), jnp.float32)
        loads[0].wait()
        loads[1].wait()
        for start in range(0, count, LANES):
            part = pl.ds(start, LANES)
            owners = owner_ref[:, part]
            mine = (owner_ids == owners).astype(jnp.float32)
            ranks = dot(mine.astype(jnp.bfloat16), before) + seen
            rank = jnp.sum(mine * ranks, axis=0, keepdims=True)
            seen = seen + jnp.sum(mine, axis=1, keepdims=True)
            slot_ref[:, part] = owners * capacity + rank.astype(jnp.int32)
            rows = jnp.transpose(
                jnp.broadcast_to(row_ref[:, part].astype(jnp.float32), (LANES, LANES))
            )
            tall = jnp.floor(rows * (1.0 / 32.0))
            extra = jnp.where(lane == 0, tall, jnp.where(lane == 1, rows - 32.0 * tall, 0.0))
            extra = jnp.where(lane == 2, 1.0, extra)
            parts_ref[part, 2 * width :] = extra.astype(jnp.bfloat16)
        loads[2].wait()
        loads[3].wait()
        for start in range(0, count, LANES):
            part = pl.ds(start, LANES)
            value = cotangent_ref[part, :] - latents_ref[part, :]
            high = value.astype(jnp.bfloat16)
            parts_ref[part, :width] = high
            parts_ref[part, width : 2 * width] = (value - high.astype(jnp.float32)).astype(
                jnp.bfloat16
            )

    ids = lax.broadcasted_iota(jnp.int32, (tile, count), 0) + step * tile
    chooser = (ids == slot_ref[...]).astype(jnp.float32).astype(jnp.bfloat16)
    both = dot(chooser, parts_ref[...])
    value = both[:, :width] + both[:, width : 2 * width]
    turned = jnp.transpose(both[:, 2 * width :])
    wanted = 32.0 * turned[0:1] + turned[1:2] + turned[2:3] - 1.0
    lane = lax.broadcasted_iota(jnp.int32, (EXTRA, LANES), 1)
    for k in range(out_ref.shape[0]):
        own = slice(k * capacity, (k + 1) * capacity)
        for j in range(width // LANES):
            out_ref[k, j * capacity : (j + 1) * capacity, :] = value[own, j * LANES : (j + 1) * LANES]
        at = k * capacity // LANES * LANES
        row = jnp.broadcast_to(wanted[:, at : at + LANES], (EXTRA, LANES))
        shift = k * capacity - at
        if shift:
            row = pltpu.roll(row, LANES - shift, 1)
        asked_ref[k] = jnp.where(lane < capacity, row, -1.0)


def route(devices, capacity, code_owner, code_row, latents, cotangent):
    count, width = latents.shape
    per_step = max(1, 512 // capacity)
    block = width // LANES * capacity
    whole = lambda *shape: pl.BlockSpec(shape, lambda i: (0,) * len(shape))
    return pl.pallas_call(
        functools.partial(route_kernel, devices, capacity),
        grid=(devices // per_step,),
        in_specs=[pl.BlockSpec(memory_space=pl.ANY)] * 4,
        out_specs=[
            pl.BlockSpec((per_step, block, LANES), lambda i: (i, 0, 0)),
            pl.BlockSpec((per_step, EXTRA, LANES), lambda i: (i, 0, 0)),
            whole(1, count),
        ],
        out_shape=[
            jax.ShapeDtypeStruct((devices, block, LANES), jnp.float32),
            jax.ShapeDtypeStruct((devices, EXTRA, LANES), jnp.float32),
            jax.ShapeDtypeStruct((1, count), jnp.int32),
        ],
        scratch_shapes=[
            pltpu.VMEM((1, count), jnp.int32),
            pltpu.VMEM((1, count), jnp.int32),
            pltpu.VMEM((count, width), jnp.float32),
            pltpu.VMEM((count, width), jnp.float32),
            pltpu.VMEM((count, 2 * width + LANES), jnp.bfloat16),
            pltpu.SemaphoreType.DMA((4,)),
        ],
        compiler_params=pltpu.CompilerParams(vmem_limit_bytes=60 * 2**20),
        name="route",
    )(code_owner.reshape(1, count), code_row.reshape(1, count), latents, cotangent)


def place(sizes, k, j):
    _, inner, chip, _ = sizes
    if k % 2:
        return j
    return j % inner * chip + j // inner


def backward_kernel(sizes, capacity, incoming_hbm, wanted_hbm, hidden_hbm, slope_hbm, projected_hbm,
                    codebook_hbm, weight_hbm, *refs):
    outer, inner, chip, core = sizes
    devices = outer * inner * chip * core
    mine_hbm, theirs_hbm, refs = refs[:outer], refs[outer : 2 * outer], refs[2 * outer :]
    (incoming, wanted, hidden, slope, projected, codebook, weight, parts, low, grad, flat,
     in_sem, out_sem) = refs
    width = projected.shape[1]
    dim_in, rows = codebook.shape
    hidden_size = hidden.shape[0]
    length = flat.shape[2] - EXTRA
    pairs = list(zip(
        (wanted_hbm, projected_hbm, weight_hbm, slope_hbm, hidden_hbm, codebook_hbm),
        (wanted, projected, weight, slope, hidden, codebook),
    ))
    loads = [pltpu.make_async_copy(a, b, in_sem.at[k]) for k, (a, b) in enumerate(pairs)]
    loads[0].start()
    blocks = width // LANES
    quarter = devices // 4
    arrivals = []
    for n in range(4):
        part = pl.ds(n * quarter, quarter)
        arrivals.append(pltpu.make_async_copy(
            incoming_hbm.at[part], incoming.at[part], in_sem.at[6 + n]
        ))
        arrivals[n].start()
    for load in loads[1:]:
        load.start()
    for n in range(4):
        arrivals[n].wait()
        for s in range(n * quarter, (n + 1) * quarter):
            own = pl.ds(s * capacity, capacity)
            for j in range(blocks):
                value = incoming[s, j * capacity : (j + 1) * capacity, :]
                high = value.astype(jnp.bfloat16)
                parts[own, j * LANES : (j + 1) * LANES] = high
                parts[own, width + j * LANES : width + (j + 1) * LANES] = (
                    value - high.astype(jnp.float32)
                ).astype(jnp.bfloat16)
    for load in loads[:4]:
        load.wait()
    tile = min(512, rows)
    bias_in = jnp.zeros((1, hidden_size), jnp.float32)
    bias_out = jnp.zeros((1, width), jnp.float32)
    for start in range(0, rows, tile):
        part = pl.ds(start, tile)
        ids = (lax.broadcasted_iota(jnp.int32, (tile, wanted.shape[1]), 0) + start).astype(
            jnp.float32
        )
        chooser = (ids == wanted[0:1, :]).astype(jnp.float32)
        times = jnp.sum(chooser, axis=1, keepdims=True)
        both = dot(chooser.astype(jnp.bfloat16), parts[...])
        code_grad = both[:, :width] + both[:, width:] + times * projected[part, :]
        bias_out += jnp.sum(code_grad, axis=0, keepdims=True)
        code_low = code_grad.astype(jnp.bfloat16)
        low[part, :] = code_low
        preact_grad = (dot(code_low, weight[...]) * slope[part, :]).astype(jnp.bfloat16)
        grad[part, :] = preact_grad
        bias_in += jnp.sum(preact_grad.astype(jnp.float32), axis=0, keepdims=True)


    first = lax.axis_index("outer")
    plane = lax.axis_index("inner") * chip + lax.axis_index("chip")
    me = lax.axis_index("core")
    band = hidden_size // outer
    pieces = inner * chip
    home = lax.rem(outer - first, outer)
    for k in range(outer):
        for e in range(pieces * core):
            flat[k, e, length:, :] = jnp.zeros((EXTRA, LANES), jnp.float32)
    for e, bias in enumerate((bias_in, bias_out)):
        for j in range(bias.shape[1] // LANES):
            flat[home, e, length + j : length + j + 1, :] = bias[:, j * LANES : (j + 1) * LANES]

    loads[4].wait()
    loads[5].wait()
    stores = []
    for k in range(outer - 1, -1, -1):
        o = lax.rem(first + k, outer)
        here = pl.ds(pl.multiple_of(o * band, band), band)

        def keep(row, value):
            for r in range(0, value.shape[0], length):
                flat[k, (row + r) // length, :length, :] = value[r : r + length, :]

        out = dot(codebook[...], grad[:, here])
        for j in range(band // LANES):
            keep(j * dim_in, out[:, j * LANES : (j + 1) * LANES])
        out = dot(hidden[here, :], low[...])
        for j in range(blocks):
            keep(band // LANES * dim_in + j * band, out[:, j * LANES : (j + 1) * LANES])
        for target, c in ((theirs_hbm, 1 - me), (mine_hbm, me)):
            for j in range(pieces):
                e = lax.bitwise_xor(plane, place(sizes, k, j)) * core + c
                copy = pltpu.make_async_copy(
                    flat.at[k, e], target[k].at[j], out_sem.at[len(stores)]
                )
                copy.start()
                stores.append(copy)
    for copy in stores:
        copy.wait()


def backward(sizes, capacity, incoming, wanted, hidden_t, slope, projected, codebook_t, weight_t):
    devices = incoming.shape[0]
    rows, width = projected.shape
    dim_in, hidden_size = codebook_t.shape[0], hidden_t.shape[0]
    length = (dim_in + width) * hidden_size // LANES // devices
    outer, inner, chip, core = sizes
    piece = jax.ShapeDtypeStruct((inner * chip, length + EXTRA, LANES), jnp.float32)
    operands = (incoming, wanted, hidden_t, slope, projected, codebook_t, weight_t)
    vmem = lambda shape, dtype: pltpu.VMEM(shape, dtype)
    slots = devices * capacity
    return pl.pallas_call(
        functools.partial(backward_kernel, sizes, capacity),
        in_specs=[pl.BlockSpec(memory_space=pl.ANY)] * len(operands),
        out_specs=[pl.BlockSpec(memory_space=pl.ANY)] * (2 * outer),
        out_shape=[piece] * (2 * outer),
        scratch_shapes=[vmem(a.shape, a.dtype) for a in operands]
        + [
            vmem((slots, 2 * width), jnp.bfloat16),
            vmem((rows, width), jnp.bfloat16),
            vmem((rows, hidden_size), jnp.bfloat16),
            vmem((outer, inner * chip * core, length + EXTRA, LANES), jnp.float32),
            pltpu.SemaphoreType.DMA((10,)),
            pltpu.SemaphoreType.DMA((devices,)),
        ],
        cost_estimate=pl.CostEstimate(
            flops=2 * rows * (slots * 2 * width + hidden_size * (2 * width + dim_in)),
            bytes_accessed=16 * rows * hidden_size,
            transcendentals=0,
        ),
        compiler_params=pltpu.CompilerParams(vmem_limit_bytes=60 * 2**20),
        name="backward",
    )(*operands)


def assemble_kernel(sizes, *refs):
    outer, inner, chip, core = sizes
    devices = outer * inner * chip * core
    pieces, refs = refs[:devices], refs[devices:]
    weight_in, weight_out, bias_in, bias_out, sems, bias_sem = refs
    length = pieces[0].shape[0] - EXTRA
    dim_in, hidden_size = weight_in.shape
    band = hidden_size // outer
    base = band // LANES * dim_in
    first = lax.axis_index("outer")
    plane = lax.axis_index("inner") * chip + lax.axis_index("chip")
    me = lax.axis_index("core")
    copies = []
    for n, piece in enumerate(pieces):
        c, n = divmod(n, devices // core)
        k, j = divmod(n, inner * chip)
        n += c * (devices // core)
        o = lax.rem(first + outer - k, outer)
        e = lax.bitwise_xor(plane, place(sizes, k, j)) * core + lax.bitwise_xor(me, c)
        at = e * length
        source = piece.at[pl.ds(0, length)]

        def copy_to(target, row, column):
            rows = pl.ds(pl.multiple_of(row, length), length)
            lanes = pl.ds(pl.multiple_of(column * LANES, LANES), LANES)
            return pltpu.make_async_copy(source, target.at[rows, lanes], sems.at[n])

        @pl.when(at < base)
        def _():
            column = o * (band // LANES) + lax.div(at, dim_in)
            copy_to(weight_in, lax.rem(at, dim_in), column).start()

        @pl.when(at >= base)
        def _():
            copy_to(weight_out, o * band + lax.rem(at - base, band), lax.div(at - base, band)).start()

        for row, bias in enumerate((bias_in, bias_out)):

            @pl.when((o == 0) & (e == row))
            def _():
                copy = pltpu.make_async_copy(
                    piece.at[pl.ds(length, EXTRA)], bias, bias_sem
                )
                copy.start()
                copy.wait()

        copies.append(copy_to(weight_in, 0, 0))
    for copy in copies:
        copy.wait()


def assemble(sizes, pieces, dim_in, hidden_size, width):
    hbm = pl.BlockSpec(memory_space=pl.ANY)
    return pl.pallas_call(
        functools.partial(assemble_kernel, sizes),
        in_specs=[hbm] * len(pieces),
        out_specs=[hbm] * 4,
        out_shape=[
            jax.ShapeDtypeStruct((dim_in, hidden_size), jnp.float32),
            jax.ShapeDtypeStruct((hidden_size, width), jnp.float32),
            jax.ShapeDtypeStruct((EXTRA, LANES), jnp.float32),
            jax.ShapeDtypeStruct((EXTRA, LANES), jnp.float32),
        ],
        scratch_shapes=[
            pltpu.SemaphoreType.DMA((len(pieces),)),
            pltpu.SemaphoreType.DMA,
        ],
        compiler_params=pltpu.CompilerParams(vmem_limit_bytes=4 * 2**20),
        name="assemble",
    )(*pieces)


def along(sizes, x, k):
    outer = sizes[0]
    return lax.ppermute(x, "outer", [(o, (o + k) % outer) for o in range(outer)])


def across(sizes, axis, x, j):
    size = sizes[AXES.index(axis)]
    return lax.ppermute(x, axis, [(p, p ^ j) for p in range(size)])


def sum_chunks(sizes, mine, theirs):
    outer, inner, chip, _ = sizes
    chunks = [None] * outer
    for k in range(outer - 1, -1, -1):
        slow, fast = ("inner", "chip") if k % 2 else ("chip", "inner")
        low = sizes[AXES.index(fast)]
        arrived = across(sizes, "core", theirs[k], 1)
        part = mine[k][:low] + arrived[:low]
        for j in range(1, sizes[AXES.index(slow)]):
            here = slice(j * low, (j + 1) * low)
            part = part + across(sizes, slow, mine[k][here] + arrived[here], j)
        chunks[k] = part[0]
        for j in range(1, low):
            chunks[k] = chunks[k] + across(sizes, fast, part[j], j)
    total = chunks[0]
    for k in range(outer - 1, 0, -1):
        total = total + along(sizes, chunks[k], k)
    return total


def spread_chunks(sizes, total):
    outer, inner, chip, _ = sizes
    near = []
    for k in range(outer):
        slow, fast = ("inner", "chip") if k % 2 else ("chip", "inner")
        x = along(sizes, total, k) if k else total
        row = [across(sizes, fast, x, j) if j else x for j in range(sizes[AXES.index(fast)])]
        for j in range(sizes[AXES.index(slow)]):
            near += [across(sizes, slow, x, j) if j else x for x in row]
    return near


def per_device(
    sizes, codebook, weight_in, bias_in, weight_out, bias_out, latents, cotangent, code_owner, code_row
):
    outer, inner, chip, core = sizes
    devices = outer * inner * chip * core
    rows, dim_in = codebook.shape
    hidden_size = weight_in.shape[1]
    count, width = latents.shape
    capacity = max(2, 2 * count // devices)

    outgoing, asked, slots = route(devices, capacity, code_owner, code_row, latents, cotangent)
    outgoing, bias_in = lax.optimization_barrier((outgoing, bias_in))
    incoming = lax.all_to_all(outgoing, AXES, split_axis=0, concat_axis=0, tiled=True)

    taken = code_row[0] >= 0

    def prepare(asked, *operands):
        asked = lax.all_to_all(asked, AXES, split_axis=0, concat_axis=0, tiled=True)
        hidden_t, codebook_t, slope, projected, parts = forward(*operands)
        picked, wanted = pick_rows(capacity, asked, parts)
        return picked, wanted, hidden_t, slope, projected, codebook_t, operands[3].T

    operands = (asked, codebook, weight_in, bias_in, weight_out, bias_out)
    picked, wanted, *states = lax.cond(
        taken, prepare,
        lambda *operands: jax.tree.map(
            lambda x: jnp.zeros(x.shape, x.dtype), jax.eval_shape(prepare, *operands)
        ),
        *operands,
    )
    answers = lax.all_to_all(picked, AXES, split_axis=0, concat_axis=0, tiled=True)

    def reduce_half(*operands):
        pieces = backward(sizes, capacity, *operands)
        return sum_chunks(sizes, list(pieces[:outer]), list(pieces[outer:]))

    def nothing(*operands):
        length = (dim_in + width) * hidden_size // LANES // devices
        return jnp.zeros((length + EXTRA, LANES), jnp.float32)

    total = lax.cond(taken, reduce_half, nothing, incoming, wanted, *states)
    total, answers = lax.optimization_barrier((total, answers))
    answers = answers.reshape(-1, width)
    near = spread_chunks(sizes, total)

    slot_ids = jnp.arange(devices * capacity, dtype=jnp.int32)
    from_slot = slots.reshape(-1, 1) == slot_ids[None, :]
    chosen = pick(from_slot.astype(jnp.bfloat16), answers)
    latent_grad = cotangent - 0.25 * (chosen - latents)
    late = len(near) - inner * chip
    near[late], latent_grad = lax.optimization_barrier((near[late], latent_grad))

    chunks = near + [across(sizes, "core", x, 1) for x in near]
    gw_in, gw_out, gb_in, gb_out = assemble(sizes, chunks, dim_in, hidden_size, width)
    gb_in, gb_out = gb_in.reshape(-1)[:hidden_size], gb_out.reshape(-1)[:width]
    return (latent_grad, gw_in, gb_in, gw_out, gb_out)


def solution(mesh):
    code, data = mesh.shape["code"], mesh.shape["dp"]
    core = 2
    outer = 1
    while outer * outer < code:
        outer *= 2
    sizes = (outer, code // outer, data // core, core)
    fine = Mesh(mesh.devices.reshape(sizes), AXES)
    rows = P(AXES, None)
    return jax.shard_map(
        functools.partial(per_device, sizes),
        mesh=fine,
        in_specs=(rows, P(), P(), P(), P(), rows, rows, rows, P(AXES)),
        out_specs=(rows, P(), P(), P(), P()),
        check_vma=False,
    )
```

```python
import functools
import math

import jax
import jax.numpy as jnp
from jax import lax
from jax.experimental import pallas as pl
from jax.experimental.pallas import tpu as pltpu
from jax.sharding import Mesh, PartitionSpec as P

scale_gelu = 0.7978845608028654
cubic_term = 0.044715
LANES = 128
EXTRA = 8
AXES = ("outer", "inner", "chip", "core")


def gelu_parts(x):
    tangent = jnp.tanh(scale_gelu * (x + cubic_term * x * x * x))
    value = 0.5 * x * (1.0 + tangent)
    slope = 0.5 * (1.0 + tangent) + 0.5 * x * (1.0 - tangent * tangent) * scale_gelu * (
        1.0 + 3.0 * cubic_term * x * x
    )
    return value, slope


def split_two(x):
    high = lax.reduce_precision(x, 8, 7)
    low = (x - high).astype(jnp.bfloat16)
    return jnp.concatenate([high.astype(jnp.bfloat16), low], axis=1)


def pick(chooser, rows):
    width = rows.shape[1]
    both = jnp.dot(chooser, split_two(rows), preferred_element_type=jnp.float32)
    return both[:, :width] + both[:, width:]


def dot(a, b):
    return jnp.dot(a, b, preferred_element_type=jnp.float32)


def forward_kernel(codebook_ref, weight_in_ref, bias_in_ref, weight_out_ref, bias_out_ref,
                   hidden_ref, codebook_t_ref, slope_ref, projected_ref, parts_ref):
    width = projected_ref.shape[1]
    codebook = codebook_ref[...]
    codebook_t_ref[...] = jnp.transpose(codebook.astype(jnp.float32)).astype(jnp.bfloat16)
    hidden, slope = gelu_parts(dot(codebook, weight_in_ref[...]) + bias_in_ref[...])
    slope_ref[...] = slope
    hidden_ref[...] = jnp.transpose(hidden).astype(jnp.bfloat16)
    projected = dot(hidden.astype(jnp.bfloat16), weight_out_ref[...]) + bias_out_ref[...]
    projected_ref[...] = projected
    high = projected.astype(jnp.bfloat16)
    parts_ref[:, :width] = high
    parts_ref[:, width:] = (projected - high.astype(jnp.float32)).astype(jnp.bfloat16)


def forward(codebook, weight_in, bias_in, weight_out, bias_out):
    rows, dim_in = codebook.shape
    hidden_size, width = weight_out.shape
    tile = min(256, rows)
    whole = lambda *shape: pl.BlockSpec(shape, lambda i: (0, 0))
    return pl.pallas_call(
        forward_kernel,
        grid=(rows // tile,),
        in_specs=[
            pl.BlockSpec((tile, dim_in), lambda i: (i, 0)),
            whole(dim_in, hidden_size),
            whole(1, hidden_size),
            whole(hidden_size, width),
            whole(1, width),
        ],
        out_specs=[
            pl.BlockSpec((hidden_size, tile), lambda i: (0, i)),
            pl.BlockSpec((dim_in, tile), lambda i: (0, i)),
            pl.BlockSpec((tile, hidden_size), lambda i: (i, 0)),
            pl.BlockSpec((tile, width), lambda i: (i, 0)),
            pl.BlockSpec((tile, 2 * width), lambda i: (i, 0)),
        ],
        out_shape=[
            jax.ShapeDtypeStruct((hidden_size, rows), jnp.bfloat16),
            jax.ShapeDtypeStruct((dim_in, rows), jnp.bfloat16),
            jax.ShapeDtypeStruct((rows, hidden_size), jnp.float32),
            jax.ShapeDtypeStruct((rows, width), jnp.float32),
            jax.ShapeDtypeStruct((rows, 2 * width), jnp.bfloat16),
        ],
        cost_estimate=pl.CostEstimate(
            flops=2 * rows * hidden_size * (dim_in + width),
            bytes_accessed=14 * rows * hidden_size,
            transcendentals=rows * hidden_size,
        ),
        compiler_params=pltpu.CompilerParams(vmem_limit_bytes=60 * 2**20),
        name="forward",
    )(codebook, weight_in, bias_in.reshape(1, -1), weight_out, bias_out.reshape(1, -1))


def pick_kernel(capacity, incoming_hbm, parts_hbm, out_ref, wanted_ref, asked_ref, parts_ref, sems):
    devices = asked_ref.shape[0]
    rows, both = parts_ref.shape
    width = both // 2
    step = pl.program_id(0)
    per_row = LANES // capacity

    @pl.when(step == 0)
    def _():
        payload = incoming_hbm.shape[1] - EXTRA
        load = pltpu.make_async_copy(
            incoming_hbm.at[pl.ds(0, devices), pl.ds(payload, EXTRA)], asked_ref, sems.at[0]
        )
        load.start()
        more = pltpu.make_async_copy(parts_hbm, parts_ref, sems.at[1])
        more.start()
        load.wait()
        for t in range(devices // per_row):
            row = asked_ref[t * per_row]
            for k in range(1, per_row):
                row = jnp.maximum(row, pltpu.roll(asked_ref[t * per_row + k], k * capacity, 1))
            wanted_ref[:, t * LANES : (t + 1) * LANES] = row
        more.wait()

    tile = out_ref.shape[0] * capacity
    lane = lax.broadcasted_iota(jnp.int32, (LANES, LANES), 1).astype(jnp.float32)
    choosers = []
    for start in range(0, tile, LANES):
        at = pl.ds(pl.multiple_of(step * tile + start, LANES), LANES)
        column = jnp.transpose(jnp.broadcast_to(wanted_ref[0:1, at], (LANES, LANES)))
        choosers.append(jnp.concatenate(
            [
                (column == lane + float(r)).astype(jnp.float32).astype(jnp.bfloat16)
                for r in range(0, rows, LANES)
            ],
            axis=1,
        ))
    value = dot(jnp.concatenate(choosers, axis=0), parts_ref[...])
    value = value[:, :width] + value[:, width:]
    for k in range(out_ref.shape[0]):
        out_ref[k] = value[k * capacity : (k + 1) * capacity]


def pick_rows(capacity, incoming, parts):
    devices = incoming.shape[0]
    rows, both = parts.shape
    steps = 4
    return pl.pallas_call(
        functools.partial(pick_kernel, capacity),
        grid=(steps,),
        in_specs=[pl.BlockSpec(memory_space=pl.ANY)] * 2,
        out_specs=[
            pl.BlockSpec((devices // steps, capacity, both // 2), lambda i: (i, 0, 0)),
            pl.BlockSpec((EXTRA, devices * capacity), lambda i: (0, 0)),
        ],
        out_shape=[
            jax.ShapeDtypeStruct((devices, capacity, both // 2), jnp.float32),
            jax.ShapeDtypeStruct((EXTRA, devices * capacity), jnp.float32),
        ],
        scratch_shapes=[
            pltpu.VMEM((devices, EXTRA, LANES), jnp.float32),
            pltpu.VMEM((rows, both), jnp.bfloat16),
            pltpu.SemaphoreType.DMA((2,)),
        ],
        cost_estimate=pl.CostEstimate(
            flops=2 * devices * capacity * rows * both,
            bytes_accessed=4 * devices * capacity * both,
            transcendentals=0,
        ),
        compiler_params=pltpu.CompilerParams(vmem_limit_bytes=60 * 2**20),
        name="pick_rows",
    )(incoming, parts)


def route_kernel(devices, capacity, owner_hbm, row_hbm, latents_hbm, cotangent_hbm,
                 out_ref, slot_ref, owner_ref, row_ref, latents_ref, cotangent_ref, parts_ref, sems):
    count, width = latents_ref.shape
    step = pl.program_id(0)
    tile = out_ref.shape[0] * capacity

    @pl.when(step == 0)
    def _():
        loads = [
            pltpu.make_async_copy(a, b, sems.at[k])
            for k, (a, b) in enumerate((
                (owner_hbm, owner_ref), (row_hbm, row_ref),
                (latents_hbm, latents_ref), (cotangent_hbm, cotangent_ref),
            ))
        ]
        for load in loads:
            load.start()
        before = (
            lax.broadcasted_iota(jnp.int32, (LANES, LANES), 0)
            < lax.broadcasted_iota(jnp.int32, (LANES, LANES), 1)
        ).astype(jnp.bfloat16)
        owner_ids = lax.broadcasted_iota(jnp.int32, (devices, LANES), 0)
        lane = lax.broadcasted_iota(jnp.int32, (LANES, LANES), 1)
        seen = jnp.zeros((devices, 1), jnp.float32)
        loads[0].wait()
        loads[1].wait()
        for start in range(0, count, LANES):
            part = pl.ds(start, LANES)
            owners = owner_ref[:, part]
            mine = (owner_ids == owners).astype(jnp.float32)
            ranks = dot(mine.astype(jnp.bfloat16), before) + seen
            rank = jnp.sum(mine * ranks, axis=0, keepdims=True)
            seen = seen + jnp.sum(mine, axis=1, keepdims=True)
            slot_ref[:, part] = owners * capacity + rank.astype(jnp.int32)
            rows = jnp.transpose(
                jnp.broadcast_to(row_ref[:, part].astype(jnp.float32), (LANES, LANES))
            )
            tall = jnp.floor(rows * (1.0 / 32.0))
            extra = jnp.where(lane == 0, tall, jnp.where(lane == 1, rows - 32.0 * tall, 0.0))
            extra = jnp.where(lane == 2, 1.0, extra)
            parts_ref[part, 2 * width :] = extra.astype(jnp.bfloat16)
        loads[2].wait()
        loads[3].wait()
        for start in range(0, count, LANES):
            part = pl.ds(start, LANES)
            value = cotangent_ref[part, :] - latents_ref[part, :]
            high = value.astype(jnp.bfloat16)
            parts_ref[part, :width] = high
            parts_ref[part, width : 2 * width] = (value - high.astype(jnp.float32)).astype(
                jnp.bfloat16
            )

    ids = lax.broadcasted_iota(jnp.int32, (tile, count), 0) + step * tile
    chooser = (ids == slot_ref[...]).astype(jnp.float32).astype(jnp.bfloat16)
    both = dot(chooser, parts_ref[...])
    value = both[:, :width] + both[:, width : 2 * width]
    turned = jnp.transpose(both[:, 2 * width :])
    wanted = 32.0 * turned[0:1] + turned[1:2] + turned[2:3] - 1.0
    lane = lax.broadcasted_iota(jnp.int32, (EXTRA, LANES), 1)
    for k in range(out_ref.shape[0]):
        own = slice(k * capacity, (k + 1) * capacity)
        for j in range(width // LANES):
            out_ref[k, j * capacity : (j + 1) * capacity, :] = value[own, j * LANES : (j + 1) * LANES]
        at = k * capacity // LANES * LANES
        row = jnp.broadcast_to(wanted[:, at : at + LANES], (EXTRA, LANES))
        shift = k * capacity - at
        if shift:
            row = pltpu.roll(row, LANES - shift, 1)
        out_ref[k, width // LANES * capacity :, :] = jnp.where(lane < capacity, row, -1.0)


def route(devices, capacity, code_owner, code_row, latents, cotangent):
    count, width = latents.shape
    per_step = max(1, 512 // capacity)
    block = width // LANES * capacity + EXTRA
    whole = lambda *shape: pl.BlockSpec(shape, lambda i: (0,) * len(shape))
    return pl.pallas_call(
        functools.partial(route_kernel, devices, capacity),
        grid=(devices // per_step,),
        in_specs=[pl.BlockSpec(memory_space=pl.ANY)] * 4,
        out_specs=[
            pl.BlockSpec((per_step, block, LANES), lambda i: (i, 0, 0)),
            whole(1, count),
        ],
        out_shape=[
            jax.ShapeDtypeStruct((devices, block, LANES), jnp.float32),
            jax.ShapeDtypeStruct((1, count), jnp.int32),
        ],
        scratch_shapes=[
            pltpu.VMEM((1, count), jnp.int32),
            pltpu.VMEM((1, count), jnp.int32),
            pltpu.VMEM((count, width), jnp.float32),
            pltpu.VMEM((count, width), jnp.float32),
            pltpu.VMEM((count, 2 * width + LANES), jnp.bfloat16),
            pltpu.SemaphoreType.DMA((4,)),
        ],
        compiler_params=pltpu.CompilerParams(vmem_limit_bytes=60 * 2**20),
        name="route",
    )(code_owner.reshape(1, count), code_row.reshape(1, count), latents, cotangent)


def place(sizes, k, j):
    _, inner, chip, _ = sizes
    if k % 2:
        return j
    return j % inner * chip + j // inner


def backward_kernel(sizes, capacity, incoming_hbm, wanted_hbm, hidden_hbm, slope_hbm, projected_hbm,
                    codebook_hbm, weight_hbm, *refs):
    outer, inner, chip, core = sizes
    devices = outer * inner * chip * core
    mine_hbm, theirs_hbm, refs = refs[:outer], refs[outer : 2 * outer], refs[2 * outer :]
    (incoming, wanted, hidden, slope, projected, codebook, weight, parts, low, grad, flat,
     in_sem, out_sem) = refs
    width = projected.shape[1]
    dim_in, rows = codebook.shape
    hidden_size = hidden.shape[0]
    length = flat.shape[2] - EXTRA
    pairs = list(zip(
        (wanted_hbm, projected_hbm, weight_hbm, slope_hbm, hidden_hbm, codebook_hbm),
        (wanted, projected, weight, slope, hidden, codebook),
    ))
    loads = [pltpu.make_async_copy(a, b, in_sem.at[k]) for k, (a, b) in enumerate(pairs)]
    loads[0].start()
    blocks = width // LANES
    quarter = devices // 4
    arrivals = []
    for n in range(4):
        part = pl.ds(n * quarter, quarter)
        arrivals.append(pltpu.make_async_copy(
            incoming_hbm.at[part, pl.ds(0, blocks * capacity)], incoming.at[part], in_sem.at[6 + n]
        ))
        arrivals[n].start()
    for load in loads[1:]:
        load.start()
    for n in range(4):
        arrivals[n].wait()
        for s in range(n * quarter, (n + 1) * quarter):
            own = pl.ds(s * capacity, capacity)
            for j in range(blocks):
                value = incoming[s, j * capacity : (j + 1) * capacity, :]
                high = value.astype(jnp.bfloat16)
                parts[own, j * LANES : (j + 1) * LANES] = high
                parts[own, width + j * LANES : width + (j + 1) * LANES] = (
                    value - high.astype(jnp.float32)
                ).astype(jnp.bfloat16)
    for load in loads[:4]:
        load.wait()
    tile = min(512, rows)
    bias_in = jnp.zeros((1, hidden_size), jnp.float32)
    bias_out = jnp.zeros((1, width), jnp.float32)
    for start in range(0, rows, tile):
        part = pl.ds(start, tile)
        ids = (lax.broadcasted_iota(jnp.int32, (tile, wanted.shape[1]), 0) + start).astype(
            jnp.float32
        )
        chooser = (ids == wanted[0:1, :]).astype(jnp.float32)
        times = jnp.sum(chooser, axis=1, keepdims=True)
        both = dot(chooser.astype(jnp.bfloat16), parts[...])
        code_grad = both[:, :width] + both[:, width:] + times * projected[part, :]
        bias_out += jnp.sum(code_grad, axis=0, keepdims=True)
        code_low = code_grad.astype(jnp.bfloat16)
        low[part, :] = code_low
        preact_grad = (dot(code_low, weight[...]) * slope[part, :]).astype(jnp.bfloat16)
        grad[part, :] = preact_grad
        bias_in += jnp.sum(preact_grad.astype(jnp.float32), axis=0, keepdims=True)


    first = lax.axis_index("outer")
    plane = lax.axis_index("inner") * chip + lax.axis_index("chip")
    me = lax.axis_index("core")
    band = hidden_size // outer
    pieces = inner * chip
    home = lax.rem(outer - first, outer)
    for k in range(outer):
        for e in range(pieces * core):
            flat[k, e, length:, :] = jnp.zeros((EXTRA, LANES), jnp.float32)
    for e, bias in enumerate((bias_in, bias_out)):
        for j in range(bias.shape[1] // LANES):
            flat[home, e, length + j : length + j + 1, :] = bias[:, j * LANES : (j + 1) * LANES]

    loads[4].wait()
    loads[5].wait()
    stores = []
    for k in range(outer - 1, -1, -1):
        o = lax.rem(first + k, outer)
        here = pl.ds(pl.multiple_of(o * band, band), band)

        def keep(row, value):
            for r in range(0, value.shape[0], length):
                flat[k, (row + r) // length, :length, :] = value[r : r + length, :]

        out = dot(codebook[...], grad[:, here])
        for j in range(band // LANES):
            keep(j * dim_in, out[:, j * LANES : (j + 1) * LANES])
        out = dot(hidden[here, :], low[...])
        for j in range(blocks):
            keep(band // LANES * dim_in + j * band, out[:, j * LANES : (j + 1) * LANES])
        for target, c in ((theirs_hbm, 1 - me), (mine_hbm, me)):
            for j in range(pieces):
                e = lax.bitwise_xor(plane, place(sizes, k, j)) * core + c
                copy = pltpu.make_async_copy(
                    flat.at[k, e], target[k].at[j], out_sem.at[len(stores)]
                )
                copy.start()
                stores.append(copy)
    for copy in stores:
        copy.wait()


def backward(sizes, capacity, incoming, wanted, hidden_t, slope, projected, codebook_t, weight_t):
    devices = incoming.shape[0]
    rows, width = projected.shape
    dim_in, hidden_size = codebook_t.shape[0], hidden_t.shape[0]
    length = (dim_in + width) * hidden_size // LANES // devices
    outer, inner, chip, core = sizes
    piece = jax.ShapeDtypeStruct((inner * chip, length + EXTRA, LANES), jnp.float32)
    operands = (incoming, wanted, hidden_t, slope, projected, codebook_t, weight_t)
    vmem = lambda shape, dtype: pltpu.VMEM(shape, dtype)
    slots = devices * capacity
    return pl.pallas_call(
        functools.partial(backward_kernel, sizes, capacity),
        in_specs=[pl.BlockSpec(memory_space=pl.ANY)] * len(operands),
        out_specs=[pl.BlockSpec(memory_space=pl.ANY)] * (2 * outer),
        out_shape=[piece] * (2 * outer),
        scratch_shapes=[vmem((devices, incoming.shape[1] - EXTRA, LANES), jnp.float32)]
        + [vmem(a.shape, a.dtype) for a in operands[1:]]
        + [
            vmem((slots, 2 * width), jnp.bfloat16),
            vmem((rows, width), jnp.bfloat16),
            vmem((rows, hidden_size), jnp.bfloat16),
            vmem((outer, inner * chip * core, length + EXTRA, LANES), jnp.float32),
            pltpu.SemaphoreType.DMA((10,)),
            pltpu.SemaphoreType.DMA((devices,)),
        ],
        cost_estimate=pl.CostEstimate(
            flops=2 * rows * (slots * 2 * width + hidden_size * (2 * width + dim_in)),
            bytes_accessed=16 * rows * hidden_size,
            transcendentals=0,
        ),
        compiler_params=pltpu.CompilerParams(vmem_limit_bytes=60 * 2**20),
        name="backward",
    )(*operands)


def assemble_kernel(sizes, *refs):
    outer, inner, chip, core = sizes
    planes = inner * chip
    operands, refs = refs[: 2 * core * planes], refs[2 * core * planes :]
    weight_in, weight_out, bias_in, bias_out, sems, bias_sem = refs
    length = operands[0].shape[0] - EXTRA
    dim_in, hidden_size = weight_in.shape
    band = hidden_size // outer
    base = band // LANES * dim_in
    first = lax.axis_index("outer")
    plane = lax.axis_index("inner") * chip + lax.axis_index("chip")
    me = lax.axis_index("core")
    pieces = []
    for n, operand in enumerate(operands):
        c, n = divmod(n, 2 * planes)
        far, j = divmod(n, planes)
        if far:
            pieces += [(operand.at[k - 1], c, k, j) for k in range(1, outer)]
        else:
            pieces.append((operand, c, 0, j))
    copies = []
    for n, (piece, c, k, j) in enumerate(pieces):
        o = lax.rem(first + outer - k, outer)
        e = lax.bitwise_xor(plane, j) * core + lax.bitwise_xor(me, c)
        at = e * length
        source = piece.at[pl.ds(0, length)]

        def copy_to(target, row, column):
            rows = pl.ds(pl.multiple_of(row, length), length)
            lanes = pl.ds(pl.multiple_of(column * LANES, LANES), LANES)
            return pltpu.make_async_copy(source, target.at[rows, lanes], sems.at[n])

        @pl.when(at < base)
        def _():
            column = o * (band // LANES) + lax.div(at, dim_in)
            copy_to(weight_in, lax.rem(at, dim_in), column).start()

        @pl.when(at >= base)
        def _():
            copy_to(weight_out, o * band + lax.rem(at - base, band), lax.div(at - base, band)).start()

        for row, bias in enumerate((bias_in, bias_out)):

            @pl.when((o == 0) & (e == row))
            def _():
                copy = pltpu.make_async_copy(
                    piece.at[pl.ds(length, EXTRA)], bias, bias_sem
                )
                copy.start()
                copy.wait()

        copies.append(copy_to(weight_in, 0, 0))
    for copy in copies:
        copy.wait()


def assemble(sizes, pieces, dim_in, hidden_size, width):
    hbm = pl.BlockSpec(memory_space=pl.ANY)
    return pl.pallas_call(
        functools.partial(assemble_kernel, sizes),
        in_specs=[hbm] * len(pieces),
        out_specs=[hbm] * 4,
        out_shape=[
            jax.ShapeDtypeStruct((dim_in, hidden_size), jnp.float32),
            jax.ShapeDtypeStruct((hidden_size, width), jnp.float32),
            jax.ShapeDtypeStruct((EXTRA, LANES), jnp.float32),
            jax.ShapeDtypeStruct((EXTRA, LANES), jnp.float32),
        ],
        scratch_shapes=[
            pltpu.SemaphoreType.DMA((math.prod(sizes),)),
            pltpu.SemaphoreType.DMA,
        ],
        compiler_params=pltpu.CompilerParams(vmem_limit_bytes=4 * 2**20),
        name="assemble",
    )(*pieces)


def along(sizes, x, k):
    outer = sizes[0]
    return lax.ppermute(x, "outer", [(o, (o + k) % outer) for o in range(outer)])


def across(sizes, axis, x, j):
    size = sizes[AXES.index(axis)]
    return lax.ppermute(x, axis, [(p, p ^ j) for p in range(size)])


def sum_chunks(sizes, mine, theirs):
    outer, inner, chip, _ = sizes
    chunks = [None] * outer
    for k in range(outer - 1, -1, -1):
        slow, fast = ("inner", "chip") if k % 2 else ("chip", "inner")
        low = sizes[AXES.index(fast)]
        arrived = across(sizes, "core", theirs[k], 1)
        part = mine[k][:low] + arrived[:low]
        for j in range(1, sizes[AXES.index(slow)]):
            here = slice(j * low, (j + 1) * low)
            part = part + across(sizes, slow, mine[k][here] + arrived[here], j)
        chunks[k] = part[0]
        for j in range(1, low):
            chunks[k] = chunks[k] + across(sizes, fast, part[j], j)
    total = chunks[0]
    for k in range(outer - 1, 0, -1):
        total = total + along(sizes, chunks[k], k)
    return total


def spread_chunks(sizes, total):
    outer, inner, chip, _ = sizes
    planes = inner * chip

    def plane(x, j):
        if j == 0:
            return x
        return lax.ppermute(x, ("inner", "chip"), [(p, p ^ j) for p in range(planes)])

    line = [along(sizes, total, k) for k in range(1, outer)]
    near = [plane(total, j) for j in range(planes)]
    line = jnp.stack(line)
    return near + [plane(line, j) for j in range(planes)]


def per_device(
    sizes, codebook, weight_in, bias_in, weight_out, bias_out, latents, cotangent, code_owner, code_row
):
    outer, inner, chip, core = sizes
    devices = outer * inner * chip * core
    rows, dim_in = codebook.shape
    hidden_size = weight_in.shape[1]
    count, width = latents.shape
    capacity = max(2, 2 * count // devices)

    outgoing, slots = route(devices, capacity, code_owner, code_row, latents, cotangent)
    outgoing, bias_in = lax.optimization_barrier((outgoing, bias_in))
    taken, bias_in = lax.optimization_barrier((code_row[0] >= 0, bias_in))
    incoming = lax.all_to_all(outgoing, AXES, split_axis=0, concat_axis=0, tiled=True)

    hidden_t, codebook_t, slope, projected, parts = forward(
        codebook, weight_in, bias_in, weight_out, bias_out
    )
    picked, wanted = pick_rows(capacity, incoming, parts)
    answers = lax.all_to_all(picked, AXES, split_axis=0, concat_axis=0, tiled=True)

    weight_t = weight_out.T

    def reduce_half(*operands):
        pieces = backward(sizes, capacity, *operands)
        return sum_chunks(sizes, list(pieces[:outer]), list(pieces[outer:]))

    def nothing(*operands):
        length = (dim_in + width) * hidden_size // LANES // devices
        return jnp.zeros((length + EXTRA, LANES), jnp.float32)

    total = lax.cond(
        taken, reduce_half, nothing,
        incoming, wanted, hidden_t, slope, projected, codebook_t, weight_t,
    )
    total, answers = lax.optimization_barrier((total, answers))
    answers = answers.reshape(-1, width)
    near = spread_chunks(sizes, total)

    slot_ids = jnp.arange(devices * capacity, dtype=jnp.int32)
    from_slot = slots.reshape(-1, 1) == slot_ids[None, :]
    chosen = pick(from_slot.astype(jnp.bfloat16), answers)
    latent_grad = cotangent - 0.25 * (chosen - latents)
    near[-1], latent_grad = lax.optimization_barrier((near[-1], latent_grad))

    chunks = near + [across(sizes, "core", x, 1) for x in near]
    gw_in, gw_out, gb_in, gb_out = assemble(sizes, chunks, dim_in, hidden_size, width)
    gb_in, gb_out = gb_in.reshape(-1)[:hidden_size], gb_out.reshape(-1)[:width]
    return (latent_grad, gw_in, gb_in, gw_out, gb_out)


def solution(mesh):
    code, data = mesh.shape["code"], mesh.shape["dp"]
    core = 2
    outer = 1
    while outer * outer < code:
        outer *= 2
    sizes = (outer, code // outer, data // core, core)
    fine = Mesh(mesh.devices.reshape(sizes), AXES)
    rows = P(AXES, None)
    return jax.shard_map(
        functools.partial(per_device, sizes),
        mesh=fine,
        in_specs=(rows, P(), P(), P(), P(), rows, rows, rows, P(AXES)),
        out_specs=(rows, P(), P(), P(), P()),
        check_vma=False,
    )
```

```python
import functools

import jax
import jax.numpy as jnp
from jax import lax
from jax.experimental import pallas as pl
from jax.experimental.pallas import tpu as pltpu
from jax.sharding import Mesh, PartitionSpec as P

scale_gelu = 0.7978845608028654
cubic_term = 0.044715
LANES = 128
EXTRA = 8
AXES = ("outer", "inner", "chip", "core")


def gelu_parts(x):
    tangent = jnp.tanh(scale_gelu * (x + cubic_term * x * x * x))
    value = 0.5 * x * (1.0 + tangent)
    slope = 0.5 * (1.0 + tangent) + 0.5 * x * (1.0 - tangent * tangent) * scale_gelu * (
        1.0 + 3.0 * cubic_term * x * x
    )
    return value, slope


def split_two(x):
    high = lax.reduce_precision(x, 8, 7)
    low = (x - high).astype(jnp.bfloat16)
    return jnp.concatenate([high.astype(jnp.bfloat16), low], axis=1)


def pick(chooser, rows):
    width = rows.shape[1]
    both = jnp.dot(chooser, split_two(rows), preferred_element_type=jnp.float32)
    return both[:, :width] + both[:, width:]


def dot(a, b):
    return jnp.dot(a, b, preferred_element_type=jnp.float32)


def forward_kernel(codebook_ref, weight_in_ref, bias_in_ref, weight_out_ref, bias_out_ref,
                   hidden_ref, codebook_t_ref, slope_ref, projected_ref, parts_ref):
    width = projected_ref.shape[1]
    codebook = codebook_ref[...]
    codebook_t_ref[...] = jnp.transpose(codebook.astype(jnp.float32)).astype(jnp.bfloat16)
    hidden, slope = gelu_parts(dot(codebook, weight_in_ref[...]) + bias_in_ref[...])
    slope_ref[...] = slope
    hidden_ref[...] = jnp.transpose(hidden).astype(jnp.bfloat16)
    projected = dot(hidden.astype(jnp.bfloat16), weight_out_ref[...]) + bias_out_ref[...]
    projected_ref[...] = projected
    high = projected.astype(jnp.bfloat16)
    parts_ref[:, :width] = high
    parts_ref[:, width:] = (projected - high.astype(jnp.float32)).astype(jnp.bfloat16)


def forward(codebook, weight_in, bias_in, weight_out, bias_out):
    rows, dim_in = codebook.shape
    hidden_size, width = weight_out.shape
    tile = min(256, rows)
    whole = lambda *shape: pl.BlockSpec(shape, lambda i: (0, 0))
    return pl.pallas_call(
        forward_kernel,
        grid=(rows // tile,),
        in_specs=[
            pl.BlockSpec((tile, dim_in), lambda i: (i, 0)),
            whole(dim_in, hidden_size),
            whole(1, hidden_size),
            whole(hidden_size, width),
            whole(1, width),
        ],
        out_specs=[
            pl.BlockSpec((hidden_size, tile), lambda i: (0, i)),
            pl.BlockSpec((dim_in, tile), lambda i: (0, i)),
            pl.BlockSpec((tile, hidden_size), lambda i: (i, 0)),
            pl.BlockSpec((tile, width), lambda i: (i, 0)),
            pl.BlockSpec((tile, 2 * width), lambda i: (i, 0)),
        ],
        out_shape=[
            jax.ShapeDtypeStruct((hidden_size, rows), jnp.bfloat16),
            jax.ShapeDtypeStruct((dim_in, rows), jnp.bfloat16),
            jax.ShapeDtypeStruct((rows, hidden_size), jnp.float32),
            jax.ShapeDtypeStruct((rows, width), jnp.float32),
            jax.ShapeDtypeStruct((rows, 2 * width), jnp.bfloat16),
        ],
        cost_estimate=pl.CostEstimate(
            flops=2 * rows * hidden_size * (dim_in + width),
            bytes_accessed=14 * rows * hidden_size,
            transcendentals=rows * hidden_size,
        ),
        compiler_params=pltpu.CompilerParams(vmem_limit_bytes=60 * 2**20),
        name="forward",
    )(codebook, weight_in, bias_in.reshape(1, -1), weight_out, bias_out.reshape(1, -1))


def pick_kernel(capacity, incoming_hbm, parts_hbm, out_ref, wanted_ref, asked_ref, parts_ref, sems):
    devices = asked_ref.shape[0]
    rows, both = parts_ref.shape
    width = both // 2
    step = pl.program_id(0)
    per_row = LANES // capacity

    @pl.when(step == 0)
    def _():
        payload = incoming_hbm.shape[1] - EXTRA
        load = pltpu.make_async_copy(
            incoming_hbm.at[pl.ds(0, devices), pl.ds(payload, EXTRA)], asked_ref, sems.at[0]
        )
        load.start()
        more = pltpu.make_async_copy(parts_hbm, parts_ref, sems.at[1])
        more.start()
        load.wait()
        for t in range(devices // per_row):
            row = asked_ref[t * per_row]
            for k in range(1, per_row):
                row = jnp.maximum(row, pltpu.roll(asked_ref[t * per_row + k], k * capacity, 1))
            wanted_ref[:, t * LANES : (t + 1) * LANES] = row
        more.wait()

    tile = out_ref.shape[0] * capacity
    lane = lax.broadcasted_iota(jnp.int32, (LANES, LANES), 1).astype(jnp.float32)
    choosers = []
    for start in range(0, tile, LANES):
        at = pl.ds(pl.multiple_of(step * tile + start, LANES), LANES)
        column = jnp.transpose(jnp.broadcast_to(wanted_ref[0:1, at], (LANES, LANES)))
        choosers.append(jnp.concatenate(
            [
                (column == lane + float(r)).astype(jnp.float32).astype(jnp.bfloat16)
                for r in range(0, rows, LANES)
            ],
            axis=1,
        ))
    value = dot(jnp.concatenate(choosers, axis=0), parts_ref[...])
    value = value[:, :width] + value[:, width:]
    for k in range(out_ref.shape[0]):
        out_ref[k] = value[k * capacity : (k + 1) * capacity]


def pick_rows(capacity, incoming, parts):
    devices = incoming.shape[0]
    rows, both = parts.shape
    steps = 4
    return pl.pallas_call(
        functools.partial(pick_kernel, capacity),
        grid=(steps,),
        in_specs=[pl.BlockSpec(memory_space=pl.ANY)] * 2,
        out_specs=[
            pl.BlockSpec((devices // steps, capacity, both // 2), lambda i: (i, 0, 0)),
            pl.BlockSpec((EXTRA, devices * capacity), lambda i: (0, 0)),
        ],
        out_shape=[
            jax.ShapeDtypeStruct((devices, capacity, both // 2), jnp.float32),
            jax.ShapeDtypeStruct((EXTRA, devices * capacity), jnp.float32),
        ],
        scratch_shapes=[
            pltpu.VMEM((devices, EXTRA, LANES), jnp.float32),
            pltpu.VMEM((rows, both), jnp.bfloat16),
            pltpu.SemaphoreType.DMA((2,)),
        ],
        cost_estimate=pl.CostEstimate(
            flops=2 * devices * capacity * rows * both,
            bytes_accessed=4 * devices * capacity * both,
            transcendentals=0,
        ),
        compiler_params=pltpu.CompilerParams(vmem_limit_bytes=60 * 2**20),
        name="pick_rows",
    )(incoming, parts)


def route_kernel(devices, capacity, owner_hbm, row_hbm, latents_hbm, cotangent_hbm,
                 out_ref, slot_ref, owner_ref, row_ref, latents_ref, cotangent_ref, parts_ref, sems):
    count, width = latents_ref.shape
    step = pl.program_id(0)
    tile = out_ref.shape[0] * capacity

    @pl.when(step == 0)
    def _():
        loads = [
            pltpu.make_async_copy(a, b, sems.at[k])
            for k, (a, b) in enumerate((
                (owner_hbm, owner_ref), (row_hbm, row_ref),
                (latents_hbm, latents_ref), (cotangent_hbm, cotangent_ref),
            ))
        ]
        for load in loads:
            load.start()
        before = (
            lax.broadcasted_iota(jnp.int32, (LANES, LANES), 0)
            < lax.broadcasted_iota(jnp.int32, (LANES, LANES), 1)
        ).astype(jnp.bfloat16)
        owner_ids = lax.broadcasted_iota(jnp.int32, (devices, LANES), 0)
        lane = lax.broadcasted_iota(jnp.int32, (LANES, LANES), 1)
        seen = jnp.zeros((devices, 1), jnp.float32)
        loads[0].wait()
        loads[1].wait()
        for start in range(0, count, LANES):
            part = pl.ds(start, LANES)
            owners = owner_ref[:, part]
            mine = (owner_ids == owners).astype(jnp.float32)
            ranks = dot(mine.astype(jnp.bfloat16), before) + seen
            rank = jnp.sum(mine * ranks, axis=0, keepdims=True)
            seen = seen + jnp.sum(mine, axis=1, keepdims=True)
            slot_ref[:, part] = owners * capacity + rank.astype(jnp.int32)
            rows = jnp.transpose(
                jnp.broadcast_to(row_ref[:, part].astype(jnp.float32), (LANES, LANES))
            )
            tall = jnp.floor(rows * (1.0 / 32.0))
            extra = jnp.where(lane == 0, tall, jnp.where(lane == 1, rows - 32.0 * tall, 0.0))
            extra = jnp.where(lane == 2, 1.0, extra)
            parts_ref[part, 2 * width :] = extra.astype(jnp.bfloat16)
        loads[2].wait()
        loads[3].wait()
        for start in range(0, count, LANES):
            part = pl.ds(start, LANES)
            value = cotangent_ref[part, :] - latents_ref[part, :]
            high = value.astype(jnp.bfloat16)
            parts_ref[part, :width] = high
            parts_ref[part, width : 2 * width] = (value - high.astype(jnp.float32)).astype(
                jnp.bfloat16
            )

    ids = lax.broadcasted_iota(jnp.int32, (tile, count), 0) + step * tile
    chooser = (ids == slot_ref[...]).astype(jnp.float32).astype(jnp.bfloat16)
    both = dot(chooser, parts_ref[...])
    value = both[:, :width] + both[:, width : 2 * width]
    turned = jnp.transpose(both[:, 2 * width :])
    wanted = 32.0 * turned[0:1] + turned[1:2] + turned[2:3] - 1.0
    lane = lax.broadcasted_iota(jnp.int32, (EXTRA, LANES), 1)
    for k in range(out_ref.shape[0]):
        own = slice(k * capacity, (k + 1) * capacity)
        for j in range(width // LANES):
            out_ref[k, j * capacity : (j + 1) * capacity, :] = value[own, j * LANES : (j + 1) * LANES]
        at = k * capacity // LANES * LANES
        row = jnp.broadcast_to(wanted[:, at : at + LANES], (EXTRA, LANES))
        shift = k * capacity - at
        if shift:
            row = pltpu.roll(row, LANES - shift, 1)
        out_ref[k, width // LANES * capacity :, :] = jnp.where(lane < capacity, row, -1.0)


def route(devices, capacity, code_owner, code_row, latents, cotangent):
    count, width = latents.shape
    per_step = max(1, 512 // capacity)
    block = width // LANES * capacity + EXTRA
    whole = lambda *shape: pl.BlockSpec(shape, lambda i: (0,) * len(shape))
    return pl.pallas_call(
        functools.partial(route_kernel, devices, capacity),
        grid=(devices // per_step,),
        in_specs=[pl.BlockSpec(memory_space=pl.ANY)] * 4,
        out_specs=[
            pl.BlockSpec((per_step, block, LANES), lambda i: (i, 0, 0)),
            whole(1, count),
        ],
        out_shape=[
            jax.ShapeDtypeStruct((devices, block, LANES), jnp.float32),
            jax.ShapeDtypeStruct((1, count), jnp.int32),
        ],
        scratch_shapes=[
            pltpu.VMEM((1, count), jnp.int32),
            pltpu.VMEM((1, count), jnp.int32),
            pltpu.VMEM((count, width), jnp.float32),
            pltpu.VMEM((count, width), jnp.float32),
            pltpu.VMEM((count, 2 * width + LANES), jnp.bfloat16),
            pltpu.SemaphoreType.DMA((4,)),
        ],
        compiler_params=pltpu.CompilerParams(vmem_limit_bytes=60 * 2**20),
        name="route",
    )(code_owner.reshape(1, count), code_row.reshape(1, count), latents, cotangent)


def place(sizes, k, j):
    _, inner, chip, _ = sizes
    if k % 2:
        return j
    return j % inner * chip + j // inner


def backward_kernel(sizes, capacity, incoming_hbm, wanted_hbm, hidden_hbm, slope_hbm, projected_hbm,
                    codebook_hbm, weight_hbm, *refs):
    outer, inner, chip, core = sizes
    devices = outer * inner * chip * core
    mine_hbm, theirs_hbm, refs = refs[:outer], refs[outer : 2 * outer], refs[2 * outer :]
    (incoming, wanted, hidden, slope, projected, codebook, weight, parts, low, grad, flat,
     in_sem, out_sem) = refs
    width = projected.shape[1]
    dim_in, rows = codebook.shape
    hidden_size = hidden.shape[0]
    length = flat.shape[2] - EXTRA
    pairs = list(zip(
        (wanted_hbm, projected_hbm, weight_hbm, slope_hbm, hidden_hbm, codebook_hbm),
        (wanted, projected, weight, slope, hidden, codebook),
    ))
    loads = [pltpu.make_async_copy(a, b, in_sem.at[k]) for k, (a, b) in enumerate(pairs)]
    loads[0].start()
    blocks = width // LANES
    quarter = devices // 4
    arrivals = []
    for n in range(4):
        part = pl.ds(n * quarter, quarter)
        arrivals.append(pltpu.make_async_copy(
            incoming_hbm.at[part, pl.ds(0, blocks * capacity)], incoming.at[part], in_sem.at[6 + n]
        ))
        arrivals[n].start()
    for load in loads[1:]:
        load.start()
    for n in range(4):
        arrivals[n].wait()
        for s in range(n * quarter, (n + 1) * quarter):
            own = pl.ds(s * capacity, capacity)
            for j in range(blocks):
                value = incoming[s, j * capacity : (j + 1) * capacity, :]
                high = value.astype(jnp.bfloat16)
                parts[own, j * LANES : (j + 1) * LANES] = high
                parts[own, width + j * LANES : width + (j + 1) * LANES] = (
                    value - high.astype(jnp.float32)
                ).astype(jnp.bfloat16)
    for load in loads[:4]:
        load.wait()
    tile = min(512, rows)
    bias_in = jnp.zeros((1, hidden_size), jnp.float32)
    bias_out = jnp.zeros((1, width), jnp.float32)
    for start in range(0, rows, tile):
        part = pl.ds(start, tile)
        ids = (lax.broadcasted_iota(jnp.int32, (tile, wanted.shape[1]), 0) + start).astype(
            jnp.float32
        )
        chooser = (ids == wanted[0:1, :]).astype(jnp.float32)
        times = jnp.sum(chooser, axis=1, keepdims=True)
        both = dot(chooser.astype(jnp.bfloat16), parts[...])
        code_grad = both[:, :width] + both[:, width:] + times * projected[part, :]
        bias_out += jnp.sum(code_grad, axis=0, keepdims=True)
        code_low = code_grad.astype(jnp.bfloat16)
        low[part, :] = code_low
        preact_grad = (dot(code_low, weight[...]) * slope[part, :]).astype(jnp.bfloat16)
        grad[part, :] = preact_grad
        bias_in += jnp.sum(preact_grad.astype(jnp.float32), axis=0, keepdims=True)


    first = lax.axis_index("outer")
    plane = lax.axis_index("inner") * chip + lax.axis_index("chip")
    me = lax.axis_index("core")
    band = hidden_size // outer
    pieces = inner * chip
    home = lax.rem(outer - first, outer)
    for k in range(outer):
        for e in range(pieces * core):
            flat[k, e, length:, :] = jnp.zeros((EXTRA, LANES), jnp.float32)
    for e, bias in enumerate((bias_in, bias_out)):
        for j in range(bias.shape[1] // LANES):
            flat[home, e, length + j : length + j + 1, :] = bias[:, j * LANES : (j + 1) * LANES]

    loads[4].wait()
    loads[5].wait()
    stores = []
    for k in range(outer - 1, -1, -1):
        o = lax.rem(first + k, outer)
        here = pl.ds(pl.multiple_of(o * band, band), band)

        def keep(row, value):
            for r in range(0, value.shape[0], length):
                flat[k, (row + r) // length, :length, :] = value[r : r + length, :]

        out = dot(codebook[...], grad[:, here])
        for j in range(band // LANES):
            keep(j * dim_in, out[:, j * LANES : (j + 1) * LANES])
        out = dot(hidden[here, :], low[...])
        for j in range(blocks):
            keep(band // LANES * dim_in + j * band, out[:, j * LANES : (j + 1) * LANES])
        for target, c in ((theirs_hbm, 1 - me), (mine_hbm, me)):
            for j in range(pieces):
                e = lax.bitwise_xor(plane, place(sizes, k, j)) * core + c
                copy = pltpu.make_async_copy(
                    flat.at[k, e], target[k].at[j], out_sem.at[len(stores)]
                )
                copy.start()
                stores.append(copy)
    for copy in stores:
        copy.wait()


def backward(sizes, capacity, incoming, wanted, hidden_t, slope, projected, codebook_t, weight_t):
    devices = incoming.shape[0]
    rows, width = projected.shape
    dim_in, hidden_size = codebook_t.shape[0], hidden_t.shape[0]
    length = (dim_in + width) * hidden_size // LANES // devices
    outer, inner, chip, core = sizes
    piece = jax.ShapeDtypeStruct((inner * chip, length + EXTRA, LANES), jnp.float32)
    operands = (incoming, wanted, hidden_t, slope, projected, codebook_t, weight_t)
    vmem = lambda shape, dtype: pltpu.VMEM(shape, dtype)
    slots = devices * capacity
    return pl.pallas_call(
        functools.partial(backward_kernel, sizes, capacity),
        in_specs=[pl.BlockSpec(memory_space=pl.ANY)] * len(operands),
        out_specs=[pl.BlockSpec(memory_space=pl.ANY)] * (2 * outer),
        out_shape=[piece] * (2 * outer),
        scratch_shapes=[vmem((devices, incoming.shape[1] - EXTRA, LANES), jnp.float32)]
        + [vmem(a.shape, a.dtype) for a in operands[1:]]
        + [
            vmem((slots, 2 * width), jnp.bfloat16),
            vmem((rows, width), jnp.bfloat16),
            vmem((rows, hidden_size), jnp.bfloat16),
            vmem((outer, inner * chip * core, length + EXTRA, LANES), jnp.float32),
            pltpu.SemaphoreType.DMA((10,)),
            pltpu.SemaphoreType.DMA((devices,)),
        ],
        cost_estimate=pl.CostEstimate(
            flops=2 * rows * (slots * 2 * width + hidden_size * (2 * width + dim_in)),
            bytes_accessed=16 * rows * hidden_size,
            transcendentals=0,
        ),
        compiler_params=pltpu.CompilerParams(vmem_limit_bytes=60 * 2**20),
        name="backward",
    )(*operands)


def assemble_kernel(sizes, *refs):
    outer, inner, chip, core = sizes
    devices = outer * inner * chip * core
    pieces, refs = refs[:devices], refs[devices:]
    weight_in, weight_out, bias_in, bias_out, sems, bias_sem = refs
    length = pieces[0].shape[0] - EXTRA
    dim_in, hidden_size = weight_in.shape
    band = hidden_size // outer
    base = band // LANES * dim_in
    first = lax.axis_index("outer")
    plane = lax.axis_index("inner") * chip + lax.axis_index("chip")
    me = lax.axis_index("core")
    copies = []
    for n, piece in enumerate(pieces):
        c, n = divmod(n, devices // core)
        k, j = divmod(n, inner * chip)
        n += c * (devices // core)
        o = lax.rem(first + outer - k, outer)
        e = lax.bitwise_xor(plane, place(sizes, k, j)) * core + lax.bitwise_xor(me, c)
        at = e * length
        source = piece.at[pl.ds(0, length)]

        def copy_to(target, row, column):
            rows = pl.ds(pl.multiple_of(row, length), length)
            lanes = pl.ds(pl.multiple_of(column * LANES, LANES), LANES)
            return pltpu.make_async_copy(source, target.at[rows, lanes], sems.at[n])

        @pl.when(at < base)
        def _():
            column = o * (band // LANES) + lax.div(at, dim_in)
            copy_to(weight_in, lax.rem(at, dim_in), column).start()

        @pl.when(at >= base)
        def _():
            copy_to(weight_out, o * band + lax.rem(at - base, band), lax.div(at - base, band)).start()

        for row, bias in enumerate((bias_in, bias_out)):

            @pl.when((o == 0) & (e == row))
            def _():
                copy = pltpu.make_async_copy(
                    piece.at[pl.ds(length, EXTRA)], bias, bias_sem
                )
                copy.start()
                copy.wait()

        copies.append(copy_to(weight_in, 0, 0))
    for copy in copies:
        copy.wait()


def assemble(sizes, pieces, dim_in, hidden_size, width):
    hbm = pl.BlockSpec(memory_space=pl.ANY)
    return pl.pallas_call(
        functools.partial(assemble_kernel, sizes),
        in_specs=[hbm] * len(pieces),
        out_specs=[hbm] * 4,
        out_shape=[
            jax.ShapeDtypeStruct((dim_in, hidden_size), jnp.float32),
            jax.ShapeDtypeStruct((hidden_size, width), jnp.float32),
            jax.ShapeDtypeStruct((EXTRA, LANES), jnp.float32),
            jax.ShapeDtypeStruct((EXTRA, LANES), jnp.float32),
        ],
        scratch_shapes=[
            pltpu.SemaphoreType.DMA((len(pieces),)),
            pltpu.SemaphoreType.DMA,
        ],
        compiler_params=pltpu.CompilerParams(vmem_limit_bytes=4 * 2**20),
        name="assemble",
    )(*pieces)


def along(sizes, x, k):
    outer = sizes[0]
    return lax.ppermute(x, "outer", [(o, (o + k) % outer) for o in range(outer)])


def across(sizes, axis, x, j):
    size = sizes[AXES.index(axis)]
    return lax.ppermute(x, axis, [(p, p ^ j) for p in range(size)])


def sum_chunks(sizes, mine, theirs):
    outer, inner, chip, _ = sizes
    chunks = [None] * outer
    for k in range(outer - 1, -1, -1):
        slow, fast = ("inner", "chip") if k % 2 else ("chip", "inner")
        low = sizes[AXES.index(fast)]
        arrived = across(sizes, "core", theirs[k], 1)
        part = mine[k][:low] + arrived[:low]
        for j in range(1, sizes[AXES.index(slow)]):
            here = slice(j * low, (j + 1) * low)
            part = part + across(sizes, slow, mine[k][here] + arrived[here], j)
        chunks[k] = part[0]
        for j in range(1, low):
            chunks[k] = chunks[k] + across(sizes, fast, part[j], j)
    total = chunks[0]
    for k in range(outer - 1, 0, -1):
        total = total + along(sizes, chunks[k], k)
    return total


def spread_chunks(sizes, total):
    outer, inner, chip, _ = sizes
    near = []
    for k in range(outer):
        slow, fast = ("inner", "chip") if k % 2 else ("chip", "inner")
        x = along(sizes, total, k) if k else total
        row = [across(sizes, fast, x, j) if j else x for j in range(sizes[AXES.index(fast)])]
        for j in range(sizes[AXES.index(slow)]):
            near += [across(sizes, slow, x, j) if j else x for x in row]
    return near


def per_device(
    sizes, codebook, weight_in, bias_in, weight_out, bias_out, latents, cotangent, code_owner, code_row
):
    outer, inner, chip, core = sizes
    devices = outer * inner * chip * core
    rows, dim_in = codebook.shape
    hidden_size = weight_in.shape[1]
    count, width = latents.shape
    capacity = max(2, 2 * count // devices)

    outgoing, slots = route(devices, capacity, code_owner, code_row, latents, cotangent)
    outgoing, bias_in = lax.optimization_barrier((outgoing, bias_in))
    taken, bias_in = lax.optimization_barrier((code_row[0] >= 0, bias_in))
    incoming = lax.all_to_all(outgoing, AXES, split_axis=0, concat_axis=0, tiled=True)

    hidden_t, codebook_t, slope, projected, parts = forward(
        codebook, weight_in, bias_in, weight_out, bias_out
    )
    picked, wanted = pick_rows(capacity, incoming, parts)
    answers = lax.all_to_all(picked, AXES, split_axis=0, concat_axis=0, tiled=True)

    weight_t = weight_out.T

    def reduce_half(*operands):
        pieces = backward(sizes, capacity, *operands)
        return sum_chunks(sizes, list(pieces[:outer]), list(pieces[outer:]))

    def nothing(*operands):
        length = (dim_in + width) * hidden_size // LANES // devices
        return jnp.zeros((length + EXTRA, LANES), jnp.float32)

    total = lax.cond(
        taken, reduce_half, nothing,
        incoming, wanted, hidden_t, slope, projected, codebook_t, weight_t,
    )
    total, answers = lax.optimization_barrier((total, answers))
    answers = answers.reshape(-1, width)
    near = spread_chunks(sizes, total)

    slot_ids = jnp.arange(devices * capacity, dtype=jnp.int32)
    from_slot = slots.reshape(-1, 1) == slot_ids[None, :]
    chosen = pick(from_slot.astype(jnp.bfloat16), answers)
    latent_grad = cotangent - 0.25 * (chosen - latents)
    late = len(near) - inner * chip
    near[late], latent_grad = lax.optimization_barrier((near[late], latent_grad))

    chunks = near + [across(sizes, "core", x, 1) for x in near]
    gw_in, gw_out, gb_in, gb_out = assemble(sizes, chunks, dim_in, hidden_size, width)
    gb_in, gb_out = gb_in.reshape(-1)[:hidden_size], gb_out.reshape(-1)[:width]
    return (latent_grad, gw_in, gb_in, gw_out, gb_out)


def solution(mesh):
    code, data = mesh.shape["code"], mesh.shape["dp"]
    core = 2
    outer = 1
    while outer * outer < code:
        outer *= 2
    sizes = (outer, code // outer, data // core, core)
    fine = Mesh(mesh.devices.reshape(sizes), AXES)
    rows = P(AXES, None)
    return jax.shard_map(
        functools.partial(per_device, sizes),
        mesh=fine,
        in_specs=(rows, P(), P(), P(), P(), rows, rows, rows, P(AXES)),
        out_specs=(rows, P(), P(), P(), P()),
        check_vma=False,
    )
```

```python
import functools

import jax
import jax.numpy as jnp
from jax import lax
from jax.experimental import pallas as pl
from jax.experimental.pallas import tpu as pltpu
from jax.sharding import Mesh, PartitionSpec as P

scale_gelu = 0.7978845608028654
cubic_term = 0.044715
LANES = 128
EXTRA = 8
AXES = ("outer", "inner", "chip", "core")


def gelu_parts(x):
    tangent = jnp.tanh(scale_gelu * (x + cubic_term * x * x * x))
    value = 0.5 * x * (1.0 + tangent)
    slope = 0.5 * (1.0 + tangent) + 0.5 * x * (1.0 - tangent * tangent) * scale_gelu * (
        1.0 + 3.0 * cubic_term * x * x
    )
    return value, slope


def split_two(x):
    high = lax.reduce_precision(x, 8, 7)
    low = (x - high).astype(jnp.bfloat16)
    return jnp.concatenate([high.astype(jnp.bfloat16), low], axis=1)


def pick(chooser, rows):
    width = rows.shape[1]
    both = jnp.dot(chooser, split_two(rows), preferred_element_type=jnp.float32)
    return both[:, :width] + both[:, width:]


def dot(a, b):
    return jnp.dot(a, b, preferred_element_type=jnp.float32)


def forward_kernel(codebook_ref, weight_in_ref, bias_in_ref, weight_out_ref, bias_out_ref,
                   hidden_ref, codebook_t_ref, slope_ref, projected_ref, parts_ref):
    width = projected_ref.shape[1]
    codebook = codebook_ref[...]
    codebook_t_ref[...] = jnp.transpose(codebook.astype(jnp.float32)).astype(jnp.bfloat16)
    hidden, slope = gelu_parts(dot(codebook, weight_in_ref[...]) + bias_in_ref[...])
    slope_ref[...] = slope
    hidden_ref[...] = jnp.transpose(hidden).astype(jnp.bfloat16)
    projected = dot(hidden.astype(jnp.bfloat16), weight_out_ref[...]) + bias_out_ref[...]
    projected_ref[...] = projected
    high = projected.astype(jnp.bfloat16)
    parts_ref[:, :width] = high
    parts_ref[:, width:] = (projected - high.astype(jnp.float32)).astype(jnp.bfloat16)


def forward(codebook, weight_in, bias_in, weight_out, bias_out):
    rows, dim_in = codebook.shape
    hidden_size, width = weight_out.shape
    tile = min(256, rows)
    whole = lambda *shape: pl.BlockSpec(shape, lambda i: (0, 0))
    return pl.pallas_call(
        forward_kernel,
        grid=(rows // tile,),
        in_specs=[
            pl.BlockSpec((tile, dim_in), lambda i: (i, 0)),
            whole(dim_in, hidden_size),
            whole(1, hidden_size),
            whole(hidden_size, width),
            whole(1, width),
        ],
        out_specs=[
            pl.BlockSpec((hidden_size, tile), lambda i: (0, i)),
            pl.BlockSpec((dim_in, tile), lambda i: (0, i)),
            pl.BlockSpec((tile, hidden_size), lambda i: (i, 0)),
            pl.BlockSpec((tile, width), lambda i: (i, 0)),
            pl.BlockSpec((tile, 2 * width), lambda i: (i, 0)),
        ],
        out_shape=[
            jax.ShapeDtypeStruct((hidden_size, rows), jnp.bfloat16),
            jax.ShapeDtypeStruct((dim_in, rows), jnp.bfloat16),
            jax.ShapeDtypeStruct((rows, hidden_size), jnp.float32),
            jax.ShapeDtypeStruct((rows, width), jnp.float32),
            jax.ShapeDtypeStruct((rows, 2 * width), jnp.bfloat16),
        ],
        cost_estimate=pl.CostEstimate(
            flops=2 * rows * hidden_size * (dim_in + width),
            bytes_accessed=14 * rows * hidden_size,
            transcendentals=rows * hidden_size,
        ),
        compiler_params=pltpu.CompilerParams(vmem_limit_bytes=60 * 2**20),
        name="forward",
    )(codebook, weight_in, bias_in.reshape(1, -1), weight_out, bias_out.reshape(1, -1))


def pick_kernel(capacity, incoming_hbm, parts_hbm, out_ref, wanted_ref, asked_ref, parts_ref, sems):
    devices = asked_ref.shape[0]
    rows, both = parts_ref.shape
    width = both // 2
    step = pl.program_id(0)
    per_row = LANES // capacity

    @pl.when(step == 0)
    def _():
        payload = incoming_hbm.shape[1] - EXTRA
        load = pltpu.make_async_copy(
            incoming_hbm.at[pl.ds(0, devices), pl.ds(payload, EXTRA)], asked_ref, sems.at[0]
        )
        load.start()
        more = pltpu.make_async_copy(parts_hbm, parts_ref, sems.at[1])
        more.start()
        load.wait()
        for t in range(devices // per_row):
            row = asked_ref[t * per_row]
            for k in range(1, per_row):
                row = jnp.maximum(row, pltpu.roll(asked_ref[t * per_row + k], k * capacity, 1))
            wanted_ref[:, t * LANES : (t + 1) * LANES] = row
        more.wait()

    tile = out_ref.shape[0] * capacity
    lane = lax.broadcasted_iota(jnp.int32, (LANES, LANES), 1).astype(jnp.float32)
    choosers = []
    for start in range(0, tile, LANES):
        at = pl.ds(pl.multiple_of(step * tile + start, LANES), LANES)
        column = jnp.transpose(jnp.broadcast_to(wanted_ref[0:1, at], (LANES, LANES)))
        choosers.append(jnp.concatenate(
            [
                (column == lane + float(r)).astype(jnp.float32).astype(jnp.bfloat16)
                for r in range(0, rows, LANES)
            ],
            axis=1,
        ))
    value = dot(jnp.concatenate(choosers, axis=0), parts_ref[...])
    value = value[:, :width] + value[:, width:]
    for k in range(out_ref.shape[0]):
        out_ref[k] = value[k * capacity : (k + 1) * capacity]


def pick_rows(capacity, incoming, parts):
    devices = incoming.shape[0]
    rows, both = parts.shape
    steps = 4
    return pl.pallas_call(
        functools.partial(pick_kernel, capacity),
        grid=(steps,),
        in_specs=[pl.BlockSpec(memory_space=pl.ANY)] * 2,
        out_specs=[
            pl.BlockSpec((devices // steps, capacity, both // 2), lambda i: (i, 0, 0)),
            pl.BlockSpec((EXTRA, devices * capacity), lambda i: (0, 0)),
        ],
        out_shape=[
            jax.ShapeDtypeStruct((devices, capacity, both // 2), jnp.float32),
            jax.ShapeDtypeStruct((EXTRA, devices * capacity), jnp.float32),
        ],
        scratch_shapes=[
            pltpu.VMEM((devices, EXTRA, LANES), jnp.float32),
            pltpu.VMEM((rows, both), jnp.bfloat16),
            pltpu.SemaphoreType.DMA((2,)),
        ],
        cost_estimate=pl.CostEstimate(
            flops=2 * devices * capacity * rows * both,
            bytes_accessed=4 * devices * capacity * both,
            transcendentals=0,
        ),
        compiler_params=pltpu.CompilerParams(vmem_limit_bytes=60 * 2**20),
        name="pick_rows",
    )(incoming, parts)


def route_kernel(devices, capacity, owner_hbm, row_hbm, latents_hbm, cotangent_hbm,
                 out_ref, slot_ref, owner_ref, row_ref, latents_ref, cotangent_ref, parts_ref, sems):
    count, width = latents_ref.shape
    step = pl.program_id(0)
    tile = out_ref.shape[0] * capacity

    @pl.when(step == 0)
    def _():
        loads = [
            pltpu.make_async_copy(a, b, sems.at[k])
            for k, (a, b) in enumerate((
                (owner_hbm, owner_ref), (row_hbm, row_ref),
                (latents_hbm, latents_ref), (cotangent_hbm, cotangent_ref),
            ))
        ]
        for load in loads:
            load.start()
        before = (
            lax.broadcasted_iota(jnp.int32, (LANES, LANES), 0)
            < lax.broadcasted_iota(jnp.int32, (LANES, LANES), 1)
        ).astype(jnp.bfloat16)
        owner_ids = lax.broadcasted_iota(jnp.int32, (devices, LANES), 0)
        lane = lax.broadcasted_iota(jnp.int32, (LANES, LANES), 1)
        seen = jnp.zeros((devices, 1), jnp.float32)
        loads[0].wait()
        loads[1].wait()
        for start in range(0, count, LANES):
            part = pl.ds(start, LANES)
            owners = owner_ref[:, part]
            mine = (owner_ids == owners).astype(jnp.float32)
            ranks = dot(mine.astype(jnp.bfloat16), before) + seen
            rank = jnp.sum(mine * ranks, axis=0, keepdims=True)
            seen = seen + jnp.sum(mine, axis=1, keepdims=True)
            slot_ref[:, part] = owners * capacity + rank.astype(jnp.int32)
            rows = jnp.transpose(
                jnp.broadcast_to(row_ref[:, part].astype(jnp.float32), (LANES, LANES))
            )
            tall = jnp.floor(rows * (1.0 / 32.0))
            extra = jnp.where(lane == 0, tall, jnp.where(lane == 1, rows - 32.0 * tall, 0.0))
            extra = jnp.where(lane == 2, 1.0, extra)
            parts_ref[part, 2 * width :] = extra.astype(jnp.bfloat16)
        loads[2].wait()
        loads[3].wait()
        for start in range(0, count, LANES):
            part = pl.ds(start, LANES)
            value = cotangent_ref[part, :] - latents_ref[part, :]
            high = value.astype(jnp.bfloat16)
            parts_ref[part, :width] = high
            parts_ref[part, width : 2 * width] = (value - high.astype(jnp.float32)).astype(
                jnp.bfloat16
            )

    ids = lax.broadcasted_iota(jnp.int32, (tile, count), 0) + step * tile
    chooser = (ids == slot_ref[...]).astype(jnp.float32).astype(jnp.bfloat16)
    both = dot(chooser, parts_ref[...])
    value = both[:, :width] + both[:, width : 2 * width]
    turned = jnp.transpose(both[:, 2 * width :])
    wanted = 32.0 * turned[0:1] + turned[1:2] + turned[2:3] - 1.0
    lane = lax.broadcasted_iota(jnp.int32, (EXTRA, LANES), 1)
    for k in range(out_ref.shape[0]):
        own = slice(k * capacity, (k + 1) * capacity)
        for j in range(width // LANES):
            out_ref[k, j * capacity : (j + 1) * capacity, :] = value[own, j * LANES : (j + 1) * LANES]
        at = k * capacity // LANES * LANES
        row = jnp.broadcast_to(wanted[:, at : at + LANES], (EXTRA, LANES))
        shift = k * capacity - at
        if shift:
            row = pltpu.roll(row, LANES - shift, 1)
        out_ref[k, width // LANES * capacity :, :] = jnp.where(lane < capacity, row, -1.0)


def route(devices, capacity, code_owner, code_row, latents, cotangent):
    count, width = latents.shape
    per_step = max(1, 512 // capacity)
    block = width // LANES * capacity + EXTRA
    whole = lambda *shape: pl.BlockSpec(shape, lambda i: (0,) * len(shape))
    return pl.pallas_call(
        functools.partial(route_kernel, devices, capacity),
        grid=(devices // per_step,),
        in_specs=[pl.BlockSpec(memory_space=pl.ANY)] * 4,
        out_specs=[
            pl.BlockSpec((per_step, block, LANES), lambda i: (i, 0, 0)),
            whole(1, count),
        ],
        out_shape=[
            jax.ShapeDtypeStruct((devices, block, LANES), jnp.float32),
            jax.ShapeDtypeStruct((1, count), jnp.int32),
        ],
        scratch_shapes=[
            pltpu.VMEM((1, count), jnp.int32),
            pltpu.VMEM((1, count), jnp.int32),
            pltpu.VMEM((count, width), jnp.float32),
            pltpu.VMEM((count, width), jnp.float32),
            pltpu.VMEM((count, 2 * width + LANES), jnp.bfloat16),
            pltpu.SemaphoreType.DMA((4,)),
        ],
        compiler_params=pltpu.CompilerParams(vmem_limit_bytes=60 * 2**20),
        name="route",
    )(code_owner.reshape(1, count), code_row.reshape(1, count), latents, cotangent)


def place(sizes, k, j):
    _, inner, chip, _ = sizes
    if k % 2:
        return j
    return j % inner * chip + j // inner


def backward_kernel(sizes, capacity, incoming_hbm, wanted_hbm, hidden_hbm, slope_hbm, projected_hbm,
                    codebook_hbm, weight_hbm, *refs):
    outer, inner, chip, core = sizes
    devices = outer * inner * chip * core
    mine_hbm, theirs_hbm, refs = refs[:outer], refs[outer : 2 * outer], refs[2 * outer :]
    (incoming, wanted, hidden, slope, projected, codebook, weight, parts, low, grad, flat,
     in_sem, out_sem) = refs
    width = projected.shape[1]
    dim_in, rows = codebook.shape
    hidden_size = hidden.shape[0]
    length = flat.shape[2] - EXTRA
    pairs = list(zip(
        (wanted_hbm, projected_hbm, weight_hbm, slope_hbm, hidden_hbm, codebook_hbm),
        (wanted, projected, weight, slope, hidden, codebook),
    ))
    loads = [pltpu.make_async_copy(a, b, in_sem.at[k]) for k, (a, b) in enumerate(pairs)]
    loads[0].start()
    blocks = width // LANES
    quarter = devices // 4
    arrivals = []
    for n in range(4):
        part = pl.ds(n * quarter, quarter)
        arrivals.append(pltpu.make_async_copy(
            incoming_hbm.at[part, pl.ds(0, blocks * capacity)], incoming.at[part], in_sem.at[6 + n]
        ))
        arrivals[n].start()
    for load in loads[1:]:
        load.start()
    for n in range(4):
        arrivals[n].wait()
        for s in range(n * quarter, (n + 1) * quarter):
            own = pl.ds(s * capacity, capacity)
            for j in range(blocks):
                value = incoming[s, j * capacity : (j + 1) * capacity, :]
                high = value.astype(jnp.bfloat16)
                parts[own, j * LANES : (j + 1) * LANES] = high
                parts[own, width + j * LANES : width + (j + 1) * LANES] = (
                    value - high.astype(jnp.float32)
                ).astype(jnp.bfloat16)
    for load in loads[:4]:
        load.wait()
    tile = min(512, rows)
    bias_in = jnp.zeros((1, hidden_size), jnp.float32)
    bias_out = jnp.zeros((1, width), jnp.float32)
    for start in range(0, rows, tile):
        part = pl.ds(start, tile)
        ids = (lax.broadcasted_iota(jnp.int32, (tile, wanted.shape[1]), 0) + start).astype(
            jnp.float32
        )
        chooser = (ids == wanted[0:1, :]).astype(jnp.float32)
        times = jnp.sum(chooser, axis=1, keepdims=True)
        both = dot(chooser.astype(jnp.bfloat16), parts[...])
        code_grad = both[:, :width] + both[:, width:] + times * projected[part, :]
        bias_out += jnp.sum(code_grad, axis=0, keepdims=True)
        code_low = code_grad.astype(jnp.bfloat16)
        low[part, :] = code_low
        preact_grad = (dot(code_low, weight[...]) * slope[part, :]).astype(jnp.bfloat16)
        grad[part, :] = preact_grad
        bias_in += jnp.sum(preact_grad.astype(jnp.float32), axis=0, keepdims=True)


    first = lax.axis_index("outer")
    plane = lax.axis_index("inner") * chip + lax.axis_index("chip")
    me = lax.axis_index("core")
    band = hidden_size // outer
    pieces = inner * chip
    home = lax.rem(outer - first, outer)
    for k in range(outer):
        for e in range(pieces * core):
            flat[k, e, length:, :] = jnp.zeros((EXTRA, LANES), jnp.float32)
    for e, bias in enumerate((bias_in, bias_out)):
        for j in range(bias.shape[1] // LANES):
            flat[home, e, length + j : length + j + 1, :] = bias[:, j * LANES : (j + 1) * LANES]

    loads[4].wait()
    loads[5].wait()
    stores = []
    for k in range(outer - 1, -1, -1):
        o = lax.rem(first + k, outer)
        here = pl.ds(pl.multiple_of(o * band, band), band)

        def keep(row, value):
            for r in range(0, value.shape[0], length):
                flat[k, (row + r) // length, :length, :] = value[r : r + length, :]

        out = dot(codebook[...], grad[:, here])
        for j in range(band // LANES):
            keep(j * dim_in, out[:, j * LANES : (j + 1) * LANES])
        out = dot(hidden[here, :], low[...])
        for j in range(blocks):
            keep(band // LANES * dim_in + j * band, out[:, j * LANES : (j + 1) * LANES])
        for target, c in ((theirs_hbm, 1 - me), (mine_hbm, me)):
            for j in range(pieces):
                e = lax.bitwise_xor(plane, place(sizes, k, j)) * core + c
                copy = pltpu.make_async_copy(
                    flat.at[k, e], target[k].at[j], out_sem.at[len(stores)]
                )
                copy.start()
                stores.append(copy)
    for copy in stores:
        copy.wait()


def backward(sizes, capacity, incoming, wanted, hidden_t, slope, projected, codebook_t, weight_t):
    devices = incoming.shape[0]
    rows, width = projected.shape
    dim_in, hidden_size = codebook_t.shape[0], hidden_t.shape[0]
    length = (dim_in + width) * hidden_size // LANES // devices
    outer, inner, chip, core = sizes
    piece = jax.ShapeDtypeStruct((inner * chip, length + EXTRA, LANES), jnp.float32)
    operands = (incoming, wanted, hidden_t, slope, projected, codebook_t, weight_t)
    vmem = lambda shape, dtype: pltpu.VMEM(shape, dtype)
    slots = devices * capacity
    return pl.pallas_call(
        functools.partial(backward_kernel, sizes, capacity),
        in_specs=[pl.BlockSpec(memory_space=pl.ANY)] * len(operands),
        out_specs=[pl.BlockSpec(memory_space=pl.ANY)] * (2 * outer),
        out_shape=[piece] * (2 * outer),
        scratch_shapes=[vmem((devices, incoming.shape[1] - EXTRA, LANES), jnp.float32)]
        + [vmem(a.shape, a.dtype) for a in operands[1:]]
        + [
            vmem((slots, 2 * width), jnp.bfloat16),
            vmem((rows, width), jnp.bfloat16),
            vmem((rows, hidden_size), jnp.bfloat16),
            vmem((outer, inner * chip * core, length + EXTRA, LANES), jnp.float32),
            pltpu.SemaphoreType.DMA((10,)),
            pltpu.SemaphoreType.DMA((devices,)),
        ],
        cost_estimate=pl.CostEstimate(
            flops=2 * rows * (slots * 2 * width + hidden_size * (2 * width + dim_in)),
            bytes_accessed=16 * rows * hidden_size,
            transcendentals=0,
        ),
        compiler_params=pltpu.CompilerParams(vmem_limit_bytes=60 * 2**20),
        name="backward",
    )(*operands)


def assemble_kernel(sizes, *refs):
    outer, inner, chip, core = sizes
    devices = outer * inner * chip * core
    pieces, refs = refs[:devices], refs[devices:]
    weight_in, weight_out, bias_in, bias_out, sems, bias_sem = refs
    length = pieces[0].shape[0] - EXTRA
    dim_in, hidden_size = weight_in.shape
    band = hidden_size // outer
    base = band // LANES * dim_in
    first = lax.axis_index("outer")
    plane = lax.axis_index("inner") * chip + lax.axis_index("chip")
    me = lax.axis_index("core")
    copies = []
    for n, piece in enumerate(pieces):
        c, n = divmod(n, devices // core)
        k, j = divmod(n, inner * chip)
        n += c * (devices // core)
        o = lax.rem(first + outer - k, outer)
        e = lax.bitwise_xor(plane, place(sizes, k, j)) * core + lax.bitwise_xor(me, c)
        at = e * length
        source = piece.at[pl.ds(0, length)]

        def copy_to(target, row, column):
            rows = pl.ds(pl.multiple_of(row, length), length)
            lanes = pl.ds(pl.multiple_of(column * LANES, LANES), LANES)
            return pltpu.make_async_copy(source, target.at[rows, lanes], sems.at[n])

        @pl.when(at < base)
        def _():
            column = o * (band // LANES) + lax.div(at, dim_in)
            copy_to(weight_in, lax.rem(at, dim_in), column).start()

        @pl.when(at >= base)
        def _():
            copy_to(weight_out, o * band + lax.rem(at - base, band), lax.div(at - base, band)).start()

        for row, bias in enumerate((bias_in, bias_out)):

            @pl.when((o == 0) & (e == row))
            def _():
                copy = pltpu.make_async_copy(
                    piece.at[pl.ds(length, EXTRA)], bias, bias_sem
                )
                copy.start()
                copy.wait()

        copies.append(copy_to(weight_in, 0, 0))
    for copy in copies:
        copy.wait()


def assemble(sizes, pieces, dim_in, hidden_size, width):
    hbm = pl.BlockSpec(memory_space=pl.ANY)
    return pl.pallas_call(
        functools.partial(assemble_kernel, sizes),
        in_specs=[hbm] * len(pieces),
        out_specs=[hbm] * 4,
        out_shape=[
            jax.ShapeDtypeStruct((dim_in, hidden_size), jnp.float32),
            jax.ShapeDtypeStruct((hidden_size, width), jnp.float32),
            jax.ShapeDtypeStruct((EXTRA, LANES), jnp.float32),
            jax.ShapeDtypeStruct((EXTRA, LANES), jnp.float32),
        ],
        scratch_shapes=[
            pltpu.SemaphoreType.DMA((len(pieces),)),
            pltpu.SemaphoreType.DMA,
        ],
        compiler_params=pltpu.CompilerParams(vmem_limit_bytes=4 * 2**20),
        name="assemble",
    )(*pieces)


def along(sizes, x, k):
    outer = sizes[0]
    return lax.ppermute(x, "outer", [(o, (o + k) % outer) for o in range(outer)])


def across(sizes, axis, x, j):
    size = sizes[AXES.index(axis)]
    return lax.ppermute(x, axis, [(p, p ^ j) for p in range(size)])


def sum_chunks(sizes, mine, theirs):
    outer, inner, chip, _ = sizes
    chunks = [None] * outer
    for k in range(outer - 1, -1, -1):
        slow, fast = ("inner", "chip") if k % 2 else ("chip", "inner")
        low = sizes[AXES.index(fast)]
        arrived = across(sizes, "core", theirs[k], 1)
        part = mine[k][:low] + arrived[:low]
        for j in range(1, sizes[AXES.index(slow)]):
            here = slice(j * low, (j + 1) * low)
            part = part + across(sizes, slow, mine[k][here] + arrived[here], j)
        chunks[k] = part[0]
        for j in range(1, low):
            chunks[k] = chunks[k] + across(sizes, fast, part[j], j)
    total = chunks[0]
    for k in range(outer - 1, 0, -1):
        total = total + along(sizes, chunks[k], k)
    return total


def spread_chunks(sizes, total):
    outer, inner, chip, _ = sizes
    near = []
    line = [along(sizes, total, k) if k else total for k in range(outer)]
    line[:2] = lax.optimization_barrier(tuple(line[:2]))
    for k, x in enumerate(line):
        slow, fast = ("inner", "chip") if k % 2 else ("chip", "inner")
        row = [across(sizes, fast, x, j) if j else x for j in range(sizes[AXES.index(fast)])]
        for j in range(sizes[AXES.index(slow)]):
            near += [across(sizes, slow, x, j) if j else x for x in row]
    return near


def per_device(
    sizes, codebook, weight_in, bias_in, weight_out, bias_out, latents, cotangent, code_owner, code_row
):
    outer, inner, chip, core = sizes
    devices = outer * inner * chip * core
    rows, dim_in = codebook.shape
    hidden_size = weight_in.shape[1]
    count, width = latents.shape
    capacity = max(2, 2 * count // devices)

    outgoing, slots = route(devices, capacity, code_owner, code_row, latents, cotangent)
    outgoing, bias_in = lax.optimization_barrier((outgoing, bias_in))
    incoming = lax.all_to_all(outgoing, AXES, split_axis=0, concat_axis=0, tiled=True)

    hidden_t, codebook_t, slope, projected, parts = forward(
        codebook, weight_in, bias_in, weight_out, bias_out
    )
    picked, wanted = pick_rows(capacity, incoming, parts)
    answers = lax.all_to_all(picked, AXES, split_axis=0, concat_axis=0, tiled=True)

    weight_t = weight_out.T

    def reduce_half(*operands):
        pieces = backward(sizes, capacity, *operands)
        return sum_chunks(sizes, list(pieces[:outer]), list(pieces[outer:]))

    def nothing(*operands):
        length = (dim_in + width) * hidden_size // LANES // devices
        return jnp.zeros((length + EXTRA, LANES), jnp.float32)

    total = lax.cond(
        code_row[0] >= 0, reduce_half, nothing,
        incoming, wanted, hidden_t, slope, projected, codebook_t, weight_t,
    )
    total, answers = lax.optimization_barrier((total, answers))
    answers = answers.reshape(-1, width)
    near = spread_chunks(sizes, total)

    slot_ids = jnp.arange(devices * capacity, dtype=jnp.int32)
    from_slot = slots.reshape(-1, 1) == slot_ids[None, :]
    chosen = pick(from_slot.astype(jnp.bfloat16), answers)
    latent_grad = cotangent - 0.25 * (chosen - latents)
    late = len(near) - inner * chip
    near[late], latent_grad = lax.optimization_barrier((near[late], latent_grad))

    chunks = near + [across(sizes, "core", x, 1) for x in near]
    gw_in, gw_out, gb_in, gb_out = assemble(sizes, chunks, dim_in, hidden_size, width)
    gb_in, gb_out = gb_in.reshape(-1)[:hidden_size], gb_out.reshape(-1)[:width]
    return (latent_grad, gw_in, gb_in, gw_out, gb_out)


def solution(mesh):
    code, data = mesh.shape["code"], mesh.shape["dp"]
    core = 2
    outer = 1
    while outer * outer < code:
        outer *= 2
    sizes = (outer, code // outer, data // core, core)
    fine = Mesh(mesh.devices.reshape(sizes), AXES)
    rows = P(AXES, None)
    return jax.shard_map(
        functools.partial(per_device, sizes),
        mesh=fine,
        in_specs=(rows, P(), P(), P(), P(), rows, rows, rows, P(AXES)),
        out_specs=(rows, P(), P(), P(), P()),
        check_vma=False,
    )
```
